32 devices in a mesh: grp: 8 (over z, x), fsdp: 4 (over y, core).
Axes of the slice: x: 2, y: 2, z: 4, core: 2. Of those that a mesh axis runs over, the one named last changes fastest.
Arguments:
- inputs: bfloat16 [96, 160, 768], P(('grp', 'fsdp')), may hold values from -6 to 6
- lengths: int32 [96], P(('grp', 'fsdp')), may hold values from 95 to 160, as said below
- cotangent: bfloat16 [96, 160, 768], P(('grp', 'fsdp')), may hold values from -6 to 6
- masters: float32 [2, 48, 384, 384], P(None, 'grp', 'fsdp')
- small_params: float32 [2, 9216], replicated
- small_moments: float32 [2, 9216], replicated, may hold values from 3840 to 15360
- left_stats: float32 [2, 48, 384, 384], P(None, 'grp', 'fsdp')
- right_stats: float32 [2, 48, 384, 384], P(None, 'grp', 'fsdp')
- left_roots: float32 [2, 48, 384, 384], P(None, 'grp', 'fsdp')
- right_roots: float32 [2, 48, 384, 384], P(None, 'grp', 'fsdp'), as said below
Outputs:
- activations: bfloat16 [96, 160, 768], P(('grp', 'fsdp'))
- input_grad: float32 [96, 160, 768], P(('grp', 'fsdp'))
- blocked_weight_gradients: float32 [2, 48, 384, 384], P(None, 'grp', 'fsdp')
- small_grads: float32 [2, 9216], replicated
- new_moments: float32 [2, 9216], replicated
- new_small: float32 [2, 9216], replicated
- new_left: float32 [2, 48, 384, 384], P(None, 'grp', 'fsdp')
- new_right: float32 [2, 48, 384, 384], P(None, 'grp', 'fsdp')
- new_masters: float32 [2, 48, 384, 384], P(None, 'grp', 'fsdp')
- new_copies: bfloat16 [2, 48, 384, 384], P(None, 'grp', 'fsdp')
The draws below stay inside these ranges and needn't reach their ends.
Inputs may be any that keep to these rules, and one draw needn't show every extreme that they name: `lengths`: in every draw some chain has exactly 160 live residues and some exactly 95. `right_roots`: every block is symmetric.
All inputs are finite; a program needn't handle non-finite values.
Results may differ from the reference program's by a relative error of at most 0.02.
Values may be sent and summed in bfloat16 or wider, within the bound.
No kernel may reach another device: no remote copies, remote signals or barrier semaphores. Data moves between devices by JAX's collectives and lax.ppermute only.
A program may use at most 256 MiB of HBM per device.

```python
import math
import jax
import jax.numpy as jnp
from jax import lax

D = 768
HEADS = 12
FF = 3072
HEAD_DIM = 64
BLOCK = 384
ENCODER_LAYERS = 2
LEN = 160
MIN_LEN = 95
CH_DEV = 3
SEQS = 96
TOKENS = 15360
NBLK = 48
SMALL = 9216


def block_scales():
    model_count = (D // BLOCK) ** 2
    ffn_count = D // BLOCK * (FF // BLOCK)
    places = jnp.arange(NBLK)
    base = D ** (-0.5)
    inner = jnp.where(places < 4 * model_count + ffn_count, base, 1.5 * FF ** (-0.5))
    middle = jnp.where(places < 4 * model_count, 0.8 * math.sqrt(MIN_LEN) * base, inner)
    return jnp.where(places < 3 * model_count, base, middle).astype(jnp.float32)


def gradient_scale():
    return 0.5 * math.sqrt(TOKENS)


def kronecker(key, level, lowest, highest, spread):
    subkeys = jax.random.split(key, 2)
    diagonal = jax.random.uniform(subkeys[0], (ENCODER_LAYERS, NBLK, BLOCK), jnp.float32, lowest, highest) * level[None, :, None]
    noise = jax.random.uniform(subkeys[1], (ENCODER_LAYERS, NBLK, BLOCK, BLOCK), jnp.float32, -1.0, 1.0)
    mirrored = 0.5 * (noise + jnp.swapaxes(noise, 2, 3))
    offdiag = mirrored * (spread / BLOCK) * level[None, :, None, None]
    identity = jnp.arange(BLOCK)[:, None] == jnp.arange(BLOCK)[None, :]
    return jnp.where(identity, diagonal[:, :, :, None], offdiag)


def draw_lengths(key, part):
    key = jax.random.fold_in(key, 11)
    subkeys = jax.random.split(key, 3)
    drawn = jax.random.randint(subkeys[0], (SEQS,), MIN_LEN, LEN + 1)
    longest = jax.random.randint(subkeys[1], (), 0, SEQS)
    shortest = (longest + 1 + jax.random.randint(subkeys[2], (), 0, SEQS - 1)) % SEQS
    places = jnp.arange(SEQS)
    drawn = jnp.where(places == longest, LEN, drawn)
    return jnp.where(places == shortest, MIN_LEN, drawn).astype(jnp.int32)


def draw_masters(key, part):
    key = jax.random.fold_in(key, 25)
    normal_draw = jax.random.truncated_normal(key, -4.0, 4.0, (ENCODER_LAYERS, NBLK, BLOCK, BLOCK), jnp.float32)
    return normal_draw * block_scales()[None, :, None, None]


def draw_small_params(key, part):
    key = jax.random.fold_in(key, 26)
    subkeys = jax.random.split(key, 2)
    segments = jnp.arange(SMALL) // D
    gains = jax.random.uniform(subkeys[0], (ENCODER_LAYERS, SMALL), jnp.float32, 0.6, 1.4)
    shifts = 0.3 * jax.random.normal(subkeys[1], (ENCODER_LAYERS, SMALL), jnp.float32)
    is_gain = (segments == 4) | (segments == 6)
    return jnp.where(is_gain[None, :], gains, shifts)


def draw_left_stats(key, part):
    key = jax.random.fold_in(key, 21)
    level = jnp.full((NBLK,), BLOCK * gradient_scale() ** 2, jnp.float32)
    return kronecker(key, level, 1.0, 4.0, 1.5)


def draw_right_stats(key, part):
    key = jax.random.fold_in(key, 22)
    level = jnp.full((NBLK,), BLOCK * gradient_scale() ** 2, jnp.float32)
    return kronecker(key, level, 1.0, 4.0, 1.5)


def draw_left_roots(key, part):
    key = jax.random.fold_in(key, 23)
    level = jnp.sqrt(block_scales() / gradient_scale())
    return kronecker(key, level, 0.7, 1.4, 1.5)


def draw_right_roots(key, part):
    key = jax.random.fold_in(key, 24)
    level = jnp.sqrt(block_scales() / gradient_scale())
    return kronecker(key, level, 0.7, 1.4, 1.5)


def shard_levels(key, dims, cuts, smallest, top_value):
    level, own = 1.0, jax.random.fold_in(key, 6)
    for dim, blocks in cuts:
        draws = jnp.exp(jax.random.uniform(jax.random.fold_in(own, dim), (blocks,), jnp.float32, smallest / len(cuts), top_value / len(cuts)))
        level = level * jnp.repeat(draws, dims[dim] // blocks).reshape([-1 if axis == dim else 1 for axis in range(len(dims))])
    return level


def scatter_about(rng, extent, scale, bound, cuts=(), kind=jnp.bfloat16):
    values = jax.random.normal(rng, extent, jnp.float32) * scale
    if len(cuts) > 0:
        values = shard_levels(rng, extent, cuts, -0.22, 0.18) * values
    return jnp.clip(values, min=-bound, max=bound).astype(kind)


def setup_inputs(seed: int = 0) -> dict:
    arg_keys = jax.random.split(jax.random.key(seed), 11)
    inputs = scatter_about(arg_keys[0], (SEQS, LEN, D), 1.0, 6.0, ((0, 32),))
    lengths = draw_lengths(jax.random.fold_in(arg_keys[10], 71), 0)
    cotangent = scatter_about(arg_keys[2], (SEQS, LEN, D), 1.0, 6.0, ((0, 32),))
    masters = draw_masters(jax.random.fold_in(arg_keys[10], 71), 0)
    small_params = draw_small_params(jax.random.fold_in(arg_keys[10], 71), 0)
    small_moments = jnp.clip(jnp.exp(jax.random.uniform(arg_keys[5], (ENCODER_LAYERS, SMALL), jnp.float32, math.log(3840.0), math.log(15360.0))), 3840.0, 15360.0)
    left_stats = draw_left_stats(jax.random.fold_in(arg_keys[10], 71), 0)
    right_stats = draw_right_stats(jax.random.fold_in(arg_keys[10], 71), 0)
    left_roots = draw_left_roots(jax.random.fold_in(arg_keys[10], 71), 0)
    right_roots = draw_right_roots(jax.random.fold_in(arg_keys[10], 71), 0)
    return dict(inputs=inputs, lengths=lengths, cotangent=cotangent, masters=masters, small_params=small_params, small_moments=small_moments, left_stats=left_stats, right_stats=right_stats, left_roots=left_roots, right_roots=right_roots)


@jax.custom_vjp
def low(v):
    return lax.optimization_barrier(v.astype(jnp.bfloat16)).astype(jnp.float32)

@jax.custom_vjp
def low_back(v):
    return v

def low_keep(v):
    return (low(v), None)

def low_pass(kept, grad):
    return (grad,)

def back_keep(v):
    return (v, None)

def back_low(kept, grad):
    return (low(grad),)
low.defvjp(low_keep, low_pass)
low_back.defvjp(back_keep, back_low)
norm_epsilon = 1e-05
matrix_rate = 1.0
small_rate = 0.3
decay_rate = 0.5
moment_epsilon = 1e-08

def products(left, right):
    return jnp.dot(left, right, precision=lax.Precision.HIGHEST, preferred_element_type=jnp.float32)

def layer_norm(values, gain, shift):
    center = values - lax.optimization_barrier(jnp.mean(values, axis=-1, keepdims=True))
    spread = lax.optimization_barrier(jnp.mean(center * center, axis=-1, keepdims=True))
    return center * lax.rsqrt(spread + norm_epsilon) * gain + shift

def unblock(weight_blocks):
    model_count = D // BLOCK
    ffn_count = FF // BLOCK
    layout = [(model_count, model_count)] * 4 + [(model_count, ffn_count), (ffn_count, model_count)]
    weight_matrices = []
    offset = 0
    for row_count, col_count in layout:
        selected = weight_blocks[offset:offset + row_count * col_count]
        weight_matrices.append(selected.reshape(row_count, col_count, BLOCK, BLOCK).transpose(0, 2, 1, 3).reshape(row_count * BLOCK, col_count * BLOCK))
        offset += row_count * col_count
    return tuple(weight_matrices)

def split_into_blocks(weight_matrices):
    pieces = []
    for matrix in weight_matrices:
        row_count = matrix.shape[0] // BLOCK
        col_count = matrix.shape[1] // BLOCK
        pieces.append(matrix.reshape(row_count, BLOCK, col_count, BLOCK).transpose(0, 2, 1, 3).reshape(row_count * col_count, BLOCK, BLOCK))
    return jnp.concatenate(pieces, axis=0)

def encoder_layer(rows, weight_matrices, small, key_valid):
    w_query, w_key, w_value, w_out, w_up, w_down = weight_matrices
    segments = [small[segment * D:(segment + 1) * D] for segment in range(8)]
    bias_query, bias_value, bias_out, bias_down, gain_one, shift_one, gain_two, shift_two = segments
    bias_up = small[8 * D:]
    heads_shape = (CH_DEV, LEN, HEADS, HEAD_DIM)
    rows_low = low(rows)
    queries = low(low_back(products(rows_low, w_query) + bias_query)).reshape(heads_shape)
    key_rows = low(low_back(products(rows_low, w_key))).reshape(heads_shape)
    values = low(low_back(products(rows_low, w_value) + bias_value)).reshape(heads_shape)
    scores = jnp.einsum('cqhd,ckhd->chqk', queries, key_rows, precision=lax.Precision.HIGHEST) * HEAD_DIM ** (-0.5)
    scores = low_back(scores)
    scores = jnp.where(key_valid[:, None, None, :], scores, -1000000000.0)
    attention = jax.nn.softmax(scores, axis=-1)
    context = jnp.einsum('chqk,ckhd->cqhd', low(attention), values, precision=lax.Precision.HIGHEST)
    context = low(low_back(context.reshape(CH_DEV * LEN, D)))
    attended = low_back(products(context, w_out) + bias_out)
    normed_one = layer_norm(rows + attended, gain_one, shift_one)
    hidden = low_back(products(low(normed_one), w_up) + bias_up)
    active = low(jax.nn.gelu(hidden, approximate=False))
    branch = low_back(products(active, w_down) + bias_down)
    return layer_norm(normed_one + branch, gain_two, shift_two)

def reference(inputs, lengths, cotangent, masters, small_params, small_moments, left_stats, right_stats, left_roots, right_roots):
    rounded = masters.astype(jnp.bfloat16).astype(jnp.float32)
    weight_matrices = tuple((unblock(rounded[layer_position]) for layer_position in range(ENCODER_LAYERS)))
    group_total = SEQS // CH_DEV
    positions = jnp.arange(LEN).astype(jnp.int32)
    valid = positions[None, :] < lengths[:, None]
    sequence = (inputs.astype(jnp.float32).reshape(group_total, CH_DEV, LEN, D), cotangent.astype(jnp.float32).reshape(group_total, CH_DEV, LEN, D), valid.reshape(group_total, CH_DEV, LEN))

    def chain_step(totals, pieces):
        states, seeds, key_valid = pieces

        def forward(states_in, matrices_in, small_in):
            current = states_in.reshape(CH_DEV * LEN, D)
            for layer_position in range(ENCODER_LAYERS):
                current = encoder_layer(current, matrices_in[layer_position], small_in[layer_position], key_valid)
            return current.reshape(CH_DEV, LEN, D)
        outputs, pullback = jax.vjp(forward, states, weight_matrices, small_params)
        grad_states, gradient_matrices, grad_small = pullback(seeds * key_valid[..., None].astype(jnp.float32))
        totals = jax.tree.map(jnp.add, totals, (gradient_matrices, grad_small))
        return (totals, (outputs.astype(jnp.bfloat16), grad_states))
    initial = jax.tree.map(jnp.zeros_like, (weight_matrices, small_params))
    (gradient_matrices, small_grads), (outputs, grad_inputs) = lax.scan(chain_step, initial, sequence)
    activations = outputs.reshape(SEQS, LEN, D)
    input_grad = grad_inputs.reshape(SEQS, LEN, D)
    blocked_weight_gradients = jnp.stack([split_into_blocks(gradient_matrices[layer_position]) for layer_position in range(ENCODER_LAYERS)])
    highest = lax.Precision.HIGHEST
    new_left = decay_rate * left_stats + (1.0 - decay_rate) * jnp.einsum('lbrk,lbck->lbrc', blocked_weight_gradients, blocked_weight_gradients, precision=highest)
    new_right = decay_rate * right_stats + (1.0 - decay_rate) * jnp.einsum('lbkr,lbkc->lbrc', blocked_weight_gradients, blocked_weight_gradients, precision=highest)
    mixed = jnp.einsum('lbrk,lbkc->lbrc', blocked_weight_gradients, right_roots, precision=highest)
    update = jnp.einsum('lbrk,lbkc->lbrc', left_roots, mixed, precision=highest)
    new_masters = masters - matrix_rate * update
    new_copies = new_masters.astype(jnp.bfloat16)
    new_moments = decay_rate * small_moments + (1.0 - decay_rate) * small_grads * small_grads
    new_small = small_params - small_rate * small_grads / (jnp.sqrt(new_moments) + moment_epsilon)
    return (activations, input_grad, blocked_weight_gradients, small_grads, new_moments, new_small, new_left, new_right, new_masters, new_copies)
```

```python
import functools

import jax
import jax.numpy as jnp
from jax import lax
from jax.experimental import pallas as pl
from jax.experimental.pallas import tpu as pltpu
from jax.sharding import PartitionSpec as P

HEADS = 12
LAYERS = 2
Z_SLABS = 4
BF = jnp.bfloat16
F32 = jnp.float32

norm_epsilon = 1e-05
matrix_rate = 1.0
small_rate = 0.3
decay_rate = 0.5
moment_epsilon = 1e-08

VMEM = pl.BlockSpec(memory_space=pltpu.VMEM)
SMEM = pl.BlockSpec(memory_space=pltpu.SMEM)
HBM = pl.BlockSpec(memory_space=pl.ANY)
VMEM_LIMIT = 56 * 1024 * 1024


def shape(dims, dtype):
    return jax.ShapeDtypeStruct(tuple(dims), dtype)


def mm(a, b):
    return jnp.dot(a, b, preferred_element_type=F32)


def mm_bt(a, b):
    return lax.dot_general(a, b, (((1,), (1,)), ((), ())), preferred_element_type=F32)


def mm_at(a, b):
    return lax.dot_general(a, b, (((0,), (0,)), ((), ())), preferred_element_type=F32)


class Part:
    def __init__(self, zs, js, last, arrays):
        self.zs, self.js, self.last, self.arrays = tuple(zs), tuple(js), last, arrays

    def flat(self):
        return [a for row in self.arrays for a in row]


class Dims:
    def __init__(self, model, ffn, block, blocks, rows):
        self.model, self.ffn, self.block, self.blocks, self.rows = model, ffn, block, blocks, rows
        self.own = blocks // (2 * Z_SLABS)
        self.piece = block // 4
        wide, tall = model // block, ffn // block
        self.places = {}
        at = 0
        for name, rows_, cols_ in (
            ("q", wide, wide),
            ("k", wide, wide),
            ("v", wide, wide),
            ("o", wide, wide),
            ("up", wide, tall),
            ("down", tall, wide),
        ):
            self.places[name] = [
                (at + r * cols_ + c, r * block, c * block) for r in range(rows_) for c in range(cols_)
            ]
            at += rows_ * cols_

    def where(self, b):
        return b // (2 * self.own), (b // self.own) % 2, b % self.own


def find_part(parts, z, j):
    for number, part in enumerate(parts):
        if z in part.zs and j in part.js:
            return number, part.zs.index(z), part.js.index(j)
    raise ValueError("no part")


def needed_parts(dims, parts, names):
    used = set()
    for name in names:
        for b, _, _ in dims.places[name]:
            z, _, j = dims.where(b)
            used.add(find_part(parts, z, j)[0])
    return [parts[n] for n in sorted(used)]


def start_loads(dims, parts, refs, pos, name, dst, row0, col0, sem):
    x, y, c = pos
    piece = dims.piece

    def rows_at(base, quarter):
        return pl.ds(pl.multiple_of(base + piece * quarter, 16), piece)

    later = []
    for b, r, col in dims.places[name]:
        z, xq, j = dims.where(b)
        number, zi, ji = find_part(parts, z, j)
        cols = pl.ds(col0 + col, dims.block)
        if parts[number].last == "y":
            for dc in range(2):
                for dy in range(2):
                    src = refs[number][dc][dy].at[x ^ xq, zi, ji]
                    rows = rows_at(row0 + r, 2 * (y ^ dy) + (c ^ dc))
                    pltpu.make_async_copy(src, dst.at[rows, cols], sem).start()
        else:
            later.append((number, zi, ji, xq, r, cols))
    if later:
        for own_x in range(2):

            @pl.when(x == own_x)
            def _(own_x=own_x):
                for number, zi, ji, xq, r, cols in later:
                    for dc in range(2):
                        for yq in range(2):
                            src = refs[number][dc][own_x ^ xq].at[y ^ yq, zi, ji]
                            rows = rows_at(row0 + r, 2 * yq + (c ^ dc))
                            pltpu.make_async_copy(src, dst.at[rows, cols], sem).start()


def wait_for(ref, sem):
    pltpu.make_async_copy(ref, ref, sem).wait()


def start_stores(dims, parts, outs, pos, places, src, sem):
    x, y, c = pos
    piece = dims.piece
    for b, r, col in places:
        z, xq, j = dims.where(b)
        number, zi, ji = find_part(parts, z, j)
        for dc in range(2):
            for yq in range(2):
                rows = pl.ds(pl.multiple_of(r + piece * (2 * yq + (c ^ dc)), 16), piece)
                first, second = y ^ yq, x ^ xq
                if parts[number].last == "x":
                    first, second = second, first
                dst = outs[number][dc].at[first, second, zi, ji]
                pltpu.make_async_copy(src.at[rows, pl.ds(col, dims.block)], dst, sem).start()


def norm_forward(values):
    center = values - jnp.mean(values, axis=-1, keepdims=True)
    spread = jnp.mean(center * center, axis=-1, keepdims=True)
    inverse = lax.rsqrt(spread + norm_epsilon)
    return center * inverse, inverse


def norm_backward(gradient, unit, inverse, gain):
    scaled = gradient * gain
    inner = (
        scaled
        - jnp.mean(scaled, axis=-1, keepdims=True)
        - unit * jnp.mean(scaled * unit, axis=-1, keepdims=True)
    )
    return inverse * inner


def col_sum(values):
    return jnp.sum(values.astype(F32), axis=0, keepdims=True)


def segment(small_ref, number, width):
    return small_ref[0:1, number * width : (number + 1) * width]


def unflatten(refs, parts):
    out, at = [], 0
    for part in parts:
        rows = []
        for row in part.arrays:
            rows.append(refs[at : at + len(row)])
            at += len(row)
        out.append(rows)
    return out, refs[at:]


def half_masks(head):
    lane = lax.broadcasted_iota(jnp.int32, (1, 2 * head), 1)
    low = lane < head
    ones = jnp.where(low, 1.0, 0.0).astype(F32)
    return low, (ones.astype(BF), (1.0 - ones).astype(BF))


def attention_forward_kernel(dims, parts, chains, pos_ref, len_ref, x_ref, small_ref, *rest):
    refs, rest = unflatten(rest, parts)
    qkv_ref, lse_ref, ctx_ref, unit_ref, inv_ref, w, sems = rest
    width, seq = dims.model, dims.rows // chains
    head = width // HEADS
    pos = (pos_ref[1], pos_ref[2], pos_ref[3])
    for n, name in enumerate(("q", "k", "v", "o")):
        start_loads(dims, parts, refs, pos, name, w, 0, n * width, sems.at[n])
    xb = x_ref[...].astype(BF)
    for n, bias in ((0, 0), (1, None), (2, 1)):
        cols = slice(n * width, (n + 1) * width)
        wait_for(w.at[:, cols], sems.at[n])
        out = mm(xb, w[:, cols])
        if bias is not None:
            out = out + segment(small_ref, bias, width)
        qkv_ref[:, cols] = out.astype(BF)
    low, masks = half_masks(head)
    scale = head**-0.5

    def chain(i, carry):
        rows = pl.ds(pl.multiple_of(i * seq, 16), seq)
        valid = lax.broadcasted_iota(jnp.int32, (seq, seq), 0) < len_ref[i]
        for pair in range(HEADS // 2):
            at = pair * 2 * head
            q = qkv_ref[rows, at : at + 2 * head]
            k = qkv_ref[rows, width + at : width + at + 2 * head]
            v = qkv_ref[rows, 2 * width + at : 2 * width + at + 2 * head]
            outs = []
            for h in range(2):
                s = jnp.where(valid, mm_bt(k, q * masks[h]) * scale, -1000000000.0)
                top = jnp.max(s, axis=0, keepdims=True)
                e = jnp.exp(s - top)
                total = jnp.sum(e, axis=0, keepdims=True)
                lse_ref[i, 2 * pair + h : 2 * pair + h + 1, :] = top + jnp.log(total)
                outs.append(mm_at((e * (1.0 / total)).astype(BF), v))
            ctx_ref[rows, at : at + 2 * head] = jnp.where(low, outs[0], outs[1]).astype(BF)
        return carry

    lax.fori_loop(0, chains, chain, 0)
    wait_for(w.at[:, 3 * width :], sems.at[3])
    attended = mm(ctx_ref[...], w[:, 3 * width :]) + segment(small_ref, 2, width)
    unit, inverse = norm_forward(x_ref[...].astype(F32) + attended)
    unit_ref[...] = unit
    inv_ref[...] = inverse


def attention_forward(dims, parts, pos, lengths, x, small):
    parts = needed_parts(dims, parts, ("q", "k", "v", "o"))
    chains = lengths.shape[0]
    seq, width = dims.rows // chains, dims.model
    flat = [a for p in parts for a in p.flat()]
    return pl.pallas_call(
        functools.partial(attention_forward_kernel, dims, parts, chains),
        in_specs=[SMEM, SMEM, VMEM, VMEM] + [HBM] * len(flat),
        out_specs=[VMEM] * 5,
        out_shape=[
            shape((dims.rows, 3 * width), BF),
            shape((chains, HEADS, seq), F32),
            shape((dims.rows, width), BF),
            shape((dims.rows, width), F32),
            shape((dims.rows, 1), F32),
        ],
        scratch_shapes=[pltpu.VMEM((width, 4 * width), BF), pltpu.SemaphoreType.DMA((4,))],
        compiler_params=pltpu.CompilerParams(vmem_limit_bytes=VMEM_LIMIT),
        cost_estimate=pl.CostEstimate(
            flops=12 * dims.rows * width * width, bytes_accessed=16 << 20, transcendentals=1 << 20
        ),
        name="attention_forward",
    )(pos, lengths, x, small, *flat)


def ffn_forward_body(dims, small_ref, unit_ref, up, down, sems, act_ref, slope_ref):
    width = dims.model
    h1 = unit_ref[...] * segment(small_ref, 4, width) + segment(small_ref, 5, width)
    hb = h1.astype(BF)
    total = h1 + segment(small_ref, 3, width)
    wait_for(up, sems.at[0])
    for n in range(dims.ffn // width):
        cols = slice(n * width, (n + 1) * width)
        u = mm(hb, up[:, cols]) + segment(small_ref, 8 + n, width)
        cdf = 0.5 * (1.0 + lax.erf(u * 0.7071067811865476))
        act = (u * cdf).astype(BF)
        act_ref[:, cols] = act
        slope_ref[:, cols] = (cdf + u * (0.3989422804014327 * jnp.exp(-0.5 * u * u))).astype(BF)
        if n == 0:
            wait_for(down, sems.at[1])
        total = total + mm(act, down[cols, :])
    return total


def ffn_forward_kernel(dims, parts, pos_ref, unit_ref, small_ref, *rest):
    refs, rest = unflatten(rest, parts)
    act_ref, slope_ref, unit2_ref, inv2_ref, y_ref, up, down, sems = rest
    pos = (pos_ref[1], pos_ref[2], pos_ref[3])
    start_loads(dims, parts, refs, pos, "up", up, 0, 0, sems.at[0])
    start_loads(dims, parts, refs, pos, "down", down, 0, 0, sems.at[1])
    width = dims.model
    total = ffn_forward_body(dims, small_ref, unit_ref, up, down, sems, act_ref, slope_ref)
    unit, inverse = norm_forward(total)
    unit2_ref[...] = unit
    inv2_ref[...] = inverse
    y_ref[...] = unit * segment(small_ref, 6, width) + segment(small_ref, 7, width)


def ffn_forward(dims, parts, pos, unit, small):
    parts = needed_parts(dims, parts, ("up", "down"))
    flat = [a for p in parts for a in p.flat()]
    rows, width, ffn = dims.rows, dims.model, dims.ffn
    return pl.pallas_call(
        functools.partial(ffn_forward_kernel, dims, parts),
        in_specs=[SMEM, VMEM, VMEM] + [HBM] * len(flat),
        out_specs=[VMEM] * 5,
        out_shape=[
            shape((rows, ffn), BF),
            shape((rows, ffn), BF),
            shape((rows, width), F32),
            shape((rows, 1), F32),
            shape((rows, width), F32),
        ],
        scratch_shapes=[
            pltpu.VMEM((width, ffn), BF),
            pltpu.VMEM((ffn, width), BF),
            pltpu.SemaphoreType.DMA((2,)),
        ],
        compiler_params=pltpu.CompilerParams(vmem_limit_bytes=VMEM_LIMIT),
        cost_estimate=pl.CostEstimate(
            flops=4 * rows * width * ffn, bytes_accessed=24 << 20, transcendentals=3 << 20
        ),
        name="ffn_forward",
    )(pos, unit, small, *flat)


def ffn_backward_body(
    dims, outs_parts, outs, pos, gy, small_ref, unit_ref, inv_ref, ctx_ref, unit2, inv2, act_ref, slope_ref,
    up, down, wo, grad_up, grad_down, grad_o, sem_out, gz1_ref, gctx_ref, sums_ref, wait_o,
):
    width = dims.model
    gain1, gain2 = segment(small_ref, 4, width), segment(small_ref, 6, width)

    def put(number, values):
        sums_ref[0:1, number * width : (number + 1) * width] = values

    put(6, col_sum(gy * unit2))
    put(7, col_sum(gy))
    gz2 = norm_backward(gy, unit2, inv2, gain2)
    gf = gz2.astype(BF)
    put(3, col_sum(gf))
    hb = (unit_ref[...] * gain1 + segment(small_ref, 5, width)).astype(BF)
    gh1 = gz2
    block = dims.block
    for n in range(dims.ffn // width):
        cols = slice(n * width, (n + 1) * width)
        gu = (slope_ref[:, cols].astype(F32) * mm_bt(gf, down[cols, :])).astype(BF)
        put(8 + n, col_sum(gu))
        grad_up[:, cols] = mm_at(hb, gu).astype(BF)
        grad_down[cols, :] = mm_at(act_ref[:, cols], gf).astype(BF)
        low, high = n * width, (n + 1) * width
        start_stores(
            dims, outs_parts, outs, pos,
            [p for p in dims.places["up"] if low <= p[2] < high], grad_up, sem_out.at[0],
        )
        start_stores(
            dims, outs_parts, outs, pos,
            [p for p in dims.places["down"] if low <= p[1] < high], grad_down, sem_out.at[1],
        )
        gh1 = gh1 + mm_bt(gu, up[:, cols])
    unit = unit_ref[...]
    put(4, col_sum(gh1 * unit))
    put(5, col_sum(gh1))
    gz1 = norm_backward(gh1, unit, inv_ref[...], gain1)
    gz1_ref[...] = gz1
    ga = gz1.astype(BF)
    put(2, col_sum(ga))
    grad_o[...] = mm_at(ctx_ref[...], ga).astype(BF)
    start_stores(dims, outs_parts, outs, pos, dims.places["o"], grad_o, sem_out.at[2])
    wait_o()
    gctx_ref[...] = mm_bt(ga, wo[...]).astype(BF)
    put(0, jnp.zeros((1, width), F32))
    put(1, jnp.zeros((1, width), F32))
    wait_for(grad_up, sem_out.at[0])
    wait_for(grad_down, sem_out.at[1])
    wait_for(grad_o, sem_out.at[2])


def grad_shapes(dims, parts):
    return [
        shape((2, 2, len(p.zs), len(p.js), dims.piece, dims.block), BF) for p in parts for _ in range(2)
    ]


def pair_up(arrays, parts):
    return [Part(p.zs, p.js, p.last, list(arrays[2 * n : 2 * n + 2])) for n, p in enumerate(parts)]


def ffn_backward_kernel(dims, parts, outs_parts, pos_ref, gy_ref, small_ref, unit_ref, inv_ref, ctx_ref, unit2_ref, inv2_ref, act_ref, slope_ref, *rest):
    refs, rest = unflatten(rest, parts)
    gz1_ref, gctx_ref, sums_ref, *rest = rest
    count = 2 * len(outs_parts)
    outs = [rest[2 * n : 2 * n + 2] for n in range(len(outs_parts))]
    up, down, wo, grad_up, grad_down, grad_o, sems, sem_out = rest[count:]
    pos = (pos_ref[1], pos_ref[2], pos_ref[3])
    start_loads(dims, parts, refs, pos, "down", down, 0, 0, sems.at[1])
    start_loads(dims, parts, refs, pos, "up", up, 0, 0, sems.at[0])
    start_loads(dims, parts, refs, pos, "o", wo, 0, 0, sems.at[2])
    wait_for(down, sems.at[1])
    wait_for(up, sems.at[0])
    ffn_backward_body(
        dims, outs_parts, outs, pos, gy_ref[...], small_ref, unit_ref, inv_ref, ctx_ref,
        unit2_ref[...], inv2_ref[...], act_ref, slope_ref, up, down, wo, grad_up, grad_down, grad_o,
        sem_out, gz1_ref, gctx_ref, sums_ref, lambda: wait_for(wo, sems.at[2]),
    )


def ffn_backward(dims, parts, outs_parts, pos, gy, small, unit, inv, ctx, unit2, inv2, act, slope):
    parts = needed_parts(dims, parts, ("up", "down", "o"))
    flat = [a for p in parts for a in p.flat()]
    rows, width, ffn = dims.rows, dims.model, dims.ffn
    grads = grad_shapes(dims, outs_parts)
    out = pl.pallas_call(
        functools.partial(ffn_backward_kernel, dims, parts, outs_parts),
        in_specs=[SMEM] + [VMEM] * 9 + [HBM] * len(flat),
        out_specs=[VMEM] * 3 + [HBM] * len(grads),
        out_shape=[
            shape((rows, width), F32),
            shape((rows, width), BF),
            shape((1, small.shape[1]), F32),
        ]
        + grads,
        scratch_shapes=[
            pltpu.VMEM((width, ffn), BF),
            pltpu.VMEM((ffn, width), BF),
            pltpu.VMEM((width, width), BF),
            pltpu.VMEM((width, ffn), BF),
            pltpu.VMEM((ffn, width), BF),
            pltpu.VMEM((width, width), BF),
            pltpu.SemaphoreType.DMA((3,)),
            pltpu.SemaphoreType.DMA((3,)),
        ],
        compiler_params=pltpu.CompilerParams(vmem_limit_bytes=VMEM_LIMIT),
        cost_estimate=pl.CostEstimate(
            flops=8 * rows * width * ffn + 4 * rows * width * width, bytes_accessed=40 << 20, transcendentals=0
        ),
        name="ffn_backward",
    )(pos, gy, small, unit, inv, ctx, unit2, inv2, act, slope, *flat)
    return out[0], out[1], out[2], pair_up(out[3:], outs_parts)


def ffn_both_kernel(dims, parts, outs_parts, chains, pos_ref, len_ref, cot_ref, small_ref, unit_ref, inv_ref, ctx_ref, *rest):
    refs, rest = unflatten(rest, parts)
    y_ref, gz1_ref, gctx_ref, sums_ref, *rest = rest
    count = 2 * len(outs_parts)
    outs = [rest[2 * n : 2 * n + 2] for n in range(len(outs_parts))]
    up, down, wo, act_ref, slope_ref, grad_up, grad_down, grad_o, sems, sem_out = rest[count:]
    pos = (pos_ref[1], pos_ref[2], pos_ref[3])
    start_loads(dims, parts, refs, pos, "up", up, 0, 0, sems.at[0])
    start_loads(dims, parts, refs, pos, "down", down, 0, 0, sems.at[1])
    start_loads(dims, parts, refs, pos, "o", wo, 0, 0, sems.at[2])
    width, seq = dims.model, dims.rows // chains
    total = ffn_forward_body(dims, small_ref, unit_ref, up, down, sems, act_ref, slope_ref)
    unit2, inv2 = norm_forward(total)
    y_ref[...] = (unit2 * segment(small_ref, 6, width) + segment(small_ref, 7, width)).astype(BF)
    place = lax.broadcasted_iota(jnp.int32, (seq, width), 0)
    gy = jnp.concatenate(
        [
            jnp.where(place < len_ref[i], cot_ref[i * seq : (i + 1) * seq, :].astype(F32), 0.0)
            for i in range(chains)
        ],
        axis=0,
    )
    ffn_backward_body(
        dims, outs_parts, outs, pos, gy, small_ref, unit_ref, inv_ref, ctx_ref,
        unit2, inv2, act_ref, slope_ref, up, down, wo, grad_up, grad_down, grad_o,
        sem_out, gz1_ref, gctx_ref, sums_ref, lambda: wait_for(wo, sems.at[2]),
    )


def ffn_both(dims, parts, outs_parts, pos, lengths, cot, small, unit, inv, ctx):
    parts = needed_parts(dims, parts, ("up", "down", "o"))
    flat = [a for p in parts for a in p.flat()]
    rows, width, ffn = dims.rows, dims.model, dims.ffn
    grads = grad_shapes(dims, outs_parts)
    out = pl.pallas_call(
        functools.partial(ffn_both_kernel, dims, parts, outs_parts, lengths.shape[0]),
        in_specs=[SMEM, SMEM] + [VMEM] * 5 + [HBM] * len(flat),
        out_specs=[VMEM] * 4 + [HBM] * len(grads),
        out_shape=[
            shape((rows, width), BF),
            shape((rows, width), F32),
            shape((rows, width), BF),
            shape((1, small.shape[1]), F32),
        ]
        + grads,
        scratch_shapes=[
            pltpu.VMEM((width, ffn), BF),
            pltpu.VMEM((ffn, width), BF),
            pltpu.VMEM((width, width), BF),
            pltpu.VMEM((rows, ffn), BF),
            pltpu.VMEM((rows, ffn), BF),
            pltpu.VMEM((width, ffn), BF),
            pltpu.VMEM((ffn, width), BF),
            pltpu.VMEM((width, width), BF),
            pltpu.SemaphoreType.DMA((3,)),
            pltpu.SemaphoreType.DMA((3,)),
        ],
        compiler_params=pltpu.CompilerParams(vmem_limit_bytes=VMEM_LIMIT),
        cost_estimate=pl.CostEstimate(
            flops=12 * rows * width * ffn + 4 * rows * width * width,
            bytes_accessed=40 << 20,
            transcendentals=3 << 20,
        ),
        name="ffn_both",
    )(pos, lengths, cot, small, unit, inv, ctx, *flat)
    return out[0], out[1], out[2], out[3], pair_up(out[4:], outs_parts)


def attention_backward_kernel(dims, parts, outs_parts, chains, pos_ref, len_ref, gz1_ref, gctx_ref, qkv_ref, lse_ref, x_ref, *rest):
    refs, rest = unflatten(rest, parts)
    gx_ref, sums_ref, *rest = rest
    count = 2 * len(outs_parts)
    outs = [rest[2 * n : 2 * n + 2] for n in range(len(outs_parts))]
    w, grads_ref, grad_w, sems, sem_out = rest[count:]
    pos = (pos_ref[1], pos_ref[2], pos_ref[3])
    width, seq = dims.model, dims.rows // chains
    head = width // HEADS
    names = ("q", "k", "v")
    for n, name in enumerate(names):
        start_loads(dims, parts, refs, pos, name, w, 0, n * width, sems.at[n])
    low, masks = half_masks(head)
    scale = head**-0.5

    def chain(i, carry):
        rows = pl.ds(pl.multiple_of(i * seq, 16), seq)
        valid = lax.broadcasted_iota(jnp.int32, (seq, seq), 0) < len_ref[i]
        for pair in range(HEADS // 2):
            at = pair * 2 * head
            q = qkv_ref[rows, at : at + 2 * head]
            k = qkv_ref[rows, width + at : width + at + 2 * head]
            v = qkv_ref[rows, 2 * width + at : 2 * width + at + 2 * head]
            g = gctx_ref[rows, at : at + 2 * head]
            gq, gk, gv = [], [], []
            for h in range(2):
                s = jnp.where(valid, mm_bt(k, q * masks[h]) * scale, -1000000000.0)
                p = jnp.exp(s - lse_ref[i, 2 * pair + h : 2 * pair + h + 1, :])
                gp = mm_bt(v, g * masks[h])
                inner = jnp.sum(p * gp, axis=0, keepdims=True)
                gs = (p * (gp - inner)).astype(BF)
                gv.append(mm(p.astype(BF), g))
                gk.append(mm(gs, q))
                gq.append(mm_at(gs, k))
            grads_ref[rows, at : at + 2 * head] = (jnp.where(low, gq[0], gq[1]) * scale).astype(BF)
            grads_ref[rows, width + at : width + at + 2 * head] = (
                jnp.where(low, gk[0], gk[1]) * scale
            ).astype(BF)
            grads_ref[rows, 2 * width + at : 2 * width + at + 2 * head] = jnp.where(
                low, gv[0], gv[1]
            ).astype(BF)
        return carry

    lax.fori_loop(0, chains, chain, 0)
    xb = x_ref[...].astype(BF)
    for n, name in enumerate(names):
        cols = slice(n * width, (n + 1) * width)
        grad_w[:, cols] = mm_at(xb, grads_ref[:, cols]).astype(BF)
        places = [(b, r, c + n * width) for b, r, c in dims.places[name]]
        start_stores(dims, outs_parts, outs, pos, places, grad_w, sem_out)
    sums_ref[0:1, :width] = col_sum(grads_ref[:, :width])
    sums_ref[0:1, width:] = col_sum(grads_ref[:, 2 * width :])
    gx = gz1_ref[...]
    for n in range(3):
        cols = slice(n * width, (n + 1) * width)
        wait_for(w.at[:, cols], sems.at[n])
        gx = gx + mm_bt(grads_ref[:, cols], w[:, cols])
    gx_ref[...] = gx
    wait_for(grad_w, sem_out)


def attention_backward(dims, parts, outs_parts, pos, lengths, gz1, gctx, qkv, lse, x):
    parts = needed_parts(dims, parts, ("q", "k", "v"))
    flat = [a for p in parts for a in p.flat()]
    rows, width = dims.rows, dims.model
    grads = grad_shapes(dims, outs_parts)
    out = pl.pallas_call(
        functools.partial(attention_backward_kernel, dims, parts, outs_parts, lengths.shape[0]),
        in_specs=[SMEM, SMEM] + [VMEM] * 5 + [HBM] * len(flat),
        out_specs=[VMEM] * 2 + [HBM] * len(grads),
        out_shape=[shape((rows, width), F32), shape((1, 2 * width), F32)] + grads,
        scratch_shapes=[
            pltpu.VMEM((width, 3 * width), BF),
            pltpu.VMEM((rows, 3 * width), BF),
            pltpu.VMEM((width, 3 * width), BF),
            pltpu.SemaphoreType.DMA((3,)),
            pltpu.SemaphoreType.DMA,
        ],
        compiler_params=pltpu.CompilerParams(vmem_limit_bytes=VMEM_LIMIT),
        cost_estimate=pl.CostEstimate(
            flops=24 * rows * width * width, bytes_accessed=24 << 20, transcendentals=1 << 20
        ),
        name="attention_backward",
    )(pos, lengths, gz1, gctx, qkv, lse, x, *flat)
    return out[0], out[1], pair_up(out[2:], outs_parts)


class AnySlice:
    def __init__(self, dims):
        self.dims = dims
        own = range(dims.own)
        self.early = [Part((1, 2, 3), own, "y", None)]
        self.late = [Part((0,), own, "y", None)]

    def position(self):
        return jnp.zeros((4,), jnp.int32)

    def gather(self, low, layer):
        dims = self.dims
        whole = lax.all_gather(low, "fsdp", axis=1, tiled=True)
        whole = lax.all_gather(whole, "grp", axis=0, tiled=True)
        split = whole.reshape(Z_SLABS, 2, dims.own, 2, 2, dims.piece, dims.block)
        arrays = [[split[:, :, :, dy, dc].transpose(1, 0, 2, 3, 4) for dy in range(2)] for dc in range(2)]
        return [Part(range(Z_SLABS), range(dims.own), "y", arrays)]

    def reduce(self, early, late, layer):
        dims = self.dims
        pieces = []
        for part in (late[0], early[0]):
            stacked = jnp.stack(part.arrays)
            pieces.append(stacked.transpose(3, 2, 4, 1, 0, 5, 6))
        whole = jnp.concatenate(pieces, axis=0).reshape(dims.blocks, dims.block, dims.block)
        rows = lax.psum_scatter(whole, "fsdp", scatter_dimension=1, tiled=True)
        return lax.psum_scatter(rows, "grp", scatter_dimension=0, tiled=True).astype(F32)

    def small_sum(self, values):
        return lax.psum(values, ("grp", "fsdp"))

    def group(self, owned):
        return lax.all_gather(owned, "fsdp", axis=1, tiled=True)


def local(
    inputs,
    lengths,
    cotangent,
    masters,
    small_params,
    small_moments,
    left_stats,
    right_stats,
    left_roots,
    right_roots,
):
    chains, seq, width = inputs.shape
    rows = chains * seq
    groups, shards = lax.axis_size("grp"), lax.axis_size("fsdp")
    block = masters.shape[3]
    own_rows = masters.shape[2]
    ffn = small_params.shape[1] - 8 * width
    dims = Dims(width, ffn, block, groups * masters.shape[1], rows)
    net = AnySlice(dims)
    pos = net.position()
    low = [masters[n].astype(BF) for n in range(LAYERS)]
    weights = [net.gather(low[n], n) for n in range(LAYERS)]
    small = [small_params[n : n + 1] for n in range(LAYERS)]
    last = LAYERS - 1

    x = inputs.reshape(rows, width)
    saved = []
    for n in range(LAYERS):
        qkv, lse, ctx, unit, inv = attention_forward(dims, weights[n], pos, lengths, x, small[n])
        if n < last:
            act, slope, unit2, inv2, y = ffn_forward(dims, weights[n], pos, unit, small[n])
            saved.append((x, qkv, lse, ctx, unit, inv, act, slope, unit2, inv2))
            x = y
        else:
            saved.append((x, qkv, lse, ctx, unit, inv))

    owned = [None] * LAYERS
    sums = [None] * LAYERS
    gy = None
    for n in reversed(range(LAYERS)):
        if n == last:
            x, qkv, lse, ctx, unit, inv = saved[n]
            cot = cotangent.reshape(rows, width)
            y, gz1, gctx, sums_a, early = ffn_both(
                dims, weights[n], net.early, pos, lengths, cot, small[n], unit, inv, ctx
            )
            activations = y.reshape(chains, seq, width)
        else:
            x, qkv, lse, ctx, unit, inv, act, slope, unit2, inv2 = saved[n]
            gz1, gctx, sums_a, early = ffn_backward(
                dims, weights[n], net.early, pos, gy, small[n], unit, inv, ctx, unit2, inv2, act, slope
            )
        gy, sums_b, late = attention_backward(
            dims, weights[n], net.late, pos, lengths, gz1, gctx, qkv, lse, x
        )
        owned[n] = net.reduce(early, late, n)
        sums[n] = jnp.concatenate([sums_b[0], sums_a[0, 2 * width :]])
    input_grad = gy.reshape(chains, seq, width)

    small_grads = net.small_sum(jnp.stack(sums))
    blocked_weight_gradients = jnp.stack(owned)
    new_left, new_right, new_masters = [], [], []
    first_row = lax.axis_index("fsdp") * own_rows
    highest = lax.Precision.HIGHEST
    for n in range(LAYERS):
        whole = net.group(owned[n].astype(BF)).astype(F32)
        roots = net.group(right_roots[n].astype(BF)).astype(F32)
        columns = lax.dynamic_slice_in_dim(whole, first_row, own_rows, 2)
        new_left.append(
            decay_rate * left_stats[n]
            + (1.0 - decay_rate) * jnp.einsum("brk,bck->brc", owned[n], whole, precision=highest)
        )
        new_right.append(
            decay_rate * right_stats[n]
            + (1.0 - decay_rate) * jnp.einsum("bkr,bkc->brc", columns, whole, precision=highest)
        )
        mixed = jnp.einsum("brk,bkc->brc", whole, roots, precision=highest)
        update = jnp.einsum("brk,bkc->brc", left_roots[n], mixed, precision=highest)
        new_masters.append(masters[n] - matrix_rate * update)
    new_masters = jnp.stack(new_masters)
    new_moments = decay_rate * small_moments + (1.0 - decay_rate) * small_grads * small_grads
    new_small = small_params - small_rate * small_grads / (jnp.sqrt(new_moments) + moment_epsilon)
    return (
        activations,
        input_grad,
        blocked_weight_gradients,
        small_grads,
        new_moments,
        new_small,
        jnp.stack(new_left),
        jnp.stack(new_right),
        new_masters,
        new_masters.astype(BF),
    )


def solution(mesh):
    tokens, blocks = P(("grp", "fsdp"), None, None), P(None, "grp", "fsdp", None)
    return jax.shard_map(
        local,
        mesh=mesh,
        in_specs=(tokens, P(("grp", "fsdp")), tokens, blocks, P(), P(), blocks, blocks, blocks, blocks),
        out_specs=(tokens, tokens, blocks, P(), P(), P(), blocks, blocks, blocks, blocks),
        check_vma=False,
    )
```

```python
import functools

import jax
import jax.numpy as jnp
from jax import lax
from jax.experimental import pallas as pl
from jax.experimental.pallas import tpu as pltpu
from jax.sharding import PartitionSpec as P

HEADS = 12
LAYERS = 2
Z_SLABS = 4
BF = jnp.bfloat16
F32 = jnp.float32

norm_epsilon = 1e-05
matrix_rate = 1.0
small_rate = 0.3
decay_rate = 0.5
moment_epsilon = 1e-08

VMEM = pl.BlockSpec(memory_space=pltpu.VMEM)
SMEM = pl.BlockSpec(memory_space=pltpu.SMEM)
HBM = pl.BlockSpec(memory_space=pl.ANY)
VMEM_LIMIT = 56 * 1024 * 1024


def shape(dims, dtype):
    return jax.ShapeDtypeStruct(tuple(dims), dtype)


def mm(a, b):
    return jnp.dot(a, b, preferred_element_type=F32)


def mm_bt(a, b):
    return lax.dot_general(a, b, (((1,), (1,)), ((), ())), preferred_element_type=F32)


def mm_at(a, b):
    return lax.dot_general(a, b, (((0,), (0,)), ((), ())), preferred_element_type=F32)


class Part:
    def __init__(self, zs, js, last, arrays):
        self.zs, self.js, self.last, self.arrays = tuple(zs), tuple(js), last, arrays

    def flat(self):
        return [a for row in self.arrays for a in row]


class Dims:
    def __init__(self, model, ffn, block, blocks, rows):
        self.model, self.ffn, self.block, self.blocks, self.rows = model, ffn, block, blocks, rows
        self.own = blocks // (2 * Z_SLABS)
        self.piece = block // 4
        wide, tall = model // block, ffn // block
        self.places = {}
        at = 0
        for name, rows_, cols_ in (
            ("q", wide, wide),
            ("k", wide, wide),
            ("v", wide, wide),
            ("o", wide, wide),
            ("up", wide, tall),
            ("down", tall, wide),
        ):
            self.places[name] = [
                (at + r * cols_ + c, r * block, c * block) for r in range(rows_) for c in range(cols_)
            ]
            at += rows_ * cols_

    def where(self, b):
        return b // (2 * self.own), (b // self.own) % 2, b % self.own


def find_part(parts, z, j):
    for number, part in enumerate(parts):
        if z in part.zs and j in part.js:
            return number, part.zs.index(z), part.js.index(j)
    raise ValueError("no part")


def needed_parts(dims, parts, names):
    used = set()
    for name in names:
        for b, _, _ in dims.places[name]:
            z, _, j = dims.where(b)
            used.add(find_part(parts, z, j)[0])
    return [parts[n] for n in sorted(used)]


def start_loads(dims, parts, refs, pos, name, dst, row0, col0, sem):
    x, y, c = pos
    piece = dims.piece

    def rows_at(base, quarter):
        return pl.ds(pl.multiple_of(base + piece * quarter, 16), piece)

    later = []
    for b, r, col in dims.places[name]:
        z, xq, j = dims.where(b)
        number, zi, ji = find_part(parts, z, j)
        cols = pl.ds(col0 + col, dims.block)
        if parts[number].last == "y":
            for dc in range(2):
                for dy in range(2):
                    src = refs[number][dc][dy].at[x ^ xq, zi, ji]
                    rows = rows_at(row0 + r, 2 * (y ^ dy) + (c ^ dc))
                    pltpu.make_async_copy(src, dst.at[rows, cols], sem).start()
        else:
            later.append((number, zi, ji, xq, r, cols))
    if later:
        for own_x in range(2):

            @pl.when(x == own_x)
            def _(own_x=own_x):
                for number, zi, ji, xq, r, cols in later:
                    for dc in range(2):
                        for yq in range(2):
                            src = refs[number][dc][own_x ^ xq].at[y ^ yq, zi, ji]
                            rows = rows_at(row0 + r, 2 * yq + (c ^ dc))
                            pltpu.make_async_copy(src, dst.at[rows, cols], sem).start()


def wait_for(ref, sem):
    pltpu.make_async_copy(ref, ref, sem).wait()


def start_stores(dims, parts, outs, pos, places, src, sem):
    x, y, c = pos
    piece = dims.piece
    for b, r, col in places:
        z, xq, j = dims.where(b)
        number, zi, ji = find_part(parts, z, j)
        for dc in range(2):
            for yq in range(2):
                rows = pl.ds(pl.multiple_of(r + piece * (2 * yq + (c ^ dc)), 16), piece)
                first, second = y ^ yq, x ^ xq
                if parts[number].last == "x":
                    first, second = second, first
                dst = outs[number][dc].at[first, second, zi, ji]
                pltpu.make_async_copy(src.at[rows, pl.ds(col, dims.block)], dst, sem).start()


def norm_forward(values):
    center = values - jnp.mean(values, axis=-1, keepdims=True)
    spread = jnp.mean(center * center, axis=-1, keepdims=True)
    inverse = lax.rsqrt(spread + norm_epsilon)
    return center * inverse, inverse


def norm_backward(gradient, unit, inverse, gain):
    scaled = gradient * gain
    inner = (
        scaled
        - jnp.mean(scaled, axis=-1, keepdims=True)
        - unit * jnp.mean(scaled * unit, axis=-1, keepdims=True)
    )
    return inverse * inner


def col_sum(values):
    return jnp.sum(values.astype(F32), axis=0, keepdims=True)


def segment(small_ref, number, width):
    return small_ref[0:1, number * width : (number + 1) * width]


def unflatten(refs, parts):
    out, at = [], 0
    for part in parts:
        rows = []
        for row in part.arrays:
            rows.append(refs[at : at + len(row)])
            at += len(row)
        out.append(rows)
    return out, refs[at:]


def half_masks(head):
    lane = lax.broadcasted_iota(jnp.int32, (1, 2 * head), 1)
    low = lane < head
    ones = jnp.where(low, 1.0, 0.0).astype(F32)
    return low, (ones.astype(BF), (1.0 - ones).astype(BF))


def attention_forward_kernel(dims, parts, chains, pos_ref, len_ref, x_ref, small_ref, *rest):
    refs, rest = unflatten(rest, parts)
    qkv_ref, lse_ref, ctx_ref, unit_ref, inv_ref, w, sems = rest
    width, seq = dims.model, dims.rows // chains
    head = width // HEADS
    pos = (pos_ref[1], pos_ref[2], pos_ref[3])
    for n, name in enumerate(("q", "k", "v", "o")):
        start_loads(dims, parts, refs, pos, name, w, 0, n * width, sems.at[n])
    xb = x_ref[...].astype(BF)
    for n, bias in ((0, 0), (1, None), (2, 1)):
        cols = slice(n * width, (n + 1) * width)
        wait_for(w.at[:, cols], sems.at[n])
        out = mm(xb, w[:, cols])
        if bias is not None:
            out = out + segment(small_ref, bias, width)
        qkv_ref[:, cols] = out.astype(BF)
    low, masks = half_masks(head)
    scale = head**-0.5

    def chain(i, carry):
        rows = pl.ds(pl.multiple_of(i * seq, 16), seq)
        valid = lax.broadcasted_iota(jnp.int32, (seq, seq), 0) < len_ref[i]
        for pair in range(HEADS // 2):
            at = pair * 2 * head
            q = qkv_ref[rows, at : at + 2 * head]
            k = qkv_ref[rows, width + at : width + at + 2 * head]
            v = qkv_ref[rows, 2 * width + at : 2 * width + at + 2 * head]
            outs = []
            for h in range(2):
                s = jnp.where(valid, mm_bt(k, q * masks[h]) * scale, -1000000000.0)
                top = jnp.max(s, axis=0, keepdims=True)
                e = jnp.exp(s - top)
                total = jnp.sum(e, axis=0, keepdims=True)
                lse_ref[i, 2 * pair + h : 2 * pair + h + 1, :] = top + jnp.log(total)
                outs.append(mm_at((e * (1.0 / total)).astype(BF), v))
            ctx_ref[rows, at : at + 2 * head] = jnp.where(low, outs[0], outs[1]).astype(BF)
        return carry

    lax.fori_loop(0, chains, chain, 0)
    wait_for(w.at[:, 3 * width :], sems.at[3])
    attended = mm(ctx_ref[...], w[:, 3 * width :]) + segment(small_ref, 2, width)
    unit, inverse = norm_forward(x_ref[...].astype(F32) + attended)
    unit_ref[...] = unit
    inv_ref[...] = inverse


def attention_forward(dims, parts, pos, lengths, x, small):
    parts = needed_parts(dims, parts, ("q", "k", "v", "o"))
    chains = lengths.shape[0]
    seq, width = dims.rows // chains, dims.model
    flat = [a for p in parts for a in p.flat()]
    return pl.pallas_call(
        functools.partial(attention_forward_kernel, dims, parts, chains),
        in_specs=[SMEM, SMEM, VMEM, VMEM] + [HBM] * len(flat),
        out_specs=[VMEM] * 5,
        out_shape=[
            shape((dims.rows, 3 * width), BF),
            shape((chains, HEADS, seq), F32),
            shape((dims.rows, width), BF),
            shape((dims.rows, width), F32),
            shape((dims.rows, 1), F32),
        ],
        scratch_shapes=[pltpu.VMEM((width, 4 * width), BF), pltpu.SemaphoreType.DMA((4,))],
        compiler_params=pltpu.CompilerParams(vmem_limit_bytes=VMEM_LIMIT),
        cost_estimate=pl.CostEstimate(
            flops=12 * dims.rows * width * width, bytes_accessed=16 << 20, transcendentals=1 << 20
        ),
        name="attention_forward",
    )(pos, lengths, x, small, *flat)


def ffn_forward_body(dims, small_ref, unit_ref, up, down, sems, act_ref, slope_ref):
    width = dims.model
    h1 = unit_ref[...] * segment(small_ref, 4, width) + segment(small_ref, 5, width)
    hb = h1.astype(BF)
    total = h1 + segment(small_ref, 3, width)
    wait_for(up, sems.at[0])
    for n in range(dims.ffn // width):
        cols = slice(n * width, (n + 1) * width)
        u = mm(hb, up[:, cols]) + segment(small_ref, 8 + n, width)
        cdf = 0.5 * (1.0 + lax.erf(u * 0.7071067811865476))
        act = (u * cdf).astype(BF)
        act_ref[:, cols] = act
        slope_ref[:, cols] = (cdf + u * (0.3989422804014327 * jnp.exp(-0.5 * u * u))).astype(BF)
        if n == 0:
            wait_for(down, sems.at[1])
        total = total + mm(act, down[cols, :])
    return total


def ffn_forward_kernel(dims, parts, pos_ref, unit_ref, small_ref, *rest):
    refs, rest = unflatten(rest, parts)
    act_ref, slope_ref, unit2_ref, inv2_ref, y_ref, up, down, sems = rest
    pos = (pos_ref[1], pos_ref[2], pos_ref[3])
    start_loads(dims, parts, refs, pos, "up", up, 0, 0, sems.at[0])
    start_loads(dims, parts, refs, pos, "down", down, 0, 0, sems.at[1])
    width = dims.model
    total = ffn_forward_body(dims, small_ref, unit_ref, up, down, sems, act_ref, slope_ref)
    unit, inverse = norm_forward(total)
    unit2_ref[...] = unit
    inv2_ref[...] = inverse
    y_ref[...] = unit * segment(small_ref, 6, width) + segment(small_ref, 7, width)


def ffn_forward(dims, parts, pos, unit, small):
    parts = needed_parts(dims, parts, ("up", "down"))
    flat = [a for p in parts for a in p.flat()]
    rows, width, ffn = dims.rows, dims.model, dims.ffn
    return pl.pallas_call(
        functools.partial(ffn_forward_kernel, dims, parts),
        in_specs=[SMEM, VMEM, VMEM] + [HBM] * len(flat),
        out_specs=[VMEM] * 5,
        out_shape=[
            shape((rows, ffn), BF),
            shape((rows, ffn), BF),
            shape((rows, width), F32),
            shape((rows, 1), F32),
            shape((rows, width), F32),
        ],
        scratch_shapes=[
            pltpu.VMEM((width, ffn), BF),
            pltpu.VMEM((ffn, width), BF),
            pltpu.SemaphoreType.DMA((2,)),
        ],
        compiler_params=pltpu.CompilerParams(vmem_limit_bytes=VMEM_LIMIT),
        cost_estimate=pl.CostEstimate(
            flops=4 * rows * width * ffn, bytes_accessed=24 << 20, transcendentals=3 << 20
        ),
        name="ffn_forward",
    )(pos, unit, small, *flat)


def ffn_backward_body(
    dims, outs_parts, outs, pos, gy, small_ref, unit_ref, inv_ref, ctx_ref, unit2, inv2, act_ref, slope_ref,
    up, down, wo, grad_up, grad_down, grad_o, sem_out, gz1_ref, gctx_ref, sums_ref, wait_o,
):
    width = dims.model
    gain1, gain2 = segment(small_ref, 4, width), segment(small_ref, 6, width)

    def put(number, values):
        sums_ref[0:1, number * width : (number + 1) * width] = values

    put(6, col_sum(gy * unit2))
    put(7, col_sum(gy))
    gz2 = norm_backward(gy, unit2, inv2, gain2)
    gf = gz2.astype(BF)
    put(3, col_sum(gf))
    hb = (unit_ref[...] * gain1 + segment(small_ref, 5, width)).astype(BF)
    gh1 = gz2
    block = dims.block
    for n in range(dims.ffn // width):
        cols = slice(n * width, (n + 1) * width)
        gu = (slope_ref[:, cols].astype(F32) * mm_bt(gf, down[cols, :])).astype(BF)
        put(8 + n, col_sum(gu))
        grad_up[:, cols] = mm_at(hb, gu).astype(BF)
        grad_down[cols, :] = mm_at(act_ref[:, cols], gf).astype(BF)
        low, high = n * width, (n + 1) * width
        start_stores(
            dims, outs_parts, outs, pos,
            [p for p in dims.places["up"] if low <= p[2] < high], grad_up, sem_out.at[0],
        )
        start_stores(
            dims, outs_parts, outs, pos,
            [p for p in dims.places["down"] if low <= p[1] < high], grad_down, sem_out.at[1],
        )
        gh1 = gh1 + mm_bt(gu, up[:, cols])
    unit = unit_ref[...]
    put(4, col_sum(gh1 * unit))
    put(5, col_sum(gh1))
    gz1 = norm_backward(gh1, unit, inv_ref[...], gain1)
    gz1_ref[...] = gz1
    ga = gz1.astype(BF)
    put(2, col_sum(ga))
    grad_o[...] = mm_at(ctx_ref[...], ga).astype(BF)
    start_stores(dims, outs_parts, outs, pos, dims.places["o"], grad_o, sem_out.at[2])
    wait_o()
    gctx_ref[...] = mm_bt(ga, wo[...]).astype(BF)
    put(0, jnp.zeros((1, width), F32))
    put(1, jnp.zeros((1, width), F32))
    wait_for(grad_up, sem_out.at[0])
    wait_for(grad_down, sem_out.at[1])
    wait_for(grad_o, sem_out.at[2])


def grad_shapes(dims, parts):
    return [
        shape((2, 2, len(p.zs), len(p.js), dims.piece, dims.block), BF) for p in parts for _ in range(2)
    ]


def pair_up(arrays, parts):
    return [Part(p.zs, p.js, p.last, list(arrays[2 * n : 2 * n + 2])) for n, p in enumerate(parts)]


def ffn_backward_kernel(dims, parts, outs_parts, pos_ref, gy_ref, small_ref, unit_ref, inv_ref, ctx_ref, unit2_ref, inv2_ref, act_ref, slope_ref, *rest):
    refs, rest = unflatten(rest, parts)
    gz1_ref, gctx_ref, sums_ref, *rest = rest
    count = 2 * len(outs_parts)
    outs = [rest[2 * n : 2 * n + 2] for n in range(len(outs_parts))]
    up, down, wo, grad_up, grad_down, grad_o, sems, sem_out = rest[count:]
    pos = (pos_ref[1], pos_ref[2], pos_ref[3])
    start_loads(dims, parts, refs, pos, "down", down, 0, 0, sems.at[1])
    start_loads(dims, parts, refs, pos, "up", up, 0, 0, sems.at[0])
    start_loads(dims, parts, refs, pos, "o", wo, 0, 0, sems.at[2])
    wait_for(down, sems.at[1])
    wait_for(up, sems.at[0])
    ffn_backward_body(
        dims, outs_parts, outs, pos, gy_ref[...], small_ref, unit_ref, inv_ref, ctx_ref,
        unit2_ref[...], inv2_ref[...], act_ref, slope_ref, up, down, wo, grad_up, grad_down, grad_o,
        sem_out, gz1_ref, gctx_ref, sums_ref, lambda: wait_for(wo, sems.at[2]),
    )


def ffn_backward(dims, parts, outs_parts, pos, gy, small, unit, inv, ctx, unit2, inv2, act, slope):
    parts = needed_parts(dims, parts, ("up", "down", "o"))
    flat = [a for p in parts for a in p.flat()]
    rows, width, ffn = dims.rows, dims.model, dims.ffn
    grads = grad_shapes(dims, outs_parts)
    out = pl.pallas_call(
        functools.partial(ffn_backward_kernel, dims, parts, outs_parts),
        in_specs=[SMEM] + [VMEM] * 9 + [HBM] * len(flat),
        out_specs=[VMEM] * 3 + [HBM] * len(grads),
        out_shape=[
            shape((rows, width), F32),
            shape((rows, width), BF),
            shape((1, small.shape[1]), F32),
        ]
        + grads,
        scratch_shapes=[
            pltpu.VMEM((width, ffn), BF),
            pltpu.VMEM((ffn, width), BF),
            pltpu.VMEM((width, width), BF),
            pltpu.VMEM((width, ffn), BF),
            pltpu.VMEM((ffn, width), BF),
            pltpu.VMEM((width, width), BF),
            pltpu.SemaphoreType.DMA((3,)),
            pltpu.SemaphoreType.DMA((3,)),
        ],
        compiler_params=pltpu.CompilerParams(vmem_limit_bytes=VMEM_LIMIT),
        cost_estimate=pl.CostEstimate(
            flops=8 * rows * width * ffn + 4 * rows * width * width, bytes_accessed=40 << 20, transcendentals=0
        ),
        name="ffn_backward",
    )(pos, gy, small, unit, inv, ctx, unit2, inv2, act, slope, *flat)
    return out[0], out[1], out[2], pair_up(out[3:], outs_parts)


def ffn_both_kernel(dims, parts, outs_parts, chains, pos_ref, len_ref, cot_ref, small_ref, unit_ref, inv_ref, ctx_ref, *rest):
    refs, rest = unflatten(rest, parts)
    y_ref, gz1_ref, gctx_ref, sums_ref, *rest = rest
    count = 2 * len(outs_parts)
    outs = [rest[2 * n : 2 * n + 2] for n in range(len(outs_parts))]
    up, down, wo, act_ref, slope_ref, grad_up, grad_down, grad_o, sems, sem_out = rest[count:]
    pos = (pos_ref[1], pos_ref[2], pos_ref[3])
    start_loads(dims, parts, refs, pos, "up", up, 0, 0, sems.at[0])
    start_loads(dims, parts, refs, pos, "down", down, 0, 0, sems.at[1])
    start_loads(dims, parts, refs, pos, "o", wo, 0, 0, sems.at[2])
    width, seq = dims.model, dims.rows // chains
    total = ffn_forward_body(dims, small_ref, unit_ref, up, down, sems, act_ref, slope_ref)
    unit2, inv2 = norm_forward(total)
    y_ref[...] = (unit2 * segment(small_ref, 6, width) + segment(small_ref, 7, width)).astype(BF)
    place = lax.broadcasted_iota(jnp.int32, (seq, width), 0)
    gy = jnp.concatenate(
        [
            jnp.where(place < len_ref[i], cot_ref[i * seq : (i + 1) * seq, :].astype(F32), 0.0)
            for i in range(chains)
        ],
        axis=0,
    )
    ffn_backward_body(
        dims, outs_parts, outs, pos, gy, small_ref, unit_ref, inv_ref, ctx_ref,
        unit2, inv2, act_ref, slope_ref, up, down, wo, grad_up, grad_down, grad_o,
        sem_out, gz1_ref, gctx_ref, sums_ref, lambda: wait_for(wo, sems.at[2]),
    )


def ffn_both(dims, parts, outs_parts, pos, lengths, cot, small, unit, inv, ctx):
    parts = needed_parts(dims, parts, ("up", "down", "o"))
    flat = [a for p in parts for a in p.flat()]
    rows, width, ffn = dims.rows, dims.model, dims.ffn
    grads = grad_shapes(dims, outs_parts)
    out = pl.pallas_call(
        functools.partial(ffn_both_kernel, dims, parts, outs_parts, lengths.shape[0]),
        in_specs=[SMEM, SMEM] + [VMEM] * 5 + [HBM] * len(flat),
        out_specs=[VMEM] * 4 + [HBM] * len(grads),
        out_shape=[
            shape((rows, width), BF),
            shape((rows, width), F32),
            shape((rows, width), BF),
            shape((1, small.shape[1]), F32),
        ]
        + grads,
        scratch_shapes=[
            pltpu.VMEM((width, ffn), BF),
            pltpu.VMEM((ffn, width), BF),
            pltpu.VMEM((width, width), BF),
            pltpu.VMEM((rows, ffn), BF),
            pltpu.VMEM((rows, ffn), BF),
            pltpu.VMEM((width, ffn), BF),
            pltpu.VMEM((ffn, width), BF),
            pltpu.VMEM((width, width), BF),
            pltpu.SemaphoreType.DMA((3,)),
            pltpu.SemaphoreType.DMA((3,)),
        ],
        compiler_params=pltpu.CompilerParams(vmem_limit_bytes=VMEM_LIMIT),
        cost_estimate=pl.CostEstimate(
            flops=12 * rows * width * ffn + 4 * rows * width * width,
            bytes_accessed=40 << 20,
            transcendentals=3 << 20,
        ),
        name="ffn_both",
    )(pos, lengths, cot, small, unit, inv, ctx, *flat)
    return out[0], out[1], out[2], out[3], pair_up(out[4:], outs_parts)


def attention_backward_kernel(dims, parts, outs_parts, chains, pos_ref, len_ref, gz1_ref, gctx_ref, qkv_ref, lse_ref, x_ref, *rest):
    refs, rest = unflatten(rest, parts)
    gx_ref, sums_ref, *rest = rest
    count = 2 * len(outs_parts)
    outs = [rest[2 * n : 2 * n + 2] for n in range(len(outs_parts))]
    w, grads_ref, grad_w, sems, sem_out = rest[count:]
    pos = (pos_ref[1], pos_ref[2], pos_ref[3])
    width, seq = dims.model, dims.rows // chains
    head = width // HEADS
    names = ("q", "k", "v")
    for n, name in enumerate(names):
        start_loads(dims, parts, refs, pos, name, w, 0, n * width, sems.at[n])
    low, masks = half_masks(head)
    scale = head**-0.5

    def chain(i, carry):
        rows = pl.ds(pl.multiple_of(i * seq, 16), seq)
        valid = lax.broadcasted_iota(jnp.int32, (seq, seq), 0) < len_ref[i]
        for pair in range(HEADS // 2):
            at = pair * 2 * head
            q = qkv_ref[rows, at : at + 2 * head]
            k = qkv_ref[rows, width + at : width + at + 2 * head]
            v = qkv_ref[rows, 2 * width + at : 2 * width + at + 2 * head]
            g = gctx_ref[rows, at : at + 2 * head]
            gq, gk, gv = [], [], []
            for h in range(2):
                s = jnp.where(valid, mm_bt(k, q * masks[h]) * scale, -1000000000.0)
                p = jnp.exp(s - lse_ref[i, 2 * pair + h : 2 * pair + h + 1, :])
                gp = mm_bt(v, g * masks[h])
                inner = jnp.sum(p * gp, axis=0, keepdims=True)
                gs = (p * (gp - inner)).astype(BF)
                gv.append(mm(p.astype(BF), g))
                gk.append(mm(gs, q))
                gq.append(mm_at(gs, k))
            grads_ref[rows, at : at + 2 * head] = (jnp.where(low, gq[0], gq[1]) * scale).astype(BF)
            grads_ref[rows, width + at : width + at + 2 * head] = (
                jnp.where(low, gk[0], gk[1]) * scale
            ).astype(BF)
            grads_ref[rows, 2 * width + at : 2 * width + at + 2 * head] = jnp.where(
                low, gv[0], gv[1]
            ).astype(BF)
        return carry

    lax.fori_loop(0, chains, chain, 0)
    xb = x_ref[...].astype(BF)
    for n, name in enumerate(names):
        cols = slice(n * width, (n + 1) * width)
        grad_w[:, cols] = mm_at(xb, grads_ref[:, cols]).astype(BF)
        places = [(b, r, c + n * width) for b, r, c in dims.places[name]]
        start_stores(dims, outs_parts, outs, pos, places, grad_w, sem_out)
    sums_ref[0:1, :width] = col_sum(grads_ref[:, :width])
    sums_ref[0:1, width:] = col_sum(grads_ref[:, 2 * width :])
    gx = gz1_ref[...]
    for n in range(3):
        cols = slice(n * width, (n + 1) * width)
        wait_for(w.at[:, cols], sems.at[n])
        gx = gx + mm_bt(grads_ref[:, cols], w[:, cols])
    gx_ref[...] = gx
    wait_for(grad_w, sem_out)


def attention_backward(dims, parts, outs_parts, pos, lengths, gz1, gctx, qkv, lse, x):
    parts = needed_parts(dims, parts, ("q", "k", "v"))
    flat = [a for p in parts for a in p.flat()]
    rows, width = dims.rows, dims.model
    grads = grad_shapes(dims, outs_parts)
    out = pl.pallas_call(
        functools.partial(attention_backward_kernel, dims, parts, outs_parts, lengths.shape[0]),
        in_specs=[SMEM, SMEM] + [VMEM] * 5 + [HBM] * len(flat),
        out_specs=[VMEM] * 2 + [HBM] * len(grads),
        out_shape=[shape((rows, width), F32), shape((1, 2 * width), F32)] + grads,
        scratch_shapes=[
            pltpu.VMEM((width, 3 * width), BF),
            pltpu.VMEM((rows, 3 * width), BF),
            pltpu.VMEM((width, 3 * width), BF),
            pltpu.SemaphoreType.DMA((3,)),
            pltpu.SemaphoreType.DMA,
        ],
        compiler_params=pltpu.CompilerParams(vmem_limit_bytes=VMEM_LIMIT),
        cost_estimate=pl.CostEstimate(
            flops=24 * rows * width * width, bytes_accessed=24 << 20, transcendentals=1 << 20
        ),
        name="attention_backward",
    )(pos, lengths, gz1, gctx, qkv, lse, x, *flat)
    return out[0], out[1], pair_up(out[2:], outs_parts)


class AnySlice:
    def __init__(self, dims):
        self.dims = dims
        own = range(dims.own)
        self.early = [Part((1, 2, 3), own, "y", None)]
        self.late = [Part((0,), own, "y", None)]

    def position(self):
        return jnp.zeros((4,), jnp.int32)

    def gather(self, low, layer):
        dims = self.dims
        whole = lax.all_gather(low, "fsdp", axis=1, tiled=True)
        whole = lax.all_gather(whole, "grp", axis=0, tiled=True)
        split = whole.reshape(Z_SLABS, 2, dims.own, 2, 2, dims.piece, dims.block)
        arrays = [[split[:, :, :, dy, dc].transpose(1, 0, 2, 3, 4) for dy in range(2)] for dc in range(2)]
        return [Part(range(Z_SLABS), range(dims.own), "y", arrays)]

    def reduce(self, early, late, layer):
        dims = self.dims
        pieces = []
        for part in (late[0], early[0]):
            stacked = jnp.stack(part.arrays)
            pieces.append(stacked.transpose(3, 2, 4, 1, 0, 5, 6))
        whole = jnp.concatenate(pieces, axis=0).reshape(dims.blocks, dims.block, dims.block)
        rows = lax.psum_scatter(whole, "fsdp", scatter_dimension=1, tiled=True)
        return lax.psum_scatter(rows, "grp", scatter_dimension=0, tiled=True).astype(F32)

    def small_sum(self, values):
        return lax.psum(values, ("grp", "fsdp"))

    def group(self, owned):
        return lax.all_gather(owned, "fsdp", axis=1, tiled=True)


def swap_of(axis):
    def move(z, x, y, c):
        return (z, x ^ (axis == "x"), y ^ (axis == "y"), c ^ (axis == "c"))

    return move


class SmallSlice:
    def __init__(self, dims):
        self.dims = dims
        a, b = range(dims.own // 2), range(dims.own // 2, dims.own)
        self.early = [Part((1, 2, 3), a, "y", None), Part((1, 2, 3), b, "x", None)]
        self.late = [Part((0,), a, "y", None), Part((0,), b, "x", None)]
        group, shard = lax.axis_index("grp"), lax.axis_index("fsdp")
        self.z, self.x, self.y, self.c = group // 2, group % 2, shard // 2, shard % 2

    def position(self):
        return jnp.stack([self.z, self.x, self.y, self.c]).astype(jnp.int32)

    def permute(self, array, move):
        pairs = []
        for flat in range(8 * Z_SLABS):
            to = move(flat // 8, flat // 4 % 2, flat // 2 % 2, flat % 2)
            if to is not None:
                pairs.append((flat, ((to[0] * 2 + to[1]) * 2 + to[2]) * 2 + to[3]))
        return lax.ppermute(array, ("grp", "fsdp"), pairs)

    def swap(self, array, axis):
        return self.permute(array, swap_of(axis))

    def slabs(self, own):
        got = [own] + [
            self.permute(own, lambda z, x, y, c, k=k: ((z + k) % Z_SLABS, x, y, c)) for k in range(1, Z_SLABS)
        ]
        stacked = jnp.stack(got)
        return [
            lax.dynamic_index_in_dim(stacked, (self.z - z) % Z_SLABS, 0, keepdims=False)
            for z in range(Z_SLABS)
        ]

    def spread(self, slabs, zs, js):
        half = len(js) // 2
        parts = []
        for pick, first, second in ((slice(0, half), "x", "y"), (slice(half, None), "y", "x")):
            own = jnp.stack([slabs[z][pick] for z in zs])
            own = jnp.stack([own, self.swap(own, first)])
            other = self.swap(own, second)
            arrays = [[own, other], [self.swap(own, "c"), self.swap(other, "c")]]
            parts.append(Part(zs, tuple(js)[pick], second, arrays))
        return parts

    def gather(self, low, layer):
        own = self.dims.own
        if layer == 0:
            third = own // 3
            parts = []
            for js in (range(third), range(third, own)):
                slabs = self.slabs(low[js.start : js.stop])
                parts += self.spread(slabs, range(Z_SLABS), js)
            return parts
        slabs = self.slabs(low)
        return self.spread(slabs, (0, 1), range(own)) + self.spread(slabs, (2, 3), range(own))

    def add(self, a, b):
        return (a.astype(F32) + b.astype(F32)).astype(BF)

    def plane_sum(self, part):
        keep, send = part.arrays
        got = self.swap(send, "c")
        first, second = (part.last, "x" if part.last == "y" else "y")
        got1 = self.swap(self.add(keep[1], got[1]), first)
        kept = self.add(keep[0], got[0])
        got2 = self.swap(self.add(kept[1], got1[1]), second)
        return self.add(self.add(kept[0], got1[0]), got2)

    def reduce(self, early, late, layer):
        z = self.z
        first = jnp.concatenate([self.plane_sum(p) for p in late], axis=1)
        rest = jnp.concatenate([self.plane_sum(p) for p in early], axis=1)
        whole = jnp.concatenate([first, rest], axis=0)

        def piece(k):
            return lax.dynamic_index_in_dim(whole, (z + k) % Z_SLABS, 0, keepdims=False)

        total = piece(0).astype(F32)
        for k in range(1, Z_SLABS):
            got = self.permute(piece(k), lambda z, x, y, c, k=k: ((z + k) % Z_SLABS, x, y, c))
            total = total + got.astype(F32)
        return total

    def small_sum(self, values):
        size = values.shape
        values = values.reshape(-1, 128)
        for axis in ("c", "x", "y"):
            values = values + self.swap(values, axis)
        for bit in (1, 2):
            values = values + self.permute(values, lambda z, x, y, c, bit=bit: (z ^ bit, x, y, c))
        return values.reshape(size)

    def group(self, owned):
        both = jnp.stack([owned, self.swap(owned, "y")])
        return [both, self.swap(both, "c")]


def update_kernel(layer, first, pos_ref, own_ref, left_ref, right_ref, roots_ref, masters_ref, *rest):
    grads, roots, rest = rest[0:2], rest[2:4], rest[4:]
    if not first:
        rest = rest[5:]
    outs, rest = rest[:5], rest[5:]
    g_ref, r_ref, gram_ref, new_left, new_right, new_masters, new_copies, sem_in, sem_out = rest
    y, c = pos_ref[2], pos_ref[3]
    count, piece, block = own_ref.shape

    def quarter(yq, cq):
        return pl.ds(pl.multiple_of(piece * (2 * yq + cq), 16), piece)

    for dc in range(2):
        for dy in range(2):
            rows = quarter(y ^ dy, c ^ dc)
            pltpu.make_async_copy(grads[dc].at[dy], g_ref.at[:, rows, :], sem_in.at[0]).start()
            pltpu.make_async_copy(roots[dc].at[dy], r_ref.at[:, rows, :], sem_in.at[1]).start()
    copies = [pltpu.make_async_copy(own_ref, outs[0].at[layer], sem_out.at[0])]
    copies[0].start()
    wait_for(g_ref, sem_in.at[0])
    wait_for(r_ref, sem_in.at[1])
    own_rows = quarter(y, c)
    for b in range(count):
        g = g_ref[b]
        mine = own_ref[b].astype(BF)
        new_left[b] = decay_rate * left_ref[b] + (1.0 - decay_rate) * mm_bt(mine, g)
        gram_ref[...] = mm_at(g, g)
        new_right[b] = decay_rate * right_ref[b] + (1.0 - decay_rate) * gram_ref[own_rows, :]
        mixed = mm(g, r_ref[b])
        update = jnp.dot(
            roots_ref[b], mixed, preferred_element_type=F32, precision=lax.Precision.HIGHEST
        )
        fresh = masters_ref[b] - matrix_rate * update
        new_masters[b] = fresh
        new_copies[b] = fresh.astype(BF)
    for n, src in enumerate((new_left, new_right, new_masters, new_copies)):
        copies.append(pltpu.make_async_copy(src, outs[n + 1].at[layer], sem_out.at[n + 1]))
        copies[-1].start()
    for copy in copies:
        copy.wait()


def update_layer(layer, pos, own, left, right, left_roots, masters, grads, roots, before):
    count, piece, block = own.shape
    whole = (LAYERS, count, piece, block)
    ins = [pos, own, left, right, left_roots, masters, *grads, *roots]
    specs = [SMEM] + [VMEM] * 5 + [HBM] * 4
    aliases = {}
    if before is not None:
        aliases = {len(ins) + n: n for n in range(5)}
        ins += list(before)
        specs += [HBM] * 5
    return pl.pallas_call(
        functools.partial(update_kernel, layer, before is None),
        in_specs=specs,
        out_specs=[HBM] * 5,
        out_shape=[shape(whole, F32)] * 4 + [shape(whole, BF)],
        input_output_aliases=aliases,
        scratch_shapes=[
            pltpu.VMEM((count, block, block), BF),
            pltpu.VMEM((count, block, block), BF),
            pltpu.VMEM((block, block), F32),
            pltpu.VMEM(own.shape, F32),
            pltpu.VMEM(own.shape, F32),
            pltpu.VMEM(own.shape, F32),
            pltpu.VMEM(own.shape, BF),
            pltpu.SemaphoreType.DMA((2,)),
            pltpu.SemaphoreType.DMA((5,)),
        ],
        compiler_params=pltpu.CompilerParams(vmem_limit_bytes=VMEM_LIMIT),
        cost_estimate=pl.CostEstimate(
            flops=6 * count * block**3, bytes_accessed=16 << 20, transcendentals=0
        ),
        name="update_layer",
    )(*ins)


def update_plain(net, owned, masters, left_stats, right_stats, left_roots, right_roots):
    own_rows = masters.shape[2]
    first_row = lax.axis_index("fsdp") * own_rows
    highest = lax.Precision.HIGHEST
    grads = jnp.stack(owned)
    whole = jnp.stack([net.group(g.astype(BF)) for g in owned]).astype(F32)
    roots = jnp.stack([net.group(right_roots[n].astype(BF)) for n in range(LAYERS)]).astype(F32)
    columns = lax.dynamic_slice_in_dim(whole, first_row, own_rows, 3)
    new_left = decay_rate * left_stats + (1.0 - decay_rate) * jnp.einsum(
        "lbrk,lbck->lbrc", grads, whole, precision=highest
    )
    new_right = decay_rate * right_stats + (1.0 - decay_rate) * jnp.einsum(
        "lbkr,lbkc->lbrc", columns, whole, precision=highest
    )
    mixed = jnp.einsum("lbrk,lbkc->lbrc", whole, roots, precision=highest)
    update = jnp.einsum("lbrk,lbkc->lbrc", left_roots, mixed, precision=highest)
    new_masters = masters - matrix_rate * update
    return grads, new_left, new_right, new_masters, new_masters.astype(BF)


def local(
    inputs,
    lengths,
    cotangent,
    masters,
    small_params,
    small_moments,
    left_stats,
    right_stats,
    left_roots,
    right_roots,
):
    chains, seq, width = inputs.shape
    rows = chains * seq
    groups, shards = lax.axis_size("grp"), lax.axis_size("fsdp")
    block = masters.shape[3]
    ffn = small_params.shape[1] - 8 * width
    dims = Dims(width, ffn, block, groups * masters.shape[1], rows)
    small_slice = groups == 2 * Z_SLABS and shards == 4
    net = SmallSlice(dims) if small_slice else AnySlice(dims)
    pos = net.position()
    low = [masters[n].astype(BF) for n in range(LAYERS)]
    weights = [net.gather(low[n], n) for n in range(LAYERS)]
    small = [small_params[n : n + 1] for n in range(LAYERS)]
    last = LAYERS - 1

    x = inputs.reshape(rows, width)
    saved = []
    for n in range(LAYERS):
        qkv, lse, ctx, unit, inv = attention_forward(dims, weights[n], pos, lengths, x, small[n])
        if n < last:
            act, slope, unit2, inv2, y = ffn_forward(dims, weights[n], pos, unit, small[n])
            saved.append((x, qkv, lse, ctx, unit, inv, act, slope, unit2, inv2))
            x = y
        else:
            saved.append((x, qkv, lse, ctx, unit, inv))
    if small_slice:
        low_roots, unit = lax.optimization_barrier((right_roots, unit))
        roots = [net.group(low_roots[n].astype(BF)) for n in range(LAYERS)]

    owned = [None] * LAYERS
    sums = [None] * LAYERS
    gy, done = None, None
    for n in reversed(range(LAYERS)):
        if n == last:
            x, qkv, lse, ctx, _, inv = saved[n]
            cot = cotangent.reshape(rows, width)
            y, gz1, gctx, sums_a, early = ffn_both(
                dims, weights[n], net.early, pos, lengths, cot, small[n], unit, inv, ctx
            )
            activations = y.reshape(chains, seq, width)
        else:
            x, qkv, lse, ctx, unit, inv, act, slope, unit2, inv2 = saved[n]
            gz1, gctx, sums_a, early = ffn_backward(
                dims, weights[n], net.early, pos, gy, small[n], unit, inv, ctx, unit2, inv2, act, slope
            )
        gy, sums_b, late = attention_backward(
            dims, weights[n], net.late, pos, lengths, gz1, gctx, qkv, lse, x
        )
        owned[n] = net.reduce(early, late, n)
        sums[n] = jnp.concatenate([sums_b[0], sums_a[0, 2 * width :]])
        if small_slice:
            done = update_layer(
                n, pos, owned[n], left_stats[n], right_stats[n], left_roots[n], masters[n],
                net.group(owned[n].astype(BF)), roots[n], done,
            )
    input_grad = gy.reshape(chains, seq, width)
    if not small_slice:
        done = update_plain(net, owned, masters, left_stats, right_stats, left_roots, right_roots)
    weight_grads, new_left, new_right, new_masters, new_copies = done

    small_grads = net.small_sum(jnp.stack(sums))
    new_moments = decay_rate * small_moments + (1.0 - decay_rate) * small_grads * small_grads
    new_small = small_params - small_rate * small_grads / (jnp.sqrt(new_moments) + moment_epsilon)
    return (
        activations,
        input_grad,
        weight_grads,
        small_grads,
        new_moments,
        new_small,
        new_left,
        new_right,
        new_masters,
        new_copies,
    )


def solution(mesh):
    tokens, blocks = P(("grp", "fsdp"), None, None), P(None, "grp", "fsdp", None)
    return jax.shard_map(
        local,
        mesh=mesh,
        in_specs=(tokens, P(("grp", "fsdp")), tokens, blocks, P(), P(), blocks, blocks, blocks, blocks),
        out_specs=(tokens, tokens, blocks, P(), P(), P(), blocks, blocks, blocks, blocks),
        check_vma=False,
    )
```

```python
import functools

import jax
import jax.numpy as jnp
from jax import lax
from jax.experimental import pallas as pl
from jax.experimental.pallas import tpu as pltpu
from jax.sharding import PartitionSpec as P

HEADS = 12
LAYERS = 2
Z_SLABS = 4
BF = jnp.bfloat16
F32 = jnp.float32

norm_epsilon = 1e-05
matrix_rate = 1.0
small_rate = 0.3
decay_rate = 0.5
moment_epsilon = 1e-08

VMEM = pl.BlockSpec(memory_space=pltpu.VMEM)
SMEM = pl.BlockSpec(memory_space=pltpu.SMEM)
ANY = pl.BlockSpec(memory_space=pl.ANY)


def shape(dims, dtype):
    return jax.ShapeDtypeStruct(tuple(dims), dtype)


def mm(a, b):
    return jnp.dot(a, b, preferred_element_type=F32)


def mm_bt(a, b):
    return lax.dot_general(a, b, (((1,), (1,)), ((), ())), preferred_element_type=F32)


def mm_at(a, b):
    return lax.dot_general(a, b, (((0,), (0,)), ((), ())), preferred_element_type=F32)


class Part:
    def __init__(self, zs, js, order, arrays=None):
        self.zs, self.js, self.order, self.arrays = tuple(zs), tuple(js), order, arrays

    def index(self, first, second, z, j):
        place = self.zs.index(z) * len(self.js) + self.js.index(j)
        return (first * 2 + second) * len(self.zs) * len(self.js) + place

    def count(self):
        return 4 * len(self.zs) * len(self.js)


def launch(body, name, ins, out_shape, out_specs, deps=(), scratch=(), cost=None, aliases=None, limit=16, **grid):
    count, extra = len(ins), len(deps)

    def kernel(*refs):
        body(*refs[:count], *refs[count + extra :])

    flops, moved, special = cost or (0, 0, 0)
    return pl.pallas_call(
        kernel,
        in_specs=[spec for _, spec in ins] + [ANY] * extra,
        out_specs=out_specs,
        out_shape=out_shape,
        scratch_shapes=list(scratch),
        input_output_aliases=aliases or {},
        compiler_params=pltpu.CompilerParams(vmem_limit_bytes=limit << 20),
        cost_estimate=pl.CostEstimate(flops=flops, bytes_accessed=moved, transcendentals=special),
        name=name,
        **grid,
    )(*[array for array, _ in ins], *deps)


class Dims:
    def __init__(self, model, ffn, block, blocks, rows):
        self.model, self.ffn, self.block, self.blocks, self.rows = model, ffn, block, blocks, rows
        self.own = blocks // (2 * Z_SLABS)
        self.piece = block // 4
        wide, tall = model // block, ffn // block
        self.places = {}
        at = 0
        for name, rows_, cols_ in (
            ("q", wide, wide),
            ("k", wide, wide),
            ("v", wide, wide),
            ("o", wide, wide),
            ("up", wide, tall),
            ("down", tall, wide),
        ):
            self.places[name] = [
                (at + r * cols_ + c, r * block, c * block) for r in range(rows_) for c in range(cols_)
            ]
            at += rows_ * cols_

    def where(self, b):
        return b // (2 * self.own), (b // self.own) % 2, b % self.own


def find_part(parts, z, j):
    for number, part in enumerate(parts):
        if z in part.zs and j in part.js:
            return number
    raise ValueError("no part")


def needed_parts(dims, parts, names):
    used = set()
    for name in names:
        for b, _, _ in dims.places[name]:
            z, _, j = dims.where(b)
            used.add(find_part(parts, z, j))
    return [parts[n] for n in sorted(used)]


def start_loads(dims, parts, refs, pos, name, dst, row0, col0, sem):
    x, y, c = pos
    by_x = []

    def start(src, row, quarter, col):
        rows = pl.ds(pl.multiple_of(row0 + row + dims.piece * quarter, 16), dims.piece)
        pltpu.make_async_copy(src, dst.at[rows, pl.ds(col0 + col, dims.block)], sem).start()

    for b, row, col in dims.places[name]:
        z, xq, j = dims.where(b)
        number = find_part(parts, z, j)
        if parts[number].order == "xy":
            by_x.append((number, z, xq, j, row, col))
            continue
        for dc in range(2):
            for dy in range(2):
                src = refs[number][2 * dc + dy].at[parts[number].index(0, x ^ xq, z, j)]
                start(src, row, 2 * (y ^ dy) + (c ^ dc), col)
    if by_x:
        for own_x in range(2):

            @pl.when(x == own_x)
            def _(own_x=own_x):
                for number, z, xq, j, row, col in by_x:
                    for dc in range(2):
                        for yq in range(2):
                            src = refs[number][2 * dc + (own_x ^ xq)].at[parts[number].index(0, y ^ yq, z, j)]
                            start(src, row, 2 * yq + (c ^ dc), col)


def wait_for(ref, sem):
    pltpu.make_async_copy(ref, ref, sem).wait()


def start_stores(dims, parts, outs, pos, places, src, sem):
    x, y, c = pos
    for b, row, col in places:
        z, xq, j = dims.where(b)
        number = find_part(parts, z, j)
        for dc in range(2):
            for yq in range(2):
                ends = (x ^ xq, y ^ yq) if parts[number].order == "xy" else (y ^ yq, x ^ xq)
                rows = pl.ds(pl.multiple_of(row + dims.piece * (2 * yq + (c ^ dc)), 16), dims.piece)
                dst = outs[number][dc].at[parts[number].index(*ends, z, j)]
                pltpu.make_async_copy(src.at[rows, pl.ds(col, dims.block)], dst, sem).start()


def norm_forward(values):
    center = values - jnp.mean(values, axis=-1, keepdims=True)
    spread = jnp.mean(center * center, axis=-1, keepdims=True)
    inverse = lax.rsqrt(spread + norm_epsilon)
    return center * inverse, inverse


def norm_backward(gradient, unit, inverse, gain):
    scaled = gradient * gain
    inner = (
        scaled
        - jnp.mean(scaled, axis=-1, keepdims=True)
        - unit * jnp.mean(scaled * unit, axis=-1, keepdims=True)
    )
    return inverse * inner


def col_sum(values):
    return jnp.sum(values.astype(F32), axis=0, keepdims=True)


def put_rows(sums_ref, number, values):
    count = values.shape[1] // 128
    for n in range(count):
        at = number * count + n
        sums_ref[at : at + 1, :] = values[:, 128 * n : 128 * (n + 1)]


def segment(small_ref, number, width):
    return small_ref[0:1, number * width : (number + 1) * width]


def unflatten(refs, parts):
    return [refs[4 * n : 4 * n + 4] for n in range(len(parts))], refs[4 * len(parts) :]


def weight_ins(parts):
    return [(a, ANY) for p in parts for a in p.arrays]


def half_masks(head):
    lane = lax.broadcasted_iota(jnp.int32, (1, 2 * head), 1)
    low = lane < head
    ones = jnp.where(low, 1.0, 0.0).astype(F32)
    return low, (ones.astype(BF), (1.0 - ones).astype(BF))


def attention_forward_kernel(dims, parts, chains, pos_ref, len_ref, x_ref, small_ref, *rest):
    refs, rest = unflatten(rest, parts)
    qkv_ref, lse_ref, ctx_ref, unit_ref, inv_ref, w, sems = rest
    width, seq = dims.model, dims.rows // chains
    head = width // HEADS
    pos = (pos_ref[1], pos_ref[2], pos_ref[3])
    for n, name in enumerate(("q", "k", "v", "o")):
        start_loads(dims, parts, refs, pos, name, w, 0, n * width, sems.at[n])
    xb = x_ref[...].astype(BF)
    for n, bias in ((0, 0), (1, None), (2, 1)):
        cols = slice(n * width, (n + 1) * width)
        wait_for(w.at[:, cols], sems.at[n])
        out = mm(xb, w[:, cols])
        if bias is not None:
            out = out + segment(small_ref, bias, width)
        qkv_ref[:, cols] = out.astype(BF)
    low, masks = half_masks(head)
    scale = head**-0.5

    def chain(i, carry):
        rows = pl.ds(pl.multiple_of(i * seq, 16), seq)
        valid = lax.broadcasted_iota(jnp.int32, (seq, seq), 0) < len_ref[i]
        for pair in range(HEADS // 2):
            at = pair * 2 * head
            q = qkv_ref[rows, at : at + 2 * head]
            k = qkv_ref[rows, width + at : width + at + 2 * head]
            v = qkv_ref[rows, 2 * width + at : 2 * width + at + 2 * head]
            outs = []
            for h in range(2):
                s = jnp.where(valid, mm_bt(k, q * masks[h]) * scale, -1000000000.0)
                top = jnp.max(s, axis=0, keepdims=True)
                e = jnp.exp(s - top)
                total = jnp.sum(e, axis=0, keepdims=True)
                lse_ref[i, 2 * pair + h : 2 * pair + h + 1, :] = top + jnp.log(total)
                outs.append(mm_at((e * (1.0 / total)).astype(BF), v))
            ctx_ref[rows, at : at + 2 * head] = jnp.where(low, outs[0], outs[1]).astype(BF)
        return carry

    lax.fori_loop(0, chains, chain, 0)
    wait_for(w.at[:, 3 * width :], sems.at[3])
    attended = mm(ctx_ref[...], w[:, 3 * width :]) + segment(small_ref, 2, width)
    unit, inverse = norm_forward(x_ref[...].astype(F32) + attended)
    unit_ref[...] = unit
    inv_ref[...] = inverse


def attention_forward(dims, parts, pos, lengths, x, small, deps=()):
    parts = needed_parts(dims, parts, ("q", "k", "v", "o"))
    chains = lengths.shape[0]
    rows, width = dims.rows, dims.model
    return launch(
        functools.partial(attention_forward_kernel, dims, parts, chains),
        "attention_forward",
        [(pos, SMEM), (lengths, SMEM), (x, VMEM), (small, VMEM)] + weight_ins(parts),
        [
            shape((rows, 3 * width), BF),
            shape((chains, HEADS, rows // chains), F32),
            shape((rows, width), BF),
            shape((rows, width), F32),
            shape((rows, 1), F32),
        ],
        [VMEM] * 5,
        deps,
        [pltpu.VMEM((width, 4 * width), BF), pltpu.SemaphoreType.DMA((4,))],
        (12 * rows * width * width, 16 << 20, 1 << 20),
        limit=56,
    )


def ffn_forward_body(dims, small_ref, unit_ref, up, down, sems, act_ref, slope_ref):
    width = dims.model
    h1 = unit_ref[...] * segment(small_ref, 4, width) + segment(small_ref, 5, width)
    hb = h1.astype(BF)
    total = h1 + segment(small_ref, 3, width)
    wait_for(up, sems.at[0])
    for n in range(dims.ffn // width):
        cols = slice(n * width, (n + 1) * width)
        u = mm(hb, up[:, cols]) + segment(small_ref, 8 + n, width)
        cdf = 0.5 * (1.0 + lax.erf(u * 0.7071067811865476))
        act = (u * cdf).astype(BF)
        act_ref[:, cols] = act
        slope_ref[:, cols] = (cdf + u * (0.3989422804014327 * jnp.exp(-0.5 * u * u))).astype(BF)
        if n == 0:
            wait_for(down, sems.at[1])
        total = total + mm(act, down[cols, :])
    return total


def ffn_forward_kernel(dims, parts, pos_ref, unit_ref, small_ref, *rest):
    refs, rest = unflatten(rest, parts)
    act_ref, slope_ref, unit2_ref, inv2_ref, y_ref, up, down, sems = rest
    pos = (pos_ref[1], pos_ref[2], pos_ref[3])
    start_loads(dims, parts, refs, pos, "up", up, 0, 0, sems.at[0])
    start_loads(dims, parts, refs, pos, "down", down, 0, 0, sems.at[1])
    width = dims.model
    total = ffn_forward_body(dims, small_ref, unit_ref, up, down, sems, act_ref, slope_ref)
    unit, inverse = norm_forward(total)
    unit2_ref[...] = unit
    inv2_ref[...] = inverse
    y_ref[...] = unit * segment(small_ref, 6, width) + segment(small_ref, 7, width)


def ffn_forward(dims, parts, pos, unit, small, deps=()):
    parts = needed_parts(dims, parts, ("up", "down"))
    rows, width, ffn = dims.rows, dims.model, dims.ffn
    return launch(
        functools.partial(ffn_forward_kernel, dims, parts),
        "ffn_forward",
        [(pos, SMEM), (unit, VMEM), (small, VMEM)] + weight_ins(parts),
        [
            shape((rows, ffn), BF),
            shape((rows, ffn), BF),
            shape((rows, width), F32),
            shape((rows, 1), F32),
            shape((rows, width), F32),
        ],
        [VMEM] * 5,
        deps,
        [pltpu.VMEM((width, ffn), BF), pltpu.VMEM((ffn, width), BF), pltpu.SemaphoreType.DMA((2,))],
        (4 * rows * width * ffn, 24 << 20, 3 << 20),
        limit=56,
    )


def ffn_backward_body(
    dims, outs_parts, outs, pos, gy, small_ref, unit_ref, inv_ref, ctx_ref, unit2, inv2, act_ref, slope_ref,
    up, down, wo, grad_up, grad_down, grad_o, sem_out, gz1_ref, gctx_ref, sums_ref, wait_o,
):
    width = dims.model
    gain1, gain2 = segment(small_ref, 4, width), segment(small_ref, 6, width)

    def put(number, values):
        put_rows(sums_ref, number, values)

    put(6, col_sum(gy * unit2))
    put(7, col_sum(gy))
    gz2 = norm_backward(gy, unit2, inv2, gain2)
    gf = gz2.astype(BF)
    put(3, col_sum(gf))
    hb = (unit_ref[...] * gain1 + segment(small_ref, 5, width)).astype(BF)
    gh1 = gz2
    block = dims.block
    for n in range(dims.ffn // width):
        cols = slice(n * width, (n + 1) * width)
        gu = (slope_ref[:, cols].astype(F32) * mm_bt(gf, down[cols, :])).astype(BF)
        put(8 + n, col_sum(gu))
        grad_up[:, cols] = mm_at(hb, gu).astype(BF)
        grad_down[cols, :] = mm_at(act_ref[:, cols], gf).astype(BF)
        low, high = n * width, (n + 1) * width
        start_stores(
            dims, outs_parts, outs, pos,
            [p for p in dims.places["up"] if low <= p[2] < high], grad_up, sem_out.at[0],
        )
        start_stores(
            dims, outs_parts, outs, pos,
            [p for p in dims.places["down"] if low <= p[1] < high], grad_down, sem_out.at[1],
        )
        gh1 = gh1 + mm_bt(gu, up[:, cols])
    unit = unit_ref[...]
    put(4, col_sum(gh1 * unit))
    put(5, col_sum(gh1))
    gz1 = norm_backward(gh1, unit, inv_ref[...], gain1)
    gz1_ref[...] = gz1
    ga = gz1.astype(BF)
    put(2, col_sum(ga))
    grad_o[...] = mm_at(ctx_ref[...], ga).astype(BF)
    start_stores(dims, outs_parts, outs, pos, dims.places["o"], grad_o, sem_out.at[2])
    wait_o()
    gctx_ref[...] = mm_bt(ga, wo[...]).astype(BF)
    put(0, jnp.zeros((1, width), F32))
    put(1, jnp.zeros((1, width), F32))
    wait_for(grad_up, sem_out.at[0])
    wait_for(grad_down, sem_out.at[1])
    wait_for(grad_o, sem_out.at[2])


def grad_shapes(dims, parts):
    return [shape((p.count(), dims.piece, dims.block), BF) for p in parts for _ in range(2)]


def pair_up(arrays, parts):
    return [Part(p.zs, p.js, p.order, list(arrays[2 * n : 2 * n + 2])) for n, p in enumerate(parts)]


def ffn_scratch(dims):
    width, ffn = dims.model, dims.ffn
    matrices = [(width, ffn), (ffn, width), (width, width)] * 2
    return [pltpu.VMEM(m, BF) for m in matrices] + [pltpu.SemaphoreType.DMA((3,))] * 2


def ffn_backward_kernel(dims, parts, outs_parts, pos_ref, gy_ref, small_ref, unit_ref, inv_ref, ctx_ref, unit2_ref, inv2_ref, act_ref, slope_ref, *rest):
    refs, rest = unflatten(rest, parts)
    gz1_ref, gctx_ref, sums_ref, *rest = rest
    count = 2 * len(outs_parts)
    outs = [rest[2 * n : 2 * n + 2] for n in range(len(outs_parts))]
    up, down, wo, grad_up, grad_down, grad_o, sems, sem_out = rest[count:]
    pos = (pos_ref[1], pos_ref[2], pos_ref[3])
    start_loads(dims, parts, refs, pos, "down", down, 0, 0, sems.at[1])
    start_loads(dims, parts, refs, pos, "up", up, 0, 0, sems.at[0])
    start_loads(dims, parts, refs, pos, "o", wo, 0, 0, sems.at[2])
    wait_for(down, sems.at[1])
    wait_for(up, sems.at[0])
    ffn_backward_body(
        dims, outs_parts, outs, pos, gy_ref[...], small_ref, unit_ref, inv_ref, ctx_ref,
        unit2_ref[...], inv2_ref[...], act_ref, slope_ref, up, down, wo, grad_up, grad_down, grad_o,
        sem_out, gz1_ref, gctx_ref, sums_ref, lambda: wait_for(wo, sems.at[2]),
    )


def ffn_backward(dims, parts, outs_parts, pos, gy, small, unit, inv, ctx, unit2, inv2, act, slope, deps=()):
    parts = needed_parts(dims, parts, ("up", "down", "o"))
    rows, width, ffn = dims.rows, dims.model, dims.ffn
    grads = grad_shapes(dims, outs_parts)
    out = launch(
        functools.partial(ffn_backward_kernel, dims, parts, outs_parts),
        "ffn_backward",
        [(pos, SMEM)]
        + [(a, VMEM) for a in (gy, small, unit, inv, ctx, unit2, inv2, act, slope)]
        + weight_ins(parts),
        [shape((rows, width), F32), shape((rows, width), BF), shape((small.shape[1] // 128, 128), F32)] + grads,
        [VMEM] * 3 + [ANY] * len(grads),
        deps,
        ffn_scratch(dims),
        (8 * rows * width * ffn + 4 * rows * width * width, 40 << 20, 0),
        limit=56,
    )
    return out[0], out[1], out[2], pair_up(out[3:], outs_parts)


def ffn_both_kernel(dims, parts, outs_parts, chains, pos_ref, len_ref, cot_ref, small_ref, unit_ref, inv_ref, ctx_ref, *rest):
    refs, rest = unflatten(rest, parts)
    y_ref, gz1_ref, gctx_ref, sums_ref, *rest = rest
    count = 2 * len(outs_parts)
    outs = [rest[2 * n : 2 * n + 2] for n in range(len(outs_parts))]
    up, down, wo, grad_up, grad_down, grad_o, sems, sem_out, act_ref, slope_ref = rest[count:]
    pos = (pos_ref[1], pos_ref[2], pos_ref[3])
    start_loads(dims, parts, refs, pos, "up", up, 0, 0, sems.at[0])
    start_loads(dims, parts, refs, pos, "down", down, 0, 0, sems.at[1])
    start_loads(dims, parts, refs, pos, "o", wo, 0, 0, sems.at[2])
    width, seq = dims.model, dims.rows // chains
    total = ffn_forward_body(dims, small_ref, unit_ref, up, down, sems, act_ref, slope_ref)
    unit2, inv2 = norm_forward(total)
    y_ref[...] = (unit2 * segment(small_ref, 6, width) + segment(small_ref, 7, width)).astype(BF)
    place = lax.broadcasted_iota(jnp.int32, (seq, width), 0)
    gy = jnp.concatenate(
        [
            jnp.where(place < len_ref[i], cot_ref[i * seq : (i + 1) * seq, :].astype(F32), 0.0)
            for i in range(chains)
        ],
        axis=0,
    )
    ffn_backward_body(
        dims, outs_parts, outs, pos, gy, small_ref, unit_ref, inv_ref, ctx_ref,
        unit2, inv2, act_ref, slope_ref, up, down, wo, grad_up, grad_down, grad_o,
        sem_out, gz1_ref, gctx_ref, sums_ref, lambda: wait_for(wo, sems.at[2]),
    )


def ffn_both(dims, parts, outs_parts, pos, lengths, cot, small, unit, inv, ctx, deps=()):
    parts = needed_parts(dims, parts, ("up", "down", "o"))
    rows, width, ffn = dims.rows, dims.model, dims.ffn
    grads = grad_shapes(dims, outs_parts)
    out = launch(
        functools.partial(ffn_both_kernel, dims, parts, outs_parts, lengths.shape[0]),
        "ffn_both",
        [(pos, SMEM), (lengths, SMEM)]
        + [(a, VMEM) for a in (cot, small, unit, inv, ctx)]
        + weight_ins(parts),
        [
            shape((rows, width), BF),
            shape((rows, width), F32),
            shape((rows, width), BF),
            shape((small.shape[1] // 128, 128), F32),
        ]
        + grads,
        [VMEM] * 4 + [ANY] * len(grads),
        deps,
        ffn_scratch(dims) + [pltpu.VMEM((rows, ffn), BF)] * 2,
        (12 * rows * width * ffn + 4 * rows * width * width, 40 << 20, 3 << 20),
        limit=56,
    )
    return out[0], out[1], out[2], out[3], pair_up(out[4:], outs_parts)


def attention_backward_kernel(dims, parts, outs_parts, chains, given, pos_ref, len_ref, gz1_ref, gctx_ref, qkv_ref, lse_ref, x_ref, *rest):
    given_refs, rest = rest[:given], rest[given:]
    refs, rest = unflatten(rest, parts)
    gx_ref, sums_ref, *rest = rest
    count = 2 * len(outs_parts)
    outs = [rest[2 * n : 2 * n + 2] for n in range(len(outs_parts))]
    w, grads_ref, grad_w, sems, sem_out = rest[count:]
    pos = (pos_ref[1], pos_ref[2], pos_ref[3])
    width, seq = dims.model, dims.rows // chains
    head = width // HEADS
    names = ("q", "k", "v")
    for n, name in enumerate(names):
        start_loads(dims, parts, refs, pos, name, w, 0, n * width, sems.at[n])
    low, masks = half_masks(head)
    scale = head**-0.5

    def chain(i, carry):
        rows = pl.ds(pl.multiple_of(i * seq, 16), seq)
        valid = lax.broadcasted_iota(jnp.int32, (seq, seq), 0) < len_ref[i]
        for pair in range(HEADS // 2):
            at = pair * 2 * head
            q = qkv_ref[rows, at : at + 2 * head]
            k = qkv_ref[rows, width + at : width + at + 2 * head]
            v = qkv_ref[rows, 2 * width + at : 2 * width + at + 2 * head]
            g = gctx_ref[rows, at : at + 2 * head]
            gq, gk, gv = [], [], []
            for h in range(2):
                s = jnp.where(valid, mm_bt(k, q * masks[h]) * scale, -1000000000.0)
                p = jnp.exp(s - lse_ref[i, 2 * pair + h : 2 * pair + h + 1, :])
                gp = mm_bt(v, g * masks[h])
                inner = jnp.sum(p * gp, axis=0, keepdims=True)
                gs = (p * (gp - inner)).astype(BF)
                gv.append(mm(p.astype(BF), g))
                gk.append(mm(gs, q))
                gq.append(mm_at(gs, k))
            grads_ref[rows, at : at + 2 * head] = (jnp.where(low, gq[0], gq[1]) * scale).astype(BF)
            grads_ref[rows, width + at : width + at + 2 * head] = (
                jnp.where(low, gk[0], gk[1]) * scale
            ).astype(BF)
            grads_ref[rows, 2 * width + at : 2 * width + at + 2 * head] = jnp.where(
                low, gv[0], gv[1]
            ).astype(BF)
        return carry

    lax.fori_loop(0, chains, chain, 0)
    xb = x_ref[...].astype(BF)
    for n, name in enumerate(names):
        cols = slice(n * width, (n + 1) * width)
        grad_w[:, cols] = mm_at(xb, grads_ref[:, cols]).astype(BF)
        places = [(b, r, c + n * width) for b, r, c in dims.places[name]]
        start_stores(dims, outs_parts, outs, pos, places, grad_w, sem_out)
    at = 0
    for ref in given_refs:
        sums_ref[at : at + ref.shape[0], :] = ref[...]
        at += ref.shape[0]
    put_rows(sums_ref, 0, col_sum(grads_ref[:, :width]))
    put_rows(sums_ref, 1, col_sum(grads_ref[:, 2 * width :]))
    gx = gz1_ref[...]
    for n in range(3):
        cols = slice(n * width, (n + 1) * width)
        wait_for(w.at[:, cols], sems.at[n])
        gx = gx + mm_bt(grads_ref[:, cols], w[:, cols])
    gx_ref[...] = gx
    wait_for(grad_w, sem_out)


def attention_backward(dims, parts, outs_parts, pos, lengths, gz1, gctx, qkv, lse, x, sums, deps=()):
    parts = needed_parts(dims, parts, ("q", "k", "v"))
    rows, width = dims.rows, dims.model
    grads = grad_shapes(dims, outs_parts)
    out = launch(
        functools.partial(attention_backward_kernel, dims, parts, outs_parts, lengths.shape[0], len(sums)),
        "attention_backward",
        [(pos, SMEM), (lengths, SMEM)] + [(a, VMEM) for a in (gz1, gctx, qkv, lse, x, *sums)] + weight_ins(parts),
        [shape((rows, width), F32), shape((sum(a.shape[0] for a in sums), 128), F32)] + grads,
        [VMEM] * 2 + [ANY] * len(grads),
        deps,
        [
            pltpu.VMEM((width, 3 * width), BF),
            pltpu.VMEM((rows, 3 * width), BF),
            pltpu.VMEM((width, 3 * width), BF),
            pltpu.SemaphoreType.DMA((3,)),
            pltpu.SemaphoreType.DMA,
        ],
        (24 * rows * width * width, 24 << 20, 1 << 20),
        limit=56,
    )
    return out[0], out[1], pair_up(out[2:], outs_parts)


class AnySlice:
    def __init__(self, dims):
        self.dims = dims
        own = range(dims.own)
        self.early = [Part((1, 2, 3), own, "yx")]
        self.late = [Part((0,), own, "yx")]

    def position(self):
        return jnp.zeros((4,), jnp.int32)

    def gather(self, low):
        dims = self.dims
        whole = lax.all_gather(low, "fsdp", axis=1, tiled=True)
        whole = lax.all_gather(whole, "grp", axis=0, tiled=True)
        split = whole.reshape(Z_SLABS, 2, dims.own, 2, 2, dims.piece, dims.block)
        order = split.transpose(4, 3, 1, 0, 2, 5, 6).reshape(4, -1, dims.piece, dims.block)
        return [Part(range(Z_SLABS), range(dims.own), "yx", [order[n] for n in range(4)])]

    def reduce(self, early, late):
        dims = self.dims
        pieces = []
        for part in (late[0], early[0]):
            stacked = jnp.stack(part.arrays)
            split = stacked.reshape(2, 2, 2, len(part.zs), dims.own, dims.piece, dims.block)
            pieces.append(split.transpose(3, 2, 4, 1, 0, 5, 6))
        whole = jnp.concatenate(pieces, axis=0).reshape(dims.blocks, dims.block, dims.block)
        rows = lax.psum_scatter(whole, "fsdp", scatter_dimension=1, tiled=True)
        return lax.psum_scatter(rows, "grp", scatter_dimension=0, tiled=True).astype(F32)

    def small_sum(self, values):
        return lax.psum(values, ("grp", "fsdp"))

    def group(self, owned):
        return lax.all_gather(owned, "fsdp", axis=1, tiled=True)


def swap_of(axis):
    def move(z, x, y, c):
        return (z, x ^ (axis == "x"), y ^ (axis == "y"), c ^ (axis == "c"))

    return move


def join_kernel(ranges, *refs):
    pairs = len(ranges)
    ins, outs, holds, sems = refs[: 2 * pairs], refs[2 * pairs : 3 * pairs], refs[3 * pairs : -2], refs[-2:]
    for n, (low, count) in enumerate(ranges):
        for half in range(2):
            src = ins[2 * n + half].at[pl.ds(low, count)]
            dst = holds[n].at[pl.ds(half * count, count)]
            pltpu.make_async_copy(src, dst, sems[0].at[n]).start()
    for n in range(pairs):
        wait_for(holds[n], sems[0].at[n])
        pltpu.make_async_copy(holds[n], outs[n], sems[1].at[n]).start()
    for n in range(pairs):
        wait_for(holds[n], sems[1].at[n])


def stack_kernel(zs, halves, pos_ref, *refs):
    ins, outs, holds, sems = refs[:Z_SLABS], refs[Z_SLABS:-4], refs[-4:-2], refs[-2:]
    z = pos_ref[0]
    for n, (low, high) in enumerate(halves):
        for place, want in enumerate(zs):
            for k in range(Z_SLABS):

                @pl.when(lax.rem(z - want + Z_SLABS, Z_SLABS) == k)
                def _(n=n, low=low, high=high, place=place, k=k):
                    dst = holds[n].at[pl.ds(place * (high - low), high - low)]
                    pltpu.make_async_copy(ins[k].at[pl.ds(low, high - low)], dst, sems[0].at[n]).start()

    for n in range(2):
        wait_for(holds[n], sems[0].at[n])
        pltpu.make_async_copy(holds[n], outs[n], sems[1].at[n]).start()
    for n in range(2):
        wait_for(holds[n], sems[1].at[n])


def round_kernel(src_ref, dst_ref):
    dst_ref[...] = src_ref[...].astype(BF)


def add_kernel(a_ref, b_ref, first_ref, second_ref):
    half = first_ref.shape[0]

    def piece(i, carry):
        for out, at in ((first_ref, i), (second_ref, i + half)):
            out[i] = (a_ref[at].astype(F32) + b_ref[at].astype(F32)).astype(BF)
        return carry

    lax.fori_loop(0, half, piece, 0)


def collect_kernel(zs, *refs):
    ins, out = refs[:-1], refs[-1]
    base = min(min(z_list) for z_list in zs)
    half = ins[0].shape[0] // len(zs[0])
    for n, z_list in enumerate(zs):
        for place, want in enumerate(z_list):
            piece = pl.ds(place * half, half)
            total = ins[2 * n][piece].astype(F32) + ins[2 * n + 1][piece].astype(F32)
            out[pl.ds((2 * (want - base) + n % 2) * half, half)] = total.astype(BF)


def pick_kernel(places, src_ref, *refs):
    outs, holds, sems = refs[: len(places)], refs[len(places) : -2], refs[-2:]
    for n, runs in enumerate(places):
        at = 0
        for low, count in runs:
            dst = holds[n].at[pl.ds(at, count)]
            pltpu.make_async_copy(src_ref.at[pl.ds(low, count)], dst, sems[0].at[n]).start()
            at += count
    for n in range(len(places)):
        wait_for(holds[n], sems[0].at[n])
        pltpu.make_async_copy(holds[n], outs[n], sems[1].at[n]).start()
    for n in range(len(places)):
        wait_for(holds[n], sems[1].at[n])


def pass_kernel(*refs):
    pass


def total_kernel(own_ref, *refs):
    *got, wide_ref, low_ref = refs
    total = own_ref[...].astype(F32)
    for ref in got:
        total = total + ref[...].astype(F32)
    wide_ref[...] = total
    low_ref[...] = total.astype(BF)


class SmallSlice:
    def __init__(self, dims):
        self.dims = dims
        a, b = range(dims.own // 2), range(dims.own // 2, dims.own)
        self.early = [Part((1, 2, 3), a, "yx"), Part((1, 2, 3), b, "xy")]
        self.late = [Part((0,), a, "yx"), Part((0,), b, "xy")]
        group, shard = lax.axis_index("grp"), lax.axis_index("fsdp")
        self.z, self.x, self.y, self.c = group // 2, group % 2, shard // 2, shard % 2
        self.pos = jnp.stack([self.z, self.x, self.y, self.c]).astype(jnp.int32)

    def position(self):
        return self.pos

    def pieces(self, count):
        return shape((count, self.dims.piece, self.dims.block), BF)

    def permute(self, array, move):
        pairs = []
        for flat in range(8 * Z_SLABS):
            to = move(flat // 8, flat // 4 % 2, flat // 2 % 2, flat % 2)
            if to is not None:
                pairs.append((flat, ((to[0] * 2 + to[1]) * 2 + to[2]) * 2 + to[3]))
        return lax.ppermute(array, ("grp", "fsdp"), pairs)

    def swap(self, array, axis):
        return self.permute(array, swap_of(axis))

    def rounded(self, wide, deps=()):
        return launch(round_kernel, "rounded", [(wide, VMEM)], shape(wide.shape, BF), VMEM, deps)

    def from_slabs(self, own):
        return [own] + [
            self.permute(own, lambda z, x, y, c, k=k: ((z + k) % Z_SLABS, x, y, c)) for k in range(1, Z_SLABS)
        ]

    def lot(self, slabs, zs, js, deps=()):
        half = len(js) // 2
        halves = [(0, half), (half, len(js))]
        sizes = [self.pieces(len(zs) * (high - low)) for low, high in halves]
        arrays = launch(
            functools.partial(stack_kernel, zs, halves),
            "stack",
            [(self.pos, SMEM)] + [(a, ANY) for a in slabs],
            sizes,
            [ANY] * 2,
            deps,
            [pltpu.VMEM(s.shape, BF) for s in sizes] + [pltpu.SemaphoreType.DMA((2,))] * 2,
        )
        return [(Part(zs, js[low:high], order), a) for (low, high), order, a in zip(halves, ("yx", "xy"), arrays)]

    def columns(self):
        return [[2 * z + x for z in range(Z_SLABS)] for x in range(2)]

    def whole_column(self, own):
        return lax.all_gather(own, "grp", axis_index_groups=self.columns(), axis=0, tiled=True)

    def whole_lot(self, whole, zs, js, deps=()):
        half, count = len(js) // 2, self.dims.own
        places = [[(z * count + js[low], half) for z in zs] for low in (0, half)]
        sizes = [self.pieces(len(zs) * half)] * 2
        arrays = launch(
            functools.partial(pick_kernel, places),
            "pick",
            [(whole, ANY)],
            sizes,
            [ANY] * 2,
            deps,
            [pltpu.VMEM(s.shape, BF) for s in sizes] + [pltpu.SemaphoreType.DMA((2,))] * 2,
        )
        halves = ((js[:half], "yx"), (js[half:], "xy"))
        return [(Part(zs, j, order), a) for (j, order), a in zip(halves, arrays)]

    def gate(self, arrays, deps):
        return launch(
            pass_kernel,
            "gate",
            [(a, ANY) for a in arrays],
            [shape(a.shape, a.dtype) for a in arrays],
            [ANY] * len(arrays),
            deps,
            aliases={n: n for n in range(len(arrays))},
        )

    def hold(self, parts, deps):
        for part, array in zip(parts, self.gate([p.arrays[1] for p in parts], deps)):
            part.arrays[1] = array

    def first_swap(self, lot):
        return [self.swap(a, part.order[1]) for part, a in lot]

    def joined(self, lot, got, zs, deps=()):
        ins, ranges, sizes = [], [], []
        for (part, own), g in zip(lot, got):
            count = len(part.js)
            ranges.append((part.zs.index(zs[0]) * count, len(zs) * count))
            sizes.append(self.pieces(2 * len(zs) * count))
            ins += [own, g]
        return launch(
            functools.partial(join_kernel, ranges),
            "join",
            [(a, ANY) for a in ins],
            sizes,
            [ANY] * len(lot),
            deps,
            [pltpu.VMEM(s.shape, BF) for s in sizes] + [pltpu.SemaphoreType.DMA((2,))] * 2,
        )

    def second_swap(self, lot, both):
        return [self.swap(b, part.order[0]) for (part, _), b in zip(lot, both)]

    def core_swap(self, lot, zs, both, got):
        return [
            Part(zs, part.js, part.order, [b, g, self.swap(b, "c"), self.swap(g, "c")])
            for (part, _), b, g in zip(lot, both, got)
        ]

    def add(self, keep, got, deps=()):
        sums = []
        for own, other in zip(keep, got):
            out = [self.pieces(own.shape[0] // 2)] * 2
            sums.append(launch(add_kernel, "add", [(own, VMEM), (other, VMEM)], out, [VMEM] * 2, deps))
        return [kept for kept, _ in sums], [sent for _, sent in sums]

    def core_sum(self, parts, deps=()):
        got = [self.swap(p.arrays[1], "c") for p in parts]
        return self.add([p.arrays[0] for p in parts], got, deps)

    def swaps(self, sums, axes):
        return [self.swap(a, axis) for a, axis in zip(sums[1], axes)]

    def collect(self, zs, sums, got, deps=()):
        ins = []
        for (kept, _), others in zip(sums, got):
            for own, other in zip(kept, others):
                ins += [own, other]
        return launch(
            functools.partial(collect_kernel, [z for z in zs for _ in range(2)]),
            "collect",
            [(a, VMEM) for a in ins],
            self.pieces(sum(len(z) for z in zs) * self.dims.own),
            VMEM,
            deps,
        )

    def deal(self, whole):
        split = whole.reshape((Z_SLABS, self.dims.own) + whole.shape[1:])
        got = []
        for k in range(Z_SLABS):
            mine = lax.dynamic_index_in_dim(split, (self.z + k) % Z_SLABS, 0, keepdims=False)
            if k > 0:
                mine = self.permute(mine, lambda z, x, y, c, k=k: ((z + k) % Z_SLABS, x, y, c))
            got.append(mine)
        return got

    def slab_sum(self, dealt, deps=()):
        size = dealt[0].shape
        return launch(
            total_kernel,
            "total",
            [(a, VMEM) for a in dealt],
            [shape(size, F32), shape(size, BF)],
            [VMEM] * 2,
            deps,
        )

    def column_sum(self, whole):
        return lax.psum_scatter(
            whole, "grp", axis_index_groups=self.columns(), scatter_dimension=0, tiled=True
        )

    def whole_group(self, own):
        return [lax.all_gather(own, "fsdp", axis=0, tiled=True)]

    def small_sum_column(self, values):
        for bit in (1, 2):
            values = values + self.permute(values, lambda z, x, y, c, bit=bit: (z ^ bit, x, y, c))
        return values

    def small_sum_plane(self, values):
        for axis in ("c", "x", "y"):
            values = values + self.swap(values, axis)
        return values

    def group(self, own):
        other = self.swap(own, "y")
        return [own, other, self.swap(own, "c"), self.swap(other, "c")]


def update_kernel(layer, first, count_grads, pos_ref, own_ref, *rest):
    stats, grads, rest = rest[:4], rest[4 : 4 + count_grads], rest[4 + count_grads :]
    roots, rest = rest[:4], rest[4:]
    if not first:
        rest = rest[5:]
    outs, rest = rest[:5], rest[5:]
    g_ref, r_ref, gram_ref, own, held, fresh, low_ref, sem_g, sem_r, sem_in, sem_out = rest
    y, c = pos_ref[2], pos_ref[3]
    count, piece, block = own_ref.shape

    def quarter(yq, cq):
        return pl.ds(pl.multiple_of(piece * (2 * yq + cq), 16), piece)

    for n in range(count_grads):
        rows = quarter(y ^ (n % 2), c ^ (n // 2)) if count_grads == 4 else pl.ds(0, block)
        if count_grads == 4:
            pltpu.make_async_copy(grads[n], g_ref.at[:, rows, :], sem_g).start()
    if count_grads == 1:
        for n in range(4):
            mine = grads[0].at[pl.ds(n * count, count)]
            pltpu.make_async_copy(mine, g_ref.at[:, pl.ds(n * piece, piece), :], sem_g).start()
    for n in range(4):
        mine = roots[n].at[pl.ds(layer * count, count)]
        pltpu.make_async_copy(mine, r_ref.at[:, quarter(y ^ (n % 2), c ^ (n // 2)), :], sem_r).start()
    for n in range(4):
        pltpu.make_async_copy(stats[n].at[layer], held.at[n], sem_in.at[n]).start()
    pltpu.make_async_copy(own_ref, own, sem_in.at[4]).start()
    own_rows = quarter(y, c)
    wait_for(g_ref, sem_g)
    for b in range(count):
        g = g_ref[b]
        if b == 0:
            wait_for(held.at[0], sem_in.at[0])
        fresh[1, b] = decay_rate * held[0, b] + (1.0 - decay_rate) * mm_bt(g_ref[b, own_rows, :], g)
        gram_ref[...] = mm_at(g, g)
        if b == 0:
            wait_for(held.at[1], sem_in.at[1])
        fresh[2, b] = decay_rate * held[1, b] + (1.0 - decay_rate) * gram_ref[own_rows, :]
        if b == 0:
            wait_for(r_ref, sem_r)
        mixed = mm(g, r_ref[b])
        if b == 0:
            wait_for(held.at[2], sem_in.at[2])
        update = jnp.dot(held[2, b], mixed, preferred_element_type=F32, precision=lax.Precision.HIGHEST)
        if b == 0:
            wait_for(held.at[3], sem_in.at[3])
            wait_for(own, sem_in.at[4])
        master = held[3, b] - matrix_rate * update
        fresh[3, b] = master
        low_ref[b] = master.astype(BF)
        fresh[0, b] = own[b].astype(F32)
        for n in range(4):
            pltpu.make_async_copy(fresh.at[n, b], outs[n].at[layer, b], sem_out.at[0]).start()
        pltpu.make_async_copy(low_ref.at[b], outs[4].at[layer, b], sem_out.at[1]).start()
    wait_for(fresh, sem_out.at[0])
    wait_for(low_ref, sem_out.at[1])


def update_layer(layer, pos, own, left, right, left_roots, masters, grads, roots, before, deps=()):
    count, piece, block = own.shape
    whole = (LAYERS, count, piece, block)
    ins = [(pos, SMEM), (own, ANY)] + [(a, ANY) for a in (left, right, left_roots, masters)]
    ins += [(a, ANY) for a in grads] + [(a, ANY) for a in roots]
    aliases = {}
    if before is not None:
        aliases = {len(ins) + n: n for n in range(5)}
        ins += [(a, ANY) for a in before]
    return launch(
        functools.partial(update_kernel, layer, before is None, len(grads)),
        "update_layer",
        ins,
        [shape(whole, F32)] * 4 + [shape(whole, BF)],
        [ANY] * 5,
        deps,
        [
            pltpu.VMEM((count, block, block), BF),
            pltpu.VMEM((count, block, block), BF),
            pltpu.VMEM((block, block), F32),
            pltpu.VMEM(own.shape, own.dtype),
            pltpu.VMEM((4,) + own.shape, F32),
            pltpu.VMEM((4,) + own.shape, F32),
            pltpu.VMEM(own.shape, BF),
            pltpu.SemaphoreType.DMA,
            pltpu.SemaphoreType.DMA,
            pltpu.SemaphoreType.DMA((5,)),
            pltpu.SemaphoreType.DMA((2,)),
        ],
        (0, 0, 0),
        aliases,
        limit=56,
    )


def update_plain(net, owned, masters, left_stats, right_stats, left_roots, right_roots):
    own_rows = masters.shape[2]
    first_row = lax.axis_index("fsdp") * own_rows
    highest = lax.Precision.HIGHEST
    grads = jnp.stack(owned)
    whole = jnp.stack([net.group(g.astype(BF)) for g in owned]).astype(F32)
    roots = jnp.stack([net.group(right_roots[n].astype(BF)) for n in range(LAYERS)]).astype(F32)
    columns = lax.dynamic_slice_in_dim(whole, first_row, own_rows, 3)
    new_left = decay_rate * left_stats + (1.0 - decay_rate) * jnp.einsum(
        "lbrk,lbck->lbrc", grads, whole, precision=highest
    )
    new_right = decay_rate * right_stats + (1.0 - decay_rate) * jnp.einsum(
        "lbkr,lbkc->lbrc", columns, whole, precision=highest
    )
    mixed = jnp.einsum("lbrk,lbkc->lbrc", whole, roots, precision=highest)
    update = jnp.einsum("lbrk,lbkc->lbrc", left_roots, mixed, precision=highest)
    new_masters = masters - matrix_rate * update
    return grads, new_left, new_right, new_masters, new_masters.astype(BF)


def update_small_kernel(sums_ref, moments_ref, params_ref, grads_out, moments_out, params_out):
    count = moments_ref.shape[1] // 128
    for layer in range(LAYERS):
        for n in range(count):
            at, cols = layer * count + n, slice(128 * n, 128 * (n + 1))
            grads_out[layer : layer + 1, cols] = sums_ref[at : at + 1, :]
    grads = grads_out[...]
    moments = decay_rate * moments_ref[...] + (1.0 - decay_rate) * grads * grads
    moments_out[...] = moments
    params_out[...] = params_ref[...] - small_rate * grads / (jnp.sqrt(moments) + moment_epsilon)


def update_small(sums, moments, params):
    return launch(
        update_small_kernel,
        "update_small",
        [(a, VMEM) for a in (sums, moments, params)],
        [shape(moments.shape, F32)] * 3,
        [VMEM] * 3,
    )


def run_any(net, dims, small, lengths, x, cot, low):
    pos = net.position()
    weights = [net.gather(low[n]) for n in range(LAYERS)]
    last = LAYERS - 1
    saved = []
    for n in range(LAYERS):
        qkv, lse, ctx, unit, inv = attention_forward(dims, weights[n], pos, lengths, x, small[n])
        saved.append([x, qkv, lse, ctx, unit, inv])
        if n < last:
            *rest, x = ffn_forward(dims, weights[n], pos, unit, small[n])
            saved[n] += rest
    owned = [None] * LAYERS
    for n in reversed(range(LAYERS)):
        x, qkv, lse, ctx, unit, inv, *rest = saved[n]
        if n == last:
            y, gz1, gctx, sums_a, early = ffn_both(
                dims, weights[n], net.early, pos, lengths, cot, small[n], unit, inv, ctx
            )
        else:
            act, slope, unit2, inv2 = rest
            gz1, gctx, sums_a, early = ffn_backward(
                dims, weights[n], net.early, pos, gy, small[n], unit, inv, ctx, unit2, inv2, act, slope
            )
        sums = [sums_a] if n == last else [sums_a, sums]
        gy, sums, late = attention_backward(
            dims, weights[n], net.late, pos, lengths, gz1, gctx, qkv, lse, x, sums
        )
        owned[n] = net.reduce(early, late)
    return y, gy, owned, net.small_sum(sums)


def run_small(net, dims, small, lengths, x, cot, left_stats, right_stats, left_roots, right_roots, masters):
    pos = net.position()
    own, every = tuple(range(dims.own)), tuple(range(Z_SLABS))
    third = dims.own // 3

    low_zs, high_zs = every[: Z_SLABS // 2], every[Z_SLABS // 2 :]
    slabs = net.from_slabs(masters[0].astype(BF))
    low1 = net.rounded(masters[1], slabs[1:])
    whole1 = net.whole_column(low1)
    lot = net.lot(slabs, every, own, [low1])
    got = net.first_swap(lot)
    both = net.joined(lot, got, low_zs)
    both_b = net.joined(lot, got, high_zs, both)
    got = net.second_swap(lot, both)
    weights0 = net.core_swap(lot, low_zs, both, got)
    got = net.second_swap(lot, both_b)
    lot_b = net.whole_lot(whole1, every, own, both_b)
    qkv0, lse0, ctx0, unit0, inv0 = attention_forward(dims, weights0, pos, lengths, x, small[0], both_b)
    weights0 += net.core_swap(lot, high_zs, both_b, net.gate(got, [inv0]))

    lot = lot_b
    got = net.first_swap(lot)
    act0, slope0, unit0b, inv0b, y0 = ffn_forward(
        dims, weights0, pos, unit0, small[0], [a for _, a in lot]
    )
    both = net.joined(lot, got, low_zs, [inv0b])
    both_b = net.joined(lot, got, high_zs, both)
    got = net.second_swap(lot, both)
    weights1 = net.core_swap(lot, low_zs, both, got)
    got = net.second_swap(lot, both_b)
    qkv1, lse1, ctx1, unit1, inv1 = attention_forward(dims, weights1, pos, lengths, y0, small[1], both_b)
    got = net.gate(got, [inv1])
    weights1 += net.core_swap(lot, high_zs, both_b, got)

    roots = net.rounded(right_roots.reshape((-1,) + right_roots.shape[2:]), got)
    y1, gz1, gctx, sums, early1 = ffn_both(
        dims, weights1, net.early, pos, lengths, cot, small[1], unit1, inv1, ctx1, [roots]
    )
    roots_y = net.swap(roots, "y")
    net.hold(early1, [roots_y])
    roots = [roots, roots_y, net.swap(roots, "c"), net.swap(roots_y, "c")]

    split = ((0,), (1, 2, 3))
    early1 = net.core_sum(early1)
    gx1, sums1, late1 = attention_backward(
        dims, weights1, net.late, pos, lengths, gz1, gctx, qkv1, lse1, y0, [sums], early1[1]
    )
    got = net.swaps(early1, "yx")
    net.hold(late1, got)
    early1 = net.add(early1[0], got, [gx1])
    late1 = net.core_sum(late1, early1[1])
    got_l, got_e = net.swaps(late1, "yx"), net.swaps(early1, "xy")
    gz0, gctx0, sums, early0 = ffn_backward(
        dims, weights0, net.early, pos, gx1, small[0], unit0, inv0, ctx0, unit0b, inv0b, act0, slope0,
        [*early1[1], *late1[1]],
    )
    net.hold(early0, [*got_l, *got_e])
    late1 = net.add(late1[0], got_l)
    got_l = net.swaps(late1, "xy")
    early0 = net.core_sum(early0, late1[1])
    whole1 = net.collect(split, (late1, early1), (got_l, got_e), early0[1])
    gx0, sums, late0 = attention_backward(
        dims, weights0, net.late, pos, lengths, gz0, gctx0, qkv0, lse0, x, [sums, sums1], [whole1]
    )

    got = net.swaps(early0, "yx")
    net.hold(late0, got)
    early0 = net.add(early0[0], got, [gx0])
    late0 = net.core_sum(late0, early0[1])
    got_l, got_e = net.swaps(late0, "yx"), net.swaps(early0, "xy")
    late0 = net.add(late0[0], got_l, got_e)
    got_l = net.swaps(late0, "xy")
    whole0 = net.collect(split, (late0, early0), (got_l, got_e))
    (low1,) = net.gate([net.column_sum(whole1)], late0[1])
    dealt = net.deal(whole0)
    (sums,) = net.gate([sums], [whole0])
    sums = net.small_sum_plane(sums)

    def update(n, wide, grads, before):
        return update_layer(
            n, pos, wide, left_stats, right_stats, left_roots, masters, grads, roots, before, [whole0]
        )

    done = update(1, low1, net.whole_group(low1), None)
    wide0, low0 = net.slab_sum(dealt, [done[0], sums])
    (sums,) = net.gate([sums], [low0])
    sums = net.small_sum_column(sums)
    done = update(0, wide0, net.group(low0), done)
    return y1, gx0, done, sums


def local(
    inputs,
    lengths,
    cotangent,
    masters,
    small_params,
    small_moments,
    left_stats,
    right_stats,
    left_roots,
    right_roots,
):
    chains, seq, width = inputs.shape
    rows = chains * seq
    groups, shards = lax.axis_size("grp"), lax.axis_size("fsdp")
    block = masters.shape[3]
    ffn = small_params.shape[1] - 8 * width
    dims = Dims(width, ffn, block, groups * masters.shape[1], rows)
    small = [small_params[n : n + 1] for n in range(LAYERS)]
    x, cot = inputs.reshape(rows, width), cotangent.reshape(rows, width)
    if groups == 2 * Z_SLABS and shards == 4:
        net = SmallSlice(dims)
        y, gx, done, sums = run_small(
            net, dims, small, lengths, x, cot, left_stats, right_stats, left_roots, right_roots, masters
        )
    else:
        net = AnySlice(dims)
        low = [masters[n].astype(BF) for n in range(LAYERS)]
        y, gx, owned, sums = run_any(net, dims, small, lengths, x, cot, low)
        done = update_plain(net, owned, masters, left_stats, right_stats, left_roots, right_roots)
    weight_grads, new_left, new_right, new_masters, new_copies = done
    small_grads, new_moments, new_small = update_small(sums, small_moments, small_params)
    return (
        y.reshape(chains, seq, width),
        gx.reshape(chains, seq, width),
        weight_grads,
        small_grads,
        new_moments,
        new_small,
        new_left,
        new_right,
        new_masters,
        new_copies,
    )


def solution(mesh):
    tokens, blocks = P(("grp", "fsdp"), None, None), P(None, "grp", "fsdp", None)
    return jax.shard_map(
        local,
        mesh=mesh,
        in_specs=(tokens, P(("grp", "fsdp")), tokens, blocks, P(), P(), blocks, blocks, blocks, blocks),
        out_specs=(tokens, tokens, blocks, P(), P(), P(), blocks, blocks, blocks, blocks),
        check_vma=False,
    )
```

```python
import functools

import jax
import jax.numpy as jnp
from jax import lax
from jax.experimental import pallas as pl
from jax.experimental.pallas import tpu as pltpu
from jax.sharding import PartitionSpec as P

HEADS = 12
LAYERS = 2
Z_SLABS = 4
BF = jnp.bfloat16
F32 = jnp.float32

norm_epsilon = 1e-05
matrix_rate = 1.0
small_rate = 0.3
decay_rate = 0.5
moment_epsilon = 1e-08

VMEM = pl.BlockSpec(memory_space=pltpu.VMEM)
SMEM = pl.BlockSpec(memory_space=pltpu.SMEM)
ANY = pl.BlockSpec(memory_space=pl.ANY)


def shape(dims, dtype):
    return jax.ShapeDtypeStruct(tuple(dims), dtype)


def mm(a, b):
    return jnp.dot(a, b, preferred_element_type=F32)


def mm_bt(a, b):
    return lax.dot_general(a, b, (((1,), (1,)), ((), ())), preferred_element_type=F32)


def mm_at(a, b):
    return lax.dot_general(a, b, (((0,), (0,)), ((), ())), preferred_element_type=F32)


class Part:
    def __init__(self, zs, js, order, arrays=None, offsets=(0, 0, 0, 0)):
        self.zs, self.js, self.order = tuple(zs), tuple(js), order
        self.arrays, self.offsets = arrays, offsets

    def index(self, first, second, z, j):
        place = self.zs.index(z) * len(self.js) + self.js.index(j)
        return (first * 2 + second) * len(self.zs) * len(self.js) + place

    def count(self):
        return 4 * len(self.zs) * len(self.js)


def launch(body, name, ins, out_shape, out_specs, deps=(), scratch=(), cost=None, aliases=None, limit=16, **grid):
    count, extra = len(ins), len(deps)

    def kernel(*refs):
        body(*refs[:count], *refs[count + extra :])

    flops, moved, special = 0, 0, 0
    return pl.pallas_call(
        kernel,
        in_specs=[spec for _, spec in ins] + [ANY] * extra,
        out_specs=out_specs,
        out_shape=out_shape,
        scratch_shapes=list(scratch),
        input_output_aliases=aliases or {},
        compiler_params=pltpu.CompilerParams(vmem_limit_bytes=limit << 20),
        cost_estimate=pl.CostEstimate(flops=flops, bytes_accessed=moved, transcendentals=special),
        name=name,
        **grid,
    )(*[array for array, _ in ins], *deps)


class Dims:
    def __init__(self, model, ffn, block, blocks, rows):
        self.model, self.ffn, self.block, self.blocks, self.rows = model, ffn, block, blocks, rows
        self.own = blocks // (2 * Z_SLABS)
        self.piece = block // 4
        wide, tall = model // block, ffn // block
        self.places = {}
        at = 0
        for name, rows_, cols_ in (
            ("q", wide, wide),
            ("k", wide, wide),
            ("v", wide, wide),
            ("o", wide, wide),
            ("up", wide, tall),
            ("down", tall, wide),
        ):
            self.places[name] = [
                (at + r * cols_ + c, r * block, c * block) for r in range(rows_) for c in range(cols_)
            ]
            at += rows_ * cols_

    def where(self, b):
        return b // (2 * self.own), (b // self.own) % 2, b % self.own


def find_part(parts, z, j):
    for number, part in enumerate(parts):
        if z in part.zs and j in part.js:
            return number
    raise ValueError("no part")


def needed_parts(dims, parts, names):
    used = set()
    for name in names:
        for b, _, _ in dims.places[name]:
            z, _, j = dims.where(b)
            used.add(find_part(parts, z, j))
    return [parts[n] for n in sorted(used)]


def start_loads(dims, parts, refs, pos, name, dst, row0, col0, sem):
    x, y, c = pos
    by_x = []

    def start(src, row, quarter, col):
        rows = pl.ds(pl.multiple_of(row0 + row + dims.piece * quarter, 16), dims.piece)
        pltpu.make_async_copy(src, dst.at[rows, pl.ds(col0 + col, dims.block)], sem).start()

    for b, row, col in dims.places[name]:
        z, xq, j = dims.where(b)
        number = find_part(parts, z, j)
        if parts[number].order == "xy":
            by_x.append((number, z, xq, j, row, col))
            continue
        for dc in range(2):
            for dy in range(2):
                n = 2 * dc + dy
                src = refs[number][n].at[parts[number].offsets[n] + parts[number].index(0, x ^ xq, z, j)]
                start(src, row, 2 * (y ^ dy) + (c ^ dc), col)
    if by_x:
        for own_x in range(2):

            @pl.when(x == own_x)
            def _(own_x=own_x):
                for number, z, xq, j, row, col in by_x:
                    for dc in range(2):
                        for yq in range(2):
                            n = 2 * dc + (own_x ^ xq)
                            at = parts[number].offsets[n] + parts[number].index(0, y ^ yq, z, j)
                            start(refs[number][n].at[at], row, 2 * yq + (c ^ dc), col)


def wait_for(ref, sem):
    pltpu.make_async_copy(ref, ref, sem).wait()


def start_stores(dims, parts, outs, pos, places, src, sem):
    x, y, c = pos
    for b, row, col in places:
        z, xq, j = dims.where(b)
        number = find_part(parts, z, j)
        for dc in range(2):
            for yq in range(2):
                ends = (x ^ xq, y ^ yq) if parts[number].order == "xy" else (y ^ yq, x ^ xq)
                rows = pl.ds(pl.multiple_of(row + dims.piece * (2 * yq + (c ^ dc)), 16), dims.piece)
                dst = outs[number][dc].at[parts[number].index(*ends, z, j)]
                pltpu.make_async_copy(src.at[rows, pl.ds(col, dims.block)], dst, sem).start()


def norm_forward(values):
    center = values - jnp.mean(values, axis=-1, keepdims=True)
    spread = jnp.mean(center * center, axis=-1, keepdims=True)
    inverse = lax.rsqrt(spread + norm_epsilon)
    return center * inverse, inverse


def norm_backward(gradient, unit, inverse, gain):
    scaled = gradient * gain
    inner = (
        scaled
        - jnp.mean(scaled, axis=-1, keepdims=True)
        - unit * jnp.mean(scaled * unit, axis=-1, keepdims=True)
    )
    return inverse * inner


def col_sum(values):
    return jnp.sum(values.astype(F32), axis=0, keepdims=True)


def put_rows(sums_ref, number, values):
    count = values.shape[1] // 128
    for n in range(count):
        at = number * count + n
        sums_ref[at : at + 1, :] = values[:, 128 * n : 128 * (n + 1)]


def launch_list(*args, **kwargs):
    return list(launch(*args, **kwargs))


def segment(small_ref, number, width):
    return small_ref[0:1, number * width : (number + 1) * width]


def unflatten(refs, parts):
    return [refs[4 * n : 4 * n + 4] for n in range(len(parts))], refs[4 * len(parts) :]


def weight_ins(parts):
    return [(a, ANY) for p in parts for a in p.arrays]


def half_masks(head):
    lane = lax.broadcasted_iota(jnp.int32, (1, 2 * head), 1)
    low = lane < head
    ones = jnp.where(low, 1.0, 0.0).astype(F32)
    return low, (ones.astype(BF), (1.0 - ones).astype(BF))


def attention_forward_kernel(dims, parts, chains, pos_ref, len_ref, x_ref, small_ref, *rest):
    refs, rest = unflatten(rest, parts)
    qkv_ref, lse_ref, ctx_ref, unit_ref, inv_ref, w, sems = rest
    width, seq = dims.model, dims.rows // chains
    head = width // HEADS
    pos = (pos_ref[1], pos_ref[2], pos_ref[3])
    for n, name in enumerate(("q", "k", "v", "o")):
        start_loads(dims, parts, refs, pos, name, w, 0, n * width, sems.at[n])
    xb = x_ref[...].astype(BF)
    for n, bias in ((0, 0), (1, None), (2, 1)):
        cols = slice(n * width, (n + 1) * width)
        wait_for(w.at[:, cols], sems.at[n])
        out = mm(xb, w[:, cols])
        if bias is not None:
            out = out + segment(small_ref, bias, width)
        qkv_ref[:, cols] = out.astype(BF)
    low, masks = half_masks(head)
    scale = head**-0.5

    def chain(i, carry):
        rows = pl.ds(pl.multiple_of(i * seq, 16), seq)
        valid = lax.broadcasted_iota(jnp.int32, (seq, seq), 0) < len_ref[i]
        for pair in range(HEADS // 2):
            at = pair * 2 * head
            q = qkv_ref[rows, at : at + 2 * head]
            k = qkv_ref[rows, width + at : width + at + 2 * head]
            v = qkv_ref[rows, 2 * width + at : 2 * width + at + 2 * head]
            outs = []
            for h in range(2):
                s = jnp.where(valid, mm_bt(k, q * masks[h]) * scale, -1000000000.0)
                top = jnp.max(s, axis=0, keepdims=True)
                e = jnp.exp(s - top)
                total = jnp.sum(e, axis=0, keepdims=True)
                lse_ref[i, 2 * pair + h : 2 * pair + h + 1, :] = top + jnp.log(total)
                outs.append(mm_at((e * (1.0 / total)).astype(BF), v))
            ctx_ref[rows, at : at + 2 * head] = jnp.where(low, outs[0], outs[1]).astype(BF)
        return carry

    lax.fori_loop(0, chains, chain, 0)
    wait_for(w.at[:, 3 * width :], sems.at[3])
    attended = mm(ctx_ref[...], w[:, 3 * width :]) + segment(small_ref, 2, width)
    unit, inverse = norm_forward(x_ref[...].astype(F32) + attended)
    unit_ref[...] = unit
    inv_ref[...] = inverse


def attention_forward(dims, parts, pos, lengths, x, small, deps=()):
    parts = needed_parts(dims, parts, ("q", "k", "v", "o"))
    chains = lengths.shape[0]
    rows, width = dims.rows, dims.model
    return launch(
        functools.partial(attention_forward_kernel, dims, parts, chains),
        "attention_forward",
        [(pos, SMEM), (lengths, SMEM), (x, VMEM), (small, VMEM)] + weight_ins(parts),
        [
            shape((rows, 3 * width), BF),
            shape((chains, HEADS, rows // chains), F32),
            shape((rows, width), BF),
            shape((rows, width), F32),
            shape((rows, 1), F32),
        ],
        [VMEM] * 5,
        deps,
        [pltpu.VMEM((width, 4 * width), BF), pltpu.SemaphoreType.DMA((4,))],
        (12 * rows * width * width, 16 << 20, 1 << 20),
        limit=56,
    )


def ffn_forward_body(dims, small_ref, unit_ref, up, down, sems, act_ref, slope_ref):
    width = dims.model
    h1 = unit_ref[...] * segment(small_ref, 4, width) + segment(small_ref, 5, width)
    hb = h1.astype(BF)
    total = h1 + segment(small_ref, 3, width)
    wait_for(up, sems.at[0])
    for n in range(dims.ffn // width):
        cols = slice(n * width, (n + 1) * width)
        u = mm(hb, up[:, cols]) + segment(small_ref, 8 + n, width)
        cdf = 0.5 * (1.0 + lax.erf(u * 0.7071067811865476))
        act = (u * cdf).astype(BF)
        act_ref[:, cols] = act
        slope_ref[:, cols] = (cdf + u * (0.3989422804014327 * jnp.exp(-0.5 * u * u))).astype(BF)
        if n == 0:
            wait_for(down, sems.at[1])
        total = total + mm(act, down[cols, :])
    return total


def ffn_forward_kernel(dims, parts, pos_ref, unit_ref, small_ref, *rest):
    refs, rest = unflatten(rest, parts)
    act_ref, slope_ref, unit2_ref, inv2_ref, y_ref, up, down, sems = rest
    pos = (pos_ref[1], pos_ref[2], pos_ref[3])
    start_loads(dims, parts, refs, pos, "up", up, 0, 0, sems.at[0])
    start_loads(dims, parts, refs, pos, "down", down, 0, 0, sems.at[1])
    width = dims.model
    total = ffn_forward_body(dims, small_ref, unit_ref, up, down, sems, act_ref, slope_ref)
    unit, inverse = norm_forward(total)
    unit2_ref[...] = unit
    inv2_ref[...] = inverse
    y_ref[...] = unit * segment(small_ref, 6, width) + segment(small_ref, 7, width)


def ffn_forward(dims, parts, pos, unit, small, deps=()):
    parts = needed_parts(dims, parts, ("up", "down"))
    rows, width, ffn = dims.rows, dims.model, dims.ffn
    return launch(
        functools.partial(ffn_forward_kernel, dims, parts),
        "ffn_forward",
        [(pos, SMEM), (unit, VMEM), (small, VMEM)] + weight_ins(parts),
        [
            shape((rows, ffn), BF),
            shape((rows, ffn), BF),
            shape((rows, width), F32),
            shape((rows, 1), F32),
            shape((rows, width), F32),
        ],
        [VMEM] * 5,
        deps,
        [pltpu.VMEM((width, ffn), BF), pltpu.VMEM((ffn, width), BF), pltpu.SemaphoreType.DMA((2,))],
        (4 * rows * width * ffn, 24 << 20, 3 << 20),
        limit=56,
    )


def ffn_backward_body(
    dims, outs_parts, outs, pos, gy, small_ref, unit_ref, inv_ref, ctx_ref, unit2, inv2, act_ref, slope_ref,
    up, down, wo, grad_up, grad_down, grad_o, sem_out, gz1_ref, gctx_ref, sums_ref, wait_o,
):
    width = dims.model
    gain1, gain2 = segment(small_ref, 4, width), segment(small_ref, 6, width)

    def put(number, values):
        put_rows(sums_ref, number, values)

    put(6, col_sum(gy * unit2))
    put(7, col_sum(gy))
    gz2 = norm_backward(gy, unit2, inv2, gain2)
    gf = gz2.astype(BF)
    put(3, col_sum(gf))
    hb = (unit_ref[...] * gain1 + segment(small_ref, 5, width)).astype(BF)
    gh1 = gz2
    block = dims.block
    for n in range(dims.ffn // width):
        cols = slice(n * width, (n + 1) * width)
        gu = (slope_ref[:, cols].astype(F32) * mm_bt(gf, down[cols, :])).astype(BF)
        put(8 + n, col_sum(gu))
        grad_up[:, cols] = mm_at(hb, gu).astype(BF)
        grad_down[cols, :] = mm_at(act_ref[:, cols], gf).astype(BF)
        low, high = n * width, (n + 1) * width
        start_stores(
            dims, outs_parts, outs, pos,
            [p for p in dims.places["up"] if low <= p[2] < high], grad_up, sem_out.at[0],
        )
        start_stores(
            dims, outs_parts, outs, pos,
            [p for p in dims.places["down"] if low <= p[1] < high], grad_down, sem_out.at[1],
        )
        gh1 = gh1 + mm_bt(gu, up[:, cols])
    unit = unit_ref[...]
    put(4, col_sum(gh1 * unit))
    put(5, col_sum(gh1))
    gz1 = norm_backward(gh1, unit, inv_ref[...], gain1)
    gz1_ref[...] = gz1
    ga = gz1.astype(BF)
    put(2, col_sum(ga))
    grad_o[...] = mm_at(ctx_ref[...], ga).astype(BF)
    start_stores(dims, outs_parts, outs, pos, dims.places["o"], grad_o, sem_out.at[2])
    wait_o()
    gctx_ref[...] = mm_bt(ga, wo[...]).astype(BF)
    put(0, jnp.zeros((1, width), F32))
    put(1, jnp.zeros((1, width), F32))
    wait_for(grad_up, sem_out.at[0])
    wait_for(grad_down, sem_out.at[1])
    wait_for(grad_o, sem_out.at[2])


def grad_shapes(dims, parts):
    return [shape((p.count(), dims.piece, dims.block), BF) for p in parts for _ in range(2)]


def pair_up(arrays, parts):
    return [Part(p.zs, p.js, p.order, list(arrays[2 * n : 2 * n + 2])) for n, p in enumerate(parts)]


def ffn_scratch(dims):
    width, ffn = dims.model, dims.ffn
    matrices = [(width, ffn), (ffn, width), (width, width)] * 2
    return [pltpu.VMEM(m, BF) for m in matrices] + [pltpu.SemaphoreType.DMA((3,))] * 2


def ffn_backward_kernel(dims, parts, outs_parts, pos_ref, gy_ref, small_ref, unit_ref, inv_ref, ctx_ref, unit2_ref, inv2_ref, act_ref, slope_ref, *rest):
    refs, rest = unflatten(rest, parts)
    gz1_ref, gctx_ref, sums_ref, *rest = rest
    count = 2 * len(outs_parts)
    outs = [rest[2 * n : 2 * n + 2] for n in range(len(outs_parts))]
    up, down, wo, grad_up, grad_down, grad_o, sems, sem_out = rest[count:]
    pos = (pos_ref[1], pos_ref[2], pos_ref[3])
    start_loads(dims, parts, refs, pos, "down", down, 0, 0, sems.at[1])
    start_loads(dims, parts, refs, pos, "up", up, 0, 0, sems.at[0])
    start_loads(dims, parts, refs, pos, "o", wo, 0, 0, sems.at[2])
    wait_for(down, sems.at[1])
    wait_for(up, sems.at[0])
    ffn_backward_body(
        dims, outs_parts, outs, pos, gy_ref[...], small_ref, unit_ref, inv_ref, ctx_ref,
        unit2_ref[...], inv2_ref[...], act_ref, slope_ref, up, down, wo, grad_up, grad_down, grad_o,
        sem_out, gz1_ref, gctx_ref, sums_ref, lambda: wait_for(wo, sems.at[2]),
    )


def ffn_backward(dims, parts, outs_parts, pos, gy, small, unit, inv, ctx, unit2, inv2, act, slope, deps=()):
    parts = needed_parts(dims, parts, ("up", "down", "o"))
    rows, width, ffn = dims.rows, dims.model, dims.ffn
    grads = grad_shapes(dims, outs_parts)
    out = launch(
        functools.partial(ffn_backward_kernel, dims, parts, outs_parts),
        "ffn_backward",
        [(pos, SMEM)]
        + [(a, VMEM) for a in (gy, small, unit, inv, ctx, unit2, inv2, act, slope)]
        + weight_ins(parts),
        [shape((rows, width), F32), shape((rows, width), BF), shape((small.shape[1] // 128, 128), F32)] + grads,
        [VMEM] * 3 + [ANY] * len(grads),
        deps,
        ffn_scratch(dims),
        (8 * rows * width * ffn + 4 * rows * width * width, 40 << 20, 0),
        limit=56,
    )
    return out[0], out[1], out[2], pair_up(out[3:], outs_parts)


def ffn_both_kernel(dims, parts, outs_parts, chains, pos_ref, len_ref, cot_ref, small_ref, unit_ref, inv_ref, ctx_ref, *rest):
    refs, rest = unflatten(rest, parts)
    y_ref, gz1_ref, gctx_ref, sums_ref, *rest = rest
    count = 2 * len(outs_parts)
    outs = [rest[2 * n : 2 * n + 2] for n in range(len(outs_parts))]
    up, down, wo, grad_up, grad_down, grad_o, sems, sem_out, act_ref, slope_ref = rest[count:]
    pos = (pos_ref[1], pos_ref[2], pos_ref[3])
    start_loads(dims, parts, refs, pos, "up", up, 0, 0, sems.at[0])
    start_loads(dims, parts, refs, pos, "down", down, 0, 0, sems.at[1])
    start_loads(dims, parts, refs, pos, "o", wo, 0, 0, sems.at[2])
    width, seq = dims.model, dims.rows // chains
    total = ffn_forward_body(dims, small_ref, unit_ref, up, down, sems, act_ref, slope_ref)
    unit2, inv2 = norm_forward(total)
    y_ref[...] = (unit2 * segment(small_ref, 6, width) + segment(small_ref, 7, width)).astype(BF)
    place = lax.broadcasted_iota(jnp.int32, (seq, width), 0)
    gy = jnp.concatenate(
        [
            jnp.where(place < len_ref[i], cot_ref[i * seq : (i + 1) * seq, :].astype(F32), 0.0)
            for i in range(chains)
        ],
        axis=0,
    )
    ffn_backward_body(
        dims, outs_parts, outs, pos, gy, small_ref, unit_ref, inv_ref, ctx_ref,
        unit2, inv2, act_ref, slope_ref, up, down, wo, grad_up, grad_down, grad_o,
        sem_out, gz1_ref, gctx_ref, sums_ref, lambda: wait_for(wo, sems.at[2]),
    )


def ffn_both(dims, parts, outs_parts, pos, lengths, cot, small, unit, inv, ctx, deps=()):
    parts = needed_parts(dims, parts, ("up", "down", "o"))
    rows, width, ffn = dims.rows, dims.model, dims.ffn
    grads = grad_shapes(dims, outs_parts)
    out = launch(
        functools.partial(ffn_both_kernel, dims, parts, outs_parts, lengths.shape[0]),
        "ffn_both",
        [(pos, SMEM), (lengths, SMEM)]
        + [(a, VMEM) for a in (cot, small, unit, inv, ctx)]
        + weight_ins(parts),
        [
            shape((rows, width), BF),
            shape((rows, width), F32),
            shape((rows, width), BF),
            shape((small.shape[1] // 128, 128), F32),
        ]
        + grads,
        [VMEM] * 4 + [ANY] * len(grads),
        deps,
        ffn_scratch(dims) + [pltpu.VMEM((rows, ffn), BF)] * 2,
        (12 * rows * width * ffn + 4 * rows * width * width, 40 << 20, 3 << 20),
        limit=56,
    )
    return out[0], out[1], out[2], out[3], pair_up(out[4:], outs_parts)


def attention_backward_kernel(dims, parts, outs_parts, chains, given, pos_ref, len_ref, gz1_ref, gctx_ref, qkv_ref, lse_ref, x_ref, *rest):
    given_refs, rest = rest[:given], rest[given:]
    refs, rest = unflatten(rest, parts)
    gx_ref, sums_ref, *rest = rest
    count = 2 * len(outs_parts)
    outs = [rest[2 * n : 2 * n + 2] for n in range(len(outs_parts))]
    w, grads_ref, grad_w, sems, sem_out = rest[count:]
    pos = (pos_ref[1], pos_ref[2], pos_ref[3])
    width, seq = dims.model, dims.rows // chains
    head = width // HEADS
    names = ("q", "k", "v")
    for n, name in enumerate(names):
        start_loads(dims, parts, refs, pos, name, w, 0, n * width, sems.at[n])
    low, masks = half_masks(head)
    scale = head**-0.5

    def chain(i, carry):
        rows = pl.ds(pl.multiple_of(i * seq, 16), seq)
        valid = lax.broadcasted_iota(jnp.int32, (seq, seq), 0) < len_ref[i]
        for pair in range(HEADS // 2):
            at = pair * 2 * head
            q = qkv_ref[rows, at : at + 2 * head]
            k = qkv_ref[rows, width + at : width + at + 2 * head]
            v = qkv_ref[rows, 2 * width + at : 2 * width + at + 2 * head]
            g = gctx_ref[rows, at : at + 2 * head]
            gq, gk, gv = [], [], []
            for h in range(2):
                s = jnp.where(valid, mm_bt(k, q * masks[h]) * scale, -1000000000.0)
                p = jnp.exp(s - lse_ref[i, 2 * pair + h : 2 * pair + h + 1, :])
                gp = mm_bt(v, g * masks[h])
                inner = jnp.sum(p * gp, axis=0, keepdims=True)
                gs = (p * (gp - inner)).astype(BF)
                gv.append(mm(p.astype(BF), g))
                gk.append(mm(gs, q))
                gq.append(mm_at(gs, k))
            grads_ref[rows, at : at + 2 * head] = (jnp.where(low, gq[0], gq[1]) * scale).astype(BF)
            grads_ref[rows, width + at : width + at + 2 * head] = (
                jnp.where(low, gk[0], gk[1]) * scale
            ).astype(BF)
            grads_ref[rows, 2 * width + at : 2 * width + at + 2 * head] = jnp.where(
                low, gv[0], gv[1]
            ).astype(BF)
        return carry

    lax.fori_loop(0, chains, chain, 0)
    xb = x_ref[...].astype(BF)
    for n, name in enumerate(names):
        cols = slice(n * width, (n + 1) * width)
        grad_w[:, cols] = mm_at(xb, grads_ref[:, cols]).astype(BF)
        places = [(b, r, c + n * width) for b, r, c in dims.places[name]]
        start_stores(dims, outs_parts, outs, pos, places, grad_w, sem_out)
    at = 0
    for ref in given_refs:
        sums_ref[at : at + ref.shape[0], :] = ref[...]
        at += ref.shape[0]
    put_rows(sums_ref, 0, col_sum(grads_ref[:, :width]))
    put_rows(sums_ref, 1, col_sum(grads_ref[:, 2 * width :]))
    gx = gz1_ref[...]
    for n in range(3):
        cols = slice(n * width, (n + 1) * width)
        wait_for(w.at[:, cols], sems.at[n])
        gx = gx + mm_bt(grads_ref[:, cols], w[:, cols])
    gx_ref[...] = gx
    wait_for(grad_w, sem_out)


def attention_backward(dims, parts, outs_parts, pos, lengths, gz1, gctx, qkv, lse, x, sums, deps=()):
    parts = needed_parts(dims, parts, ("q", "k", "v"))
    rows, width = dims.rows, dims.model
    grads = grad_shapes(dims, outs_parts)
    out = launch(
        functools.partial(attention_backward_kernel, dims, parts, outs_parts, lengths.shape[0], len(sums)),
        "attention_backward",
        [(pos, SMEM), (lengths, SMEM)] + [(a, VMEM) for a in (gz1, gctx, qkv, lse, x, *sums)] + weight_ins(parts),
        [shape((rows, width), F32), shape((sum(a.shape[0] for a in sums), 128), F32)] + grads,
        [VMEM] * 2 + [ANY] * len(grads),
        deps,
        [
            pltpu.VMEM((width, 3 * width), BF),
            pltpu.VMEM((rows, 3 * width), BF),
            pltpu.VMEM((width, 3 * width), BF),
            pltpu.SemaphoreType.DMA((3,)),
            pltpu.SemaphoreType.DMA,
        ],
        (24 * rows * width * width, 24 << 20, 1 << 20),
        limit=56,
    )
    return out[0], out[1], pair_up(out[2:], outs_parts)


class AnySlice:
    def __init__(self, dims):
        self.dims = dims
        own = range(dims.own)
        self.early = [Part((1, 2, 3), own, "yx")]
        self.late = [Part((0,), own, "yx")]

    def position(self):
        return jnp.zeros((4,), jnp.int32)

    def gather(self, low):
        dims = self.dims
        whole = lax.all_gather(low, "fsdp", axis=1, tiled=True)
        whole = lax.all_gather(whole, "grp", axis=0, tiled=True)
        split = whole.reshape(Z_SLABS, 2, dims.own, 2, 2, dims.piece, dims.block)
        order = split.transpose(4, 3, 1, 0, 2, 5, 6).reshape(4, -1, dims.piece, dims.block)
        return [Part(range(Z_SLABS), range(dims.own), "yx", [order[n] for n in range(4)])]

    def reduce(self, early, late):
        dims = self.dims
        pieces = []
        for part in (late[0], early[0]):
            stacked = jnp.stack(part.arrays)
            split = stacked.reshape(2, 2, 2, len(part.zs), dims.own, dims.piece, dims.block)
            pieces.append(split.transpose(3, 2, 4, 1, 0, 5, 6))
        whole = jnp.concatenate(pieces, axis=0).reshape(dims.blocks, dims.block, dims.block)
        rows = lax.psum_scatter(whole, "fsdp", scatter_dimension=1, tiled=True)
        return lax.psum_scatter(rows, "grp", scatter_dimension=0, tiled=True).astype(F32)

    def small_sum(self, values):
        return lax.psum(values, ("grp", "fsdp"))

    def group(self, owned):
        return lax.all_gather(owned, "fsdp", axis=1, tiled=True)


def swap_of(axis):
    def move(z, x, y, c):
        return (z, x ^ (axis == "x"), y ^ (axis == "y"), c ^ (axis == "c"))

    return move


def join_kernel(ranges, *refs):
    pairs = len(ranges)
    ins, outs, hold, sems = refs[: 2 * pairs], refs[2 * pairs : 3 * pairs + 1], refs[-3], refs[-2:]
    runs, at = [], 0
    for n, (low, count) in enumerate(ranges):
        runs.append(hold.at[pl.ds(at, 2 * count)])
        for half in range(2):
            src = ins[2 * n + half].at[pl.ds(low, count)]
            pltpu.make_async_copy(src, hold.at[pl.ds(at + half * count, count)], sems[0].at[n]).start()
        at += 2 * count
    for n in range(pairs):
        wait_for(runs[n], sems[0].at[n])
        pltpu.make_async_copy(runs[n], outs[n], sems[1].at[n]).start()
    pltpu.make_async_copy(hold, outs[pairs], sems[1].at[pairs]).start()
    for n in range(pairs):
        wait_for(runs[n], sems[1].at[n])
    wait_for(hold, sems[1].at[pairs])


def round_kernel(src_ref, dst_ref):
    dst_ref[...] = src_ref[...].astype(BF)


def add_kernel(a_ref, b_ref, first_ref, second_ref):
    half = first_ref.shape[0]

    def piece(i, carry):
        for out, at in ((first_ref, i), (second_ref, i + half)):
            out[i] = (a_ref[at].astype(F32) + b_ref[at].astype(F32)).astype(BF)
        return carry

    lax.fori_loop(0, half, piece, 0)


def collect_kernel(zs, *refs):
    pairs = len(zs)
    ins, out, total, holds, sems = refs[: 2 * pairs], refs[2 * pairs], refs[2 * pairs + 1], refs[2 * pairs + 2 : -1], refs[-1]
    for n in range(2 * pairs):
        pltpu.make_async_copy(ins[n], holds[n], sems.at[n]).start()
    half = holds[0].shape[0] // len(zs[0])
    copies = []
    for n, z_list in enumerate(zs):
        wait_for(holds[2 * n], sems.at[2 * n])
        wait_for(holds[2 * n + 1], sems.at[2 * n + 1])
        for place, want in enumerate(z_list):
            piece, at = pl.ds(place * half, half), pl.ds((2 * want + n % 2) * half, half)
            value = holds[2 * n][piece].astype(F32) + holds[2 * n + 1][piece].astype(F32)
            total[at] = value.astype(BF)
            copies.append(pltpu.make_async_copy(total.at[at], out.at[at], sems.at[2 * pairs]))
            copies[-1].start()
    wait_for(total, sems.at[2 * pairs])


def pick_kernel(places, src_ref, *refs):
    outs, holds, sems = refs[: len(places)], refs[len(places) : -2], refs[-2:]
    for n, runs in enumerate(places):
        at = 0
        for low, count in runs:
            dst = holds[n].at[pl.ds(at, count)]
            pltpu.make_async_copy(src_ref.at[pl.ds(low, count)], dst, sems[0].at[n]).start()
            at += count
    for n in range(len(places)):
        wait_for(holds[n], sems[0].at[n])
        pltpu.make_async_copy(holds[n], outs[n], sems[1].at[n]).start()
    for n in range(len(places)):
        wait_for(holds[n], sems[1].at[n])


def pass_kernel(*refs):
    pass


class SmallSlice:
    def __init__(self, dims):
        self.dims = dims
        a, b = range(dims.own // 2), range(dims.own // 2, dims.own)
        self.early = [Part((1, 2, 3), a, "yx"), Part((1, 2, 3), b, "xy")]
        self.late = [Part((0,), a, "yx"), Part((0,), b, "xy")]
        group, shard = lax.axis_index("grp"), lax.axis_index("fsdp")
        self.z, self.x, self.y, self.c = group // 2, group % 2, shard // 2, shard % 2
        self.pos = jnp.stack([self.z, self.x, self.y, self.c]).astype(jnp.int32)

    def position(self):
        return self.pos

    def pieces(self, count):
        return shape((count, self.dims.piece, self.dims.block), BF)

    def permute(self, array, move):
        pairs = []
        for flat in range(8 * Z_SLABS):
            to = move(flat // 8, flat // 4 % 2, flat // 2 % 2, flat % 2)
            if to is not None:
                pairs.append((flat, ((to[0] * 2 + to[1]) * 2 + to[2]) * 2 + to[3]))
        return lax.ppermute(array, ("grp", "fsdp"), pairs)

    def swap(self, array, axis):
        return self.permute(array, swap_of(axis))

    def rounded(self, wide, deps=()):
        return launch(round_kernel, "rounded", [(wide, VMEM)], shape(wide.shape, BF), VMEM, deps)

    def columns(self):
        return [[2 * z + x for z in range(Z_SLABS)] for x in range(2)]

    def whole_column(self, own):
        return lax.all_gather(own, "grp", axis_index_groups=self.columns(), axis=0, tiled=True)

    def whole_lot(self, whole, zs, js, deps=()):
        half, count = len(js) // 2, len(js)
        places = [[(z * count + low, half) for z in zs] for low in (0, half)]
        sizes = [self.pieces(len(zs) * half)] * 2
        arrays = launch(
            functools.partial(pick_kernel, places),
            "pick",
            [(whole, ANY)],
            sizes,
            [ANY] * 2,
            deps,
            [pltpu.VMEM(s.shape, BF) for s in sizes] + [pltpu.SemaphoreType.DMA((2,))] * 2,
            limit=60,
        )
        halves = ((js[:half], "yx"), (js[half:], "xy"))
        return [(Part(zs, j, order), a) for (j, order), a in zip(halves, arrays)]

    def gate(self, arrays, deps):
        return launch(
            pass_kernel,
            "gate",
            [(a, ANY) for a in arrays],
            [shape(a.shape, a.dtype) for a in arrays],
            [ANY] * len(arrays),
            deps,
            aliases={n: n for n in range(len(arrays))},
            limit=60,
        )

    def hold(self, parts, deps):
        for part, array in zip(parts, self.gate([p.arrays[1] for p in parts], deps)):
            part.arrays[1] = array

    def first_swap(self, lot):
        return [self.swap(a, part.order[1]) for part, a in lot]

    def joined(self, lot, got, zs, deps=()):
        ins, ranges, sizes = [], [], []
        for (part, own), g in zip(lot, got):
            count = len(part.js)
            ranges.append((part.zs.index(zs[0]) * count, len(zs) * count))
            sizes.append(self.pieces(2 * len(zs) * count))
            ins += [own, g]
        return launch_list(
            functools.partial(join_kernel, ranges),
            "join",
            [(a, ANY) for a in ins],
            sizes + [self.pieces(sum(a.shape[0] for a in sizes))],
            [ANY] * (len(lot) + 1),
            deps,
            [pltpu.VMEM((sum(a.shape[0] for a in sizes),) + sizes[0].shape[1:], BF)]
            + [pltpu.SemaphoreType.DMA((2,)), pltpu.SemaphoreType.DMA((3,))],
        )

    def second_swap(self, lot, both):
        return [self.swap(b, part.order[0]) for (part, _), b in zip(lot, both)]

    def core_swap(self, lot, zs, both, got):
        others = self.swap(both[-1], "c")
        parts, at = [], 0
        for (part, _), b, g in zip(lot, both, got):
            parts.append(Part(zs, part.js, part.order, [b, g, others, self.swap(g, "c")], (0, 0, at, 0)))
            at += b.shape[0]
        return parts

    def add(self, keep, got, deps=()):
        sums = []
        for own, other in zip(keep, got):
            out = [self.pieces(own.shape[0] // 2)] * 2
            sums.append(launch(add_kernel, "add", [(own, VMEM), (other, VMEM)], out, [VMEM] * 2, deps))
        return [kept for kept, _ in sums], [sent for _, sent in sums]

    def core_sum(self, parts, deps=()):
        got = [self.swap(p.arrays[1], "c") for p in parts]
        return self.add([p.arrays[0] for p in parts], got, deps)

    def swaps(self, sums, axes):
        return [self.swap(a, axis) for a, axis in zip(sums[1], axes)]

    def collect(self, zs, sums, got, deps=()):
        ins = []
        for (kept, _), others in zip(sums, got):
            for own, other in zip(kept, others):
                ins += [own, other]
        return launch(
            functools.partial(collect_kernel, [z for z in zs for _ in range(2)]),
            "collect",
            [(a, ANY) for a in ins],
            self.pieces(Z_SLABS * self.dims.own),
            ANY,
            deps,
            [pltpu.VMEM((Z_SLABS * self.dims.own,) + ins[0].shape[1:], BF)]
            + [pltpu.VMEM(a.shape, BF) for a in ins]
            + [pltpu.SemaphoreType.DMA((len(ins) + 1,))],
        )

    def column_sum(self, whole):
        return lax.psum_scatter(
            whole, "grp", axis_index_groups=self.columns(), scatter_dimension=0, tiled=True
        )

    def small_sum(self, values, axes, bits):
        for axis in axes:
            values = values + self.swap(values, axis)
        for bit in bits:
            values = values + self.permute(values, lambda z, x, y, c, bit=bit: (z ^ bit, x, y, c))
        return values

    def group(self, own):
        other = self.swap(own, "y")
        return [own, other, self.swap(own, "c"), self.swap(other, "c")]


def update_kernel(layer, first, count_grads, pos_ref, own_ref, *rest):
    stats, grads, rest = rest[:4], rest[4 : 4 + count_grads], rest[4 + count_grads :]
    roots, rest = rest[:4], rest[4:]
    if not first:
        rest = rest[5:]
    outs, rest = rest[:5], rest[5:]
    g_ref, r_ref, turned, own, held, fresh, low_ref, sem_g, sem_r, sem_in, sem_out = rest
    y, c = pos_ref[2], pos_ref[3]
    count, piece, block = own_ref.shape

    def quarter(yq, cq):
        return pl.ds(pl.multiple_of(piece * (2 * yq + cq), 16), piece)

    for n in range(count_grads):
        rows = quarter(y ^ (n % 2), c ^ (n // 2)) if count_grads == 4 else pl.ds(0, block)
        if count_grads == 4:
            pltpu.make_async_copy(grads[n], g_ref.at[:, rows, :], sem_g).start()
    if count_grads == 1:
        for n in range(4):
            mine = grads[0].at[pl.ds(n * count, count)]
            pltpu.make_async_copy(mine, g_ref.at[:, pl.ds(n * piece, piece), :], sem_g).start()
    for n in range(4):
        mine = roots[n].at[pl.ds(layer * count, count)]
        pltpu.make_async_copy(mine, r_ref.at[:, quarter(y ^ (n % 2), c ^ (n // 2)), :], sem_r).start()
    for n in range(4):
        pltpu.make_async_copy(stats[n].at[layer], held.at[n], sem_in.at[n]).start()
    pltpu.make_async_copy(own_ref, own, sem_in.at[4]).start()
    own_rows = quarter(y, c)
    wait_for(g_ref, sem_g)
    def halves(value):
        high = value.astype(BF)
        return [high, (value - high.astype(F32)).astype(BF)]

    for b in range(count):
        g = g_ref[b]
        turned[...] = g.T
        if b == 0:
            wait_for(held.at[0], sem_in.at[0])
        fresh[1, b] = decay_rate * held[0, b] + (1.0 - decay_rate) * mm_bt(g_ref[b, own_rows, :], g)
        if b == 0:
            wait_for(held.at[1], sem_in.at[1])
            wait_for(held.at[2], sem_in.at[2])
        products = mm(jnp.concatenate([turned[own_rows, :], *halves(held[2, b])], axis=0), g)
        fresh[2, b] = decay_rate * held[1, b] + (1.0 - decay_rate) * products[:piece]
        if b == 0:
            wait_for(r_ref, sem_r)
        mixed = products[piece : 2 * piece] + products[2 * piece :]
        products = mm(jnp.concatenate(halves(mixed), axis=0), r_ref[b])
        update = products[:piece] + products[piece:]
        if b == 0:
            wait_for(held.at[3], sem_in.at[3])
            wait_for(own, sem_in.at[4])
        master = held[3, b] - matrix_rate * update
        fresh[3, b] = master
        low_ref[b] = master.astype(BF)
        fresh[0, b] = own[b].astype(F32)
        for n in range(4):
            pltpu.make_async_copy(fresh.at[n, b], outs[n].at[layer, b], sem_out.at[0]).start()
        pltpu.make_async_copy(low_ref.at[b], outs[4].at[layer, b], sem_out.at[1]).start()
    wait_for(fresh, sem_out.at[0])
    wait_for(low_ref, sem_out.at[1])


def update_layer(layer, pos, own, left, right, left_roots, masters, grads, roots, before, deps=()):
    count, piece, block = own.shape
    whole = (LAYERS, count, piece, block)
    ins = [(pos, SMEM), (own, ANY)] + [(a, ANY) for a in (left, right, left_roots, masters)]
    ins += [(a, ANY) for a in grads] + [(a, ANY) for a in roots]
    aliases = {}
    if before is not None:
        aliases = {len(ins) + n: n for n in range(5)}
        ins += [(a, ANY) for a in before]
    return launch(
        functools.partial(update_kernel, layer, before is None, len(grads)),
        "update_layer",
        ins,
        [shape(whole, F32)] * 4 + [shape(whole, BF)],
        [ANY] * 5,
        deps,
        [
            pltpu.VMEM((count, block, block), BF),
            pltpu.VMEM((count, block, block), BF),
            pltpu.VMEM((block, block), BF),
            pltpu.VMEM(own.shape, own.dtype),
            pltpu.VMEM((4,) + own.shape, F32),
            pltpu.VMEM((4,) + own.shape, F32),
            pltpu.VMEM(own.shape, BF),
            pltpu.SemaphoreType.DMA,
            pltpu.SemaphoreType.DMA,
            pltpu.SemaphoreType.DMA((5,)),
            pltpu.SemaphoreType.DMA((2,)),
        ],
        (0, 0, 0),
        aliases,
        limit=56,
    )


def update_plain(net, owned, masters, left_stats, right_stats, left_roots, right_roots):
    own_rows = masters.shape[2]
    first_row = lax.axis_index("fsdp") * own_rows
    highest = lax.Precision.HIGHEST
    grads = jnp.stack(owned)
    whole = jnp.stack([net.group(g.astype(BF)) for g in owned]).astype(F32)
    roots = jnp.stack([net.group(right_roots[n].astype(BF)) for n in range(LAYERS)]).astype(F32)
    columns = lax.dynamic_slice_in_dim(whole, first_row, own_rows, 3)
    new_left = decay_rate * left_stats + (1.0 - decay_rate) * jnp.einsum(
        "lbrk,lbck->lbrc", grads, whole, precision=highest
    )
    new_right = decay_rate * right_stats + (1.0 - decay_rate) * jnp.einsum(
        "lbkr,lbkc->lbrc", columns, whole, precision=highest
    )
    mixed = jnp.einsum("lbrk,lbkc->lbrc", whole, roots, precision=highest)
    update = jnp.einsum("lbrk,lbkc->lbrc", left_roots, mixed, precision=highest)
    new_masters = masters - matrix_rate * update
    return grads, new_left, new_right, new_masters, new_masters.astype(BF)


def update_small_kernel(sums_ref, moments_ref, params_ref, grads_out, moments_out, params_out):
    count = moments_ref.shape[1] // 128
    for layer in range(LAYERS):
        for n in range(count):
            at, cols = layer * count + n, slice(128 * n, 128 * (n + 1))
            grads_out[layer : layer + 1, cols] = sums_ref[at : at + 1, :]
    grads = grads_out[...]
    moments = decay_rate * moments_ref[...] + (1.0 - decay_rate) * grads * grads
    moments_out[...] = moments
    params_out[...] = params_ref[...] - small_rate * grads / (jnp.sqrt(moments) + moment_epsilon)


def update_small(sums, moments, params):
    return launch(
        update_small_kernel,
        "update_small",
        [(a, VMEM) for a in (sums, moments, params)],
        [shape(moments.shape, F32)] * 3,
        [VMEM] * 3,
    )


def run_any(net, dims, small, lengths, x, cot, low):
    pos = net.position()
    weights = [net.gather(low[n]) for n in range(LAYERS)]
    last = LAYERS - 1
    saved = []
    for n in range(LAYERS):
        qkv, lse, ctx, unit, inv = attention_forward(dims, weights[n], pos, lengths, x, small[n])
        saved.append([x, qkv, lse, ctx, unit, inv])
        if n < last:
            *rest, x = ffn_forward(dims, weights[n], pos, unit, small[n])
            saved[n] += rest
    owned = [None] * LAYERS
    for n in reversed(range(LAYERS)):
        x, qkv, lse, ctx, unit, inv, *rest = saved[n]
        if n == last:
            y, gz1, gctx, sums_a, early = ffn_both(
                dims, weights[n], net.early, pos, lengths, cot, small[n], unit, inv, ctx
            )
        else:
            act, slope, unit2, inv2 = rest
            gz1, gctx, sums_a, early = ffn_backward(
                dims, weights[n], net.early, pos, gy, small[n], unit, inv, ctx, unit2, inv2, act, slope
            )
        sums = [sums_a] if n == last else [sums_a, sums]
        gy, sums, late = attention_backward(
            dims, weights[n], net.late, pos, lengths, gz1, gctx, qkv, lse, x, sums
        )
        owned[n] = net.reduce(early, late)
    return y, gy, owned, net.small_sum(sums)


def run_small(net, dims, small, lengths, x, cot, left_stats, right_stats, left_roots, right_roots, masters):
    pos = net.position()
    own, every = tuple(range(dims.own)), tuple(range(Z_SLABS))
    third = dims.own // 3

    low_zs, high_zs = every[: Z_SLABS // 2], every[Z_SLABS // 2 :]
    third = dims.own // 3
    whole_a = net.whole_column(masters[0, :third].astype(BF))
    whole_b = net.whole_column(masters[0, third:].astype(BF))
    whole1 = net.whole_column(masters[1].astype(BF))
    lot = net.whole_lot(whole_a, every, own[:third])
    both = net.joined(lot, net.first_swap(lot), every)
    got = net.second_swap(lot, both)
    weights0 = net.core_swap(lot, every, both, got)
    lot = net.whole_lot(whole_b, every, own[third:], both)
    both = net.joined(lot, net.first_swap(lot), every, got)
    got = net.second_swap(lot, both)
    lot_b = net.whole_lot(whole1, every, own, both)
    weights0 += net.core_swap(lot, every, both, net.gate(got, [a for _, a in lot_b]))

    lot = lot_b
    got = net.first_swap(lot)
    qkv0, lse0, ctx0, unit0, inv0 = attention_forward(
        dims, weights0, pos, lengths, x, small[0], [a for _, a in lot]
    )
    both = net.joined(lot, got, low_zs, [inv0])
    both_b = net.joined(lot, got, high_zs, both)
    act0, slope0, unit0b, inv0b, y0 = ffn_forward(dims, weights0, pos, unit0, small[0], both_b)
    got = net.gate(net.second_swap(lot, both), [inv0b])
    weights1 = net.core_swap(lot, low_zs, both, got)
    got = net.second_swap(lot, both_b)
    qkv1, lse1, ctx1, unit1, inv1 = attention_forward(dims, weights1, pos, lengths, y0, small[1])
    got = net.gate(got, [inv1])
    weights1 += net.core_swap(lot, high_zs, both_b, got)

    roots = net.rounded(right_roots.reshape((-1,) + right_roots.shape[2:]), got)
    y1, gz1, gctx, sums, early1 = ffn_both(
        dims, weights1, net.early, pos, lengths, cot, small[1], unit1, inv1, ctx1, [roots]
    )
    roots_y = net.swap(roots, "y")
    net.hold(early1, [roots_y])
    roots = [roots, roots_y, net.swap(roots, "c"), net.swap(roots_y, "c")]

    split = ((0,), (1, 2, 3))
    early1 = net.core_sum(early1)
    gx1, sums1, late1 = attention_backward(
        dims, weights1, net.late, pos, lengths, gz1, gctx, qkv1, lse1, y0, [sums], early1[1]
    )
    got = net.swaps(early1, "yx")
    net.hold(late1, got)
    early1 = net.add(early1[0], got, [gx1])
    late1 = net.core_sum(late1, early1[1])
    got_l, got_e = net.swaps(late1, "yx"), net.swaps(early1, "xy")
    gz0, gctx0, sums, early0 = ffn_backward(
        dims, weights0, net.early, pos, gx1, small[0], unit0, inv0, ctx0, unit0b, inv0b, act0, slope0,
        [*early1[1], *late1[1]],
    )
    net.hold(early0, [*got_l, *got_e])
    late1 = net.add(late1[0], got_l)
    got_l = net.swaps(late1, "xy")
    early0 = net.core_sum(early0, late1[1])
    whole1 = net.collect(split, (late1, early1), (got_l, got_e), early0[1])
    gx0, sums, late0 = attention_backward(
        dims, weights0, net.late, pos, lengths, gz0, gctx0, qkv0, lse0, x, [sums, sums1], [whole1]
    )

    got = net.swaps(early0, "yx")
    net.hold(late0, got)
    early0 = net.add(early0[0], got, [gx0])
    late0 = net.core_sum(late0, early0[1])
    got_l, got_e = net.swaps(late0, "yx"), net.swaps(early0, "xy")
    (sums,) = net.gate([sums], late0[1])
    sums = net.small_sum(sums, ("c",), (1, 2))
    late0 = net.add(late0[0], got_l, [*got_e, sums])
    got_l = net.swaps(late0, "xy")
    whole0 = net.collect(split, (late0, early0), (got_l, got_e))
    low0 = net.column_sum(whole0)
    (low1,) = net.gate([net.column_sum(whole1)], [whole0])
    grads1 = net.group(low1)
    (sums,) = net.gate([sums], [whole0])
    sums = net.small_sum(sums, ("x", "y"), ())

    def update(n, wide, grads, before):
        return update_layer(
            n, pos, wide, left_stats, right_stats, left_roots, masters, grads, roots, before, [whole0]
        )

    done = update(1, low1, grads1, None)
    (low0,) = net.gate([low0], [done[0], sums])
    done = update(0, low0, net.group(low0), done)
    return y1, gx0, done, sums


def local(
    inputs,
    lengths,
    cotangent,
    masters,
    small_params,
    small_moments,
    left_stats,
    right_stats,
    left_roots,
    right_roots,
):
    chains, seq, width = inputs.shape
    rows = chains * seq
    groups, shards = lax.axis_size("grp"), lax.axis_size("fsdp")
    block = masters.shape[3]
    ffn = small_params.shape[1] - 8 * width
    dims = Dims(width, ffn, block, groups * masters.shape[1], rows)
    small = [small_params[n : n + 1] for n in range(LAYERS)]
    x, cot = inputs.reshape(rows, width), cotangent.reshape(rows, width)
    if groups == 2 * Z_SLABS and shards == 4:
        net = SmallSlice(dims)
        y, gx, done, sums = run_small(
            net, dims, small, lengths, x, cot, left_stats, right_stats, left_roots, right_roots, masters
        )
    else:
        net = AnySlice(dims)
        low = [masters[n].astype(BF) for n in range(LAYERS)]
        y, gx, owned, sums = run_any(net, dims, small, lengths, x, cot, low)
        done = update_plain(net, owned, masters, left_stats, right_stats, left_roots, right_roots)
    weight_grads, new_left, new_right, new_masters, new_copies = done
    small_grads, new_moments, new_small = update_small(sums, small_moments, small_params)
    return (
        y.reshape(chains, seq, width),
        gx.reshape(chains, seq, width),
        weight_grads,
        small_grads,
        new_moments,
        new_small,
        new_left,
        new_right,
        new_masters,
        new_copies,
    )


def solution(mesh):
    tokens, blocks = P(("grp", "fsdp"), None, None), P(None, "grp", "fsdp", None)
    return jax.shard_map(
        local,
        mesh=mesh,
        in_specs=(tokens, P(("grp", "fsdp")), tokens, blocks, P(), P(), blocks, blocks, blocks, blocks),
        out_specs=(tokens, tokens, blocks, P(), P(), P(), blocks, blocks, blocks, blocks),
        check_vma=False,
    )
```

```python
import functools

import jax
import jax.numpy as jnp
from jax import lax
from jax.experimental import pallas as pl
from jax.experimental.pallas import tpu as pltpu
from jax.sharding import PartitionSpec as P

HEADS = 12
LAYERS = 2
Z_SLABS = 4
BF = jnp.bfloat16
F32 = jnp.float32

norm_epsilon = 1e-05
matrix_rate = 1.0
small_rate = 0.3
decay_rate = 0.5
moment_epsilon = 1e-08

VMEM = pl.BlockSpec(memory_space=pltpu.VMEM)
SMEM = pl.BlockSpec(memory_space=pltpu.SMEM)
ANY = pl.BlockSpec(memory_space=pl.ANY)


def shape(dims, dtype):
    return jax.ShapeDtypeStruct(tuple(dims), dtype)


def mm(a, b):
    return jnp.dot(a, b, preferred_element_type=F32)


def mm_bt(a, b):
    return lax.dot_general(a, b, (((1,), (1,)), ((), ())), preferred_element_type=F32)


def mm_at(a, b):
    return lax.dot_general(a, b, (((0,), (0,)), ((), ())), preferred_element_type=F32)


class Part:
    def __init__(self, zs, js, order, arrays=None, offsets=(0, 0, 0, 0), strides=None):
        self.zs, self.js, self.order = tuple(zs), tuple(js), order
        self.arrays, self.offsets = arrays, offsets
        many = len(self.zs) * len(self.js)
        self.strides = strides or (2 * many, many, len(self.js), 1)

    def index(self, first, second, z, j):
        of_first, of_second, of_z, of_j = self.strides
        return first * of_first + second * of_second + self.zs.index(z) * of_z + self.js.index(j) * of_j

    def count(self):
        return 4 * len(self.zs) * len(self.js)


def launch(body, name, ins, out_shape, out_specs, deps=(), scratch=(), cost=None, aliases=None, limit=16, weight=0, **grid):
    count, extra = len(ins), len(deps)

    def kernel(*refs):
        body(*refs[:count], *refs[count + extra :])

    flops, moved, special = weight, 0, 0
    return pl.pallas_call(
        kernel,
        in_specs=[spec for _, spec in ins] + [ANY] * extra,
        out_specs=out_specs,
        out_shape=out_shape,
        scratch_shapes=list(scratch),
        input_output_aliases=aliases or {},
        compiler_params=pltpu.CompilerParams(vmem_limit_bytes=limit << 20),
        cost_estimate=pl.CostEstimate(flops=flops, bytes_accessed=moved, transcendentals=special),
        name=name,
        **grid,
    )(*[array for array, _ in ins], *deps)


class Dims:
    def __init__(self, model, ffn, block, blocks, rows):
        self.model, self.ffn, self.block, self.blocks, self.rows = model, ffn, block, blocks, rows
        self.own = blocks // (2 * Z_SLABS)
        self.piece = block // 4
        wide, tall = model // block, ffn // block
        self.places = {}
        at = 0
        for name, rows_, cols_ in (
            ("q", wide, wide),
            ("k", wide, wide),
            ("v", wide, wide),
            ("o", wide, wide),
            ("up", wide, tall),
            ("down", tall, wide),
        ):
            self.places[name] = [
                (at + r * cols_ + c, r * block, c * block) for r in range(rows_) for c in range(cols_)
            ]
            at += rows_ * cols_

    def where(self, b):
        return b // (2 * self.own), (b // self.own) % 2, b % self.own


def find_part(parts, z, j):
    for number, part in enumerate(parts):
        if z in part.zs and j in part.js:
            return number
    raise ValueError("no part")


def needed_parts(dims, parts, names):
    used = set()
    for name in names:
        for b, _, _ in dims.places[name]:
            z, _, j = dims.where(b)
            used.add(find_part(parts, z, j))
    return [parts[n] for n in sorted(used)]


def start_loads(dims, parts, refs, pos, name, dst, row0, col0, sem):
    x, y, c = pos
    by_x = []

    def start(src, row, quarter, col):
        rows = pl.ds(pl.multiple_of(row0 + row + dims.piece * quarter, 16), dims.piece)
        pltpu.make_async_copy(src, dst.at[rows, pl.ds(col0 + col, dims.block)], sem).start()

    for b, row, col in dims.places[name]:
        z, xq, j = dims.where(b)
        number = find_part(parts, z, j)
        if parts[number].order == "xy":
            by_x.append((number, z, xq, j, row, col))
            continue
        for dc in range(2):
            for dy in range(2):
                n = 2 * dc + dy
                src = refs[number][n].at[parts[number].offsets[n] + parts[number].index(0, x ^ xq, z, j)]
                start(src, row, 2 * (y ^ dy) + (c ^ dc), col)
    if by_x:
        for own_x in range(2):

            @pl.when(x == own_x)
            def _(own_x=own_x):
                for number, z, xq, j, row, col in by_x:
                    for dc in range(2):
                        for yq in range(2):
                            n = 2 * dc + (own_x ^ xq)
                            at = parts[number].offsets[n] + parts[number].index(0, y ^ yq, z, j)
                            start(refs[number][n].at[at], row, 2 * yq + (c ^ dc), col)


def wait_for(ref, sem):
    pltpu.make_async_copy(ref, ref, sem).wait()


def start_stores(dims, parts, outs, pos, places, src, sem):
    x, y, c = pos
    for b, row, col in places:
        z, xq, j = dims.where(b)
        number = find_part(parts, z, j)
        for dc in range(2):
            for yq in range(2):
                ends = (x ^ xq, y ^ yq) if parts[number].order == "xy" else (y ^ yq, x ^ xq)
                rows = pl.ds(pl.multiple_of(row + dims.piece * (2 * yq + (c ^ dc)), 16), dims.piece)
                dst = outs[number][dc].at[parts[number].index(*ends, z, j)]
                pltpu.make_async_copy(src.at[rows, pl.ds(col, dims.block)], dst, sem).start()


def norm_forward(values):
    center = values - jnp.mean(values, axis=-1, keepdims=True)
    spread = jnp.mean(center * center, axis=-1, keepdims=True)
    inverse = lax.rsqrt(spread + norm_epsilon)
    return center * inverse, inverse


def norm_backward(gradient, unit, inverse, gain):
    scaled = gradient * gain
    inner = (
        scaled
        - jnp.mean(scaled, axis=-1, keepdims=True)
        - unit * jnp.mean(scaled * unit, axis=-1, keepdims=True)
    )
    return inverse * inner


def col_sum(values):
    return jnp.sum(values.astype(F32), axis=0, keepdims=True)


def put_rows(sums_ref, number, values):
    count = values.shape[1] // 128
    for n in range(count):
        at = number * count + n
        sums_ref[at : at + 1, :] = values[:, 128 * n : 128 * (n + 1)]


def segment(small_ref, number, width):
    return small_ref[0:1, number * width : (number + 1) * width]


def unflatten(refs, parts):
    return [refs[4 * n : 4 * n + 4] for n in range(len(parts))], refs[4 * len(parts) :]


def weight_ins(parts):
    return [(a, ANY) for p in parts for a in p.arrays]


def half_masks(head):
    lane = lax.broadcasted_iota(jnp.int32, (1, 2 * head), 1)
    low = lane < head
    ones = jnp.where(low, 1.0, 0.0).astype(F32)
    return low, (ones.astype(BF), (1.0 - ones).astype(BF))


def project(small_ref, x, ctx, wo):
    attended = mm(ctx, wo) + segment(small_ref, 2, x.shape[1])
    return norm_forward(x.astype(F32) + attended)


def attention_forward_kernel(dims, parts, names, chains, pos_ref, len_ref, x_ref, small_ref, *rest):
    refs, rest = unflatten(rest, parts)
    qkv_ref, lse_ref, ctx_ref, *normed, w, sems = rest
    width, seq = dims.model, dims.rows // chains
    head = width // HEADS
    pos = (pos_ref[1], pos_ref[2], pos_ref[3])
    for n, name in enumerate(names):
        start_loads(dims, parts, refs, pos, name, w, 0, n * width, sems.at[n])
    xb = x_ref[...].astype(BF)
    for n, bias in ((0, 0), (1, None), (2, 1)):
        cols = slice(n * width, (n + 1) * width)
        wait_for(w.at[:, cols], sems.at[n])
        out = mm(xb, w[:, cols])
        if bias is not None:
            out = out + segment(small_ref, bias, width)
        qkv_ref[:, cols] = out.astype(BF)
    low, masks = half_masks(head)
    scale = head**-0.5

    def chain(i, carry):
        rows = pl.ds(pl.multiple_of(i * seq, 16), seq)
        valid = lax.broadcasted_iota(jnp.int32, (seq, seq), 0) < len_ref[i]
        for pair in range(HEADS // 2):
            at = pair * 2 * head
            q = qkv_ref[rows, at : at + 2 * head]
            k = qkv_ref[rows, width + at : width + at + 2 * head]
            v = qkv_ref[rows, 2 * width + at : 2 * width + at + 2 * head]
            outs = []
            for h in range(2):
                s = jnp.where(valid, mm_bt(k, q * masks[h]) * scale, -1000000000.0)
                top = jnp.max(s, axis=0, keepdims=True)
                e = jnp.exp(s - top)
                total = jnp.sum(e, axis=0, keepdims=True)
                lse_ref[i, 2 * pair + h : 2 * pair + h + 1, :] = top + jnp.log(total)
                outs.append(mm_at((e * (1.0 / total)).astype(BF), v))
            ctx_ref[rows, at : at + 2 * head] = jnp.where(low, outs[0], outs[1]).astype(BF)
        return carry

    lax.fori_loop(0, chains, chain, 0)
    if normed:
        wait_for(w.at[:, 3 * width :], sems.at[3])
        unit, inverse = project(small_ref, x_ref[...], ctx_ref[...], w[:, 3 * width :])
        normed[0][...] = unit
        normed[1][...] = inverse


def attention_forward(dims, parts, pos, lengths, x, small, deps=(), projected=True):
    names = ("q", "k", "v", "o") if projected else ("q", "k", "v")
    parts = needed_parts(dims, parts, names)
    chains = lengths.shape[0]
    rows, width = dims.rows, dims.model
    outs = [
        shape((rows, 3 * width), BF),
        shape((chains, HEADS, rows // chains), F32),
        shape((rows, width), BF),
    ]
    if projected:
        outs += [shape((rows, width), F32), shape((rows, 1), F32)]
    return launch(
        functools.partial(attention_forward_kernel, dims, parts, names, chains),
        "attention_forward",
        [(pos, SMEM), (lengths, SMEM), (x, VMEM), (small, VMEM)] + weight_ins(parts),
        outs,
        [VMEM] * len(outs),
        deps,
        [pltpu.VMEM((width, len(names) * width), BF), pltpu.SemaphoreType.DMA((4,))],
        limit=56,
    )


def ffn_forward_body(dims, small_ref, unit_ref, up, down, sems, act_ref, slope_ref):
    width = dims.model
    h1 = unit_ref[...] * segment(small_ref, 4, width) + segment(small_ref, 5, width)
    hb = h1.astype(BF)
    total = h1 + segment(small_ref, 3, width)
    wait_for(up, sems.at[0])
    for n in range(dims.ffn // width):
        cols = slice(n * width, (n + 1) * width)
        u = mm(hb, up[:, cols]) + segment(small_ref, 8 + n, width)
        cdf = 0.5 * (1.0 + lax.erf(u * 0.7071067811865476))
        act = (u * cdf).astype(BF)
        act_ref[:, cols] = act
        slope_ref[:, cols] = (cdf + u * (0.3989422804014327 * jnp.exp(-0.5 * u * u))).astype(BF)
        if n == 0:
            wait_for(down, sems.at[1])
        total = total + mm(act, down[cols, :])
    return total


def ffn_forward_kernel(dims, parts, pos_ref, unit_ref, small_ref, *rest):
    refs, rest = unflatten(rest, parts)
    act_ref, slope_ref, unit2_ref, inv2_ref, y_ref, up, down, sems = rest
    pos = (pos_ref[1], pos_ref[2], pos_ref[3])
    start_loads(dims, parts, refs, pos, "up", up, 0, 0, sems.at[0])
    start_loads(dims, parts, refs, pos, "down", down, 0, 0, sems.at[1])
    width = dims.model
    total = ffn_forward_body(dims, small_ref, unit_ref, up, down, sems, act_ref, slope_ref)
    unit, inverse = norm_forward(total)
    unit2_ref[...] = unit
    inv2_ref[...] = inverse
    y_ref[...] = unit * segment(small_ref, 6, width) + segment(small_ref, 7, width)


def ffn_forward(dims, parts, pos, unit, small, deps=(), weight=0):
    parts = needed_parts(dims, parts, ("up", "down"))
    rows, width, ffn = dims.rows, dims.model, dims.ffn
    return launch(
        functools.partial(ffn_forward_kernel, dims, parts),
        "ffn_forward",
        [(pos, SMEM), (unit, VMEM), (small, VMEM)] + weight_ins(parts),
        [
            shape((rows, ffn), BF),
            shape((rows, ffn), BF),
            shape((rows, width), F32),
            shape((rows, 1), F32),
            shape((rows, width), F32),
        ],
        [VMEM] * 5,
        deps,
        [pltpu.VMEM((width, ffn), BF), pltpu.VMEM((ffn, width), BF), pltpu.SemaphoreType.DMA((2,))],
        (4 * rows * width * ffn, 24 << 20, 3 << 20),
        weight=weight,
        limit=56,
    )


def ffn_backward_body(
    dims, outs_parts, outs, pos, gy, small_ref, unit_ref, inv_ref, ctx_ref, unit2, inv2, act_ref, slope_ref,
    up, down, wo, grad_up, grad_down, grad_o, sem_out, gz1_ref, gctx_ref, sums_ref, wait_o,
):
    width = dims.model
    gain1, gain2 = segment(small_ref, 4, width), segment(small_ref, 6, width)

    def put(number, values):
        put_rows(sums_ref, number, values)

    put(6, col_sum(gy * unit2))
    put(7, col_sum(gy))
    gz2 = norm_backward(gy, unit2, inv2, gain2)
    gf = gz2.astype(BF)
    put(3, col_sum(gf))
    hb = (unit_ref[...] * gain1 + segment(small_ref, 5, width)).astype(BF)
    gh1 = gz2
    block = dims.block
    for n in range(dims.ffn // width):
        cols = slice(n * width, (n + 1) * width)
        gu = (slope_ref[:, cols].astype(F32) * mm_bt(gf, down[cols, :])).astype(BF)
        put(8 + n, col_sum(gu))
        grad_up[:, cols] = mm_at(hb, gu).astype(BF)
        grad_down[cols, :] = mm_at(act_ref[:, cols], gf).astype(BF)
        low, high = n * width, (n + 1) * width
        start_stores(
            dims, outs_parts, outs, pos,
            [p for p in dims.places["up"] if low <= p[2] < high], grad_up, sem_out.at[0],
        )
        start_stores(
            dims, outs_parts, outs, pos,
            [p for p in dims.places["down"] if low <= p[1] < high], grad_down, sem_out.at[1],
        )
        gh1 = gh1 + mm_bt(gu, up[:, cols])
    unit = unit_ref[...]
    put(4, col_sum(gh1 * unit))
    put(5, col_sum(gh1))
    gz1 = norm_backward(gh1, unit, inv_ref[...], gain1)
    gz1_ref[...] = gz1
    ga = gz1.astype(BF)
    put(2, col_sum(ga))
    grad_o[...] = mm_at(ctx_ref[...], ga).astype(BF)
    start_stores(dims, outs_parts, outs, pos, dims.places["o"], grad_o, sem_out.at[2])
    wait_o()
    gctx_ref[...] = mm_bt(ga, wo[...]).astype(BF)
    put(0, jnp.zeros((1, width), F32))
    put(1, jnp.zeros((1, width), F32))
    wait_for(grad_up, sem_out.at[0])
    wait_for(grad_down, sem_out.at[1])
    wait_for(grad_o, sem_out.at[2])


def grad_shapes(dims, parts):
    return [shape((p.count(), dims.piece, dims.block), BF) for p in parts for _ in range(2)]


def pair_up(arrays, parts):
    return [Part(p.zs, p.js, p.order, list(arrays[2 * n : 2 * n + 2])) for n, p in enumerate(parts)]


def ffn_scratch(dims):
    width, ffn = dims.model, dims.ffn
    matrices = [(width, ffn), (ffn, width), (width, width)] * 2
    return [pltpu.VMEM(m, BF) for m in matrices] + [pltpu.SemaphoreType.DMA((3,))] * 2


def ffn_backward_kernel(dims, parts, outs_parts, pos_ref, gy_ref, small_ref, unit_ref, inv_ref, ctx_ref, unit2_ref, inv2_ref, act_ref, slope_ref, *rest):
    refs, rest = unflatten(rest, parts)
    gz1_ref, gctx_ref, sums_ref, *rest = rest
    count = 2 * len(outs_parts)
    outs = [rest[2 * n : 2 * n + 2] for n in range(len(outs_parts))]
    up, down, wo, grad_up, grad_down, grad_o, sems, sem_out = rest[count:]
    pos = (pos_ref[1], pos_ref[2], pos_ref[3])
    start_loads(dims, parts, refs, pos, "down", down, 0, 0, sems.at[1])
    start_loads(dims, parts, refs, pos, "up", up, 0, 0, sems.at[0])
    start_loads(dims, parts, refs, pos, "o", wo, 0, 0, sems.at[2])
    wait_for(down, sems.at[1])
    wait_for(up, sems.at[0])
    ffn_backward_body(
        dims, outs_parts, outs, pos, gy_ref[...], small_ref, unit_ref, inv_ref, ctx_ref,
        unit2_ref[...], inv2_ref[...], act_ref, slope_ref, up, down, wo, grad_up, grad_down, grad_o,
        sem_out, gz1_ref, gctx_ref, sums_ref, lambda: wait_for(wo, sems.at[2]),
    )


def ffn_backward(dims, parts, outs_parts, pos, gy, small, unit, inv, ctx, unit2, inv2, act, slope, deps=()):
    parts = needed_parts(dims, parts, ("up", "down", "o"))
    rows, width, ffn = dims.rows, dims.model, dims.ffn
    grads = grad_shapes(dims, outs_parts)
    out = launch(
        functools.partial(ffn_backward_kernel, dims, parts, outs_parts),
        "ffn_backward",
        [(pos, SMEM)]
        + [(a, VMEM) for a in (gy, small, unit, inv, ctx, unit2, inv2, act, slope)]
        + weight_ins(parts),
        [shape((rows, width), F32), shape((rows, width), BF), shape((small.shape[1] // 128, 128), F32)] + grads,
        [VMEM] * 3 + [ANY] * len(grads),
        deps,
        ffn_scratch(dims),
        (8 * rows * width * ffn + 4 * rows * width * width, 40 << 20, 0),
        limit=56,
    )
    return out[0], out[1], out[2], pair_up(out[3:], outs_parts)


def ffn_both_kernel(dims, parts, outs_parts, chains, pos_ref, len_ref, cot_ref, small_ref, x_ref, ctx_ref, *rest):
    refs, rest = unflatten(rest, parts)
    y_ref, gz1_ref, gctx_ref, sums_ref, *rest = rest
    count = 2 * len(outs_parts)
    outs = [rest[2 * n : 2 * n + 2] for n in range(len(outs_parts))]
    up, down, wo, grad_up, grad_down, grad_o, sems, sem_out, act_ref, slope_ref, unit_ref, inv_ref = rest[count:]
    pos = (pos_ref[1], pos_ref[2], pos_ref[3])
    start_loads(dims, parts, refs, pos, "o", wo, 0, 0, sems.at[2])
    start_loads(dims, parts, refs, pos, "up", up, 0, 0, sems.at[0])
    start_loads(dims, parts, refs, pos, "down", down, 0, 0, sems.at[1])
    width, seq = dims.model, dims.rows // chains
    wait_for(wo, sems.at[2])
    unit, inverse = project(small_ref, x_ref[...], ctx_ref[...], wo[...])
    unit_ref[...] = unit
    inv_ref[...] = inverse
    total = ffn_forward_body(dims, small_ref, unit_ref, up, down, sems, act_ref, slope_ref)
    unit2, inv2 = norm_forward(total)
    y_ref[...] = (unit2 * segment(small_ref, 6, width) + segment(small_ref, 7, width)).astype(BF)
    place = lax.broadcasted_iota(jnp.int32, (seq, width), 0)
    gy = jnp.concatenate(
        [
            jnp.where(place < len_ref[i], cot_ref[i * seq : (i + 1) * seq, :].astype(F32), 0.0)
            for i in range(chains)
        ],
        axis=0,
    )
    ffn_backward_body(
        dims, outs_parts, outs, pos, gy, small_ref, unit_ref, inv_ref, ctx_ref,
        unit2, inv2, act_ref, slope_ref, up, down, wo, grad_up, grad_down, grad_o,
        sem_out, gz1_ref, gctx_ref, sums_ref, lambda: None,
    )


def ffn_both(dims, parts, outs_parts, pos, lengths, cot, small, x, ctx, deps=()):
    parts = needed_parts(dims, parts, ("up", "down", "o"))
    rows, width, ffn = dims.rows, dims.model, dims.ffn
    grads = grad_shapes(dims, outs_parts)
    out = launch(
        functools.partial(ffn_both_kernel, dims, parts, outs_parts, lengths.shape[0]),
        "ffn_both",
        [(pos, SMEM), (lengths, SMEM)]
        + [(a, VMEM) for a in (cot, small, x, ctx)]
        + weight_ins(parts),
        [
            shape((rows, width), BF),
            shape((rows, width), F32),
            shape((rows, width), BF),
            shape((small.shape[1] // 128, 128), F32),
        ]
        + grads,
        [VMEM] * 4 + [ANY] * len(grads),
        deps,
        ffn_scratch(dims)
        + [pltpu.VMEM((rows, ffn), BF)] * 2
        + [pltpu.VMEM((rows, width), F32), pltpu.VMEM((rows, 1), F32)],
        (12 * rows * width * ffn + 4 * rows * width * width, 40 << 20, 3 << 20),
        limit=56,
    )
    return out[0], out[1], out[2], out[3], pair_up(out[4:], outs_parts)


def attention_backward_kernel(dims, parts, outs_parts, chains, given, pos_ref, len_ref, gz1_ref, gctx_ref, qkv_ref, lse_ref, x_ref, *rest):
    given_refs, rest = rest[:given], rest[given:]
    refs, rest = unflatten(rest, parts)
    gx_ref, sums_ref, *rest = rest
    count = 2 * len(outs_parts)
    outs = [rest[2 * n : 2 * n + 2] for n in range(len(outs_parts))]
    w, grads_ref, grad_w, sems, sem_out = rest[count:]
    pos = (pos_ref[1], pos_ref[2], pos_ref[3])
    width, seq = dims.model, dims.rows // chains
    head = width // HEADS
    names = ("q", "k", "v")
    for n, name in enumerate(names):
        start_loads(dims, parts, refs, pos, name, w, 0, n * width, sems.at[n])
    low, masks = half_masks(head)
    scale = head**-0.5

    def chain(i, carry):
        rows = pl.ds(pl.multiple_of(i * seq, 16), seq)
        valid = lax.broadcasted_iota(jnp.int32, (seq, seq), 0) < len_ref[i]
        for pair in range(HEADS // 2):
            at = pair * 2 * head
            q = qkv_ref[rows, at : at + 2 * head]
            k = qkv_ref[rows, width + at : width + at + 2 * head]
            v = qkv_ref[rows, 2 * width + at : 2 * width + at + 2 * head]
            g = gctx_ref[rows, at : at + 2 * head]
            gq, gk, gv = [], [], []
            for h in range(2):
                s = jnp.where(valid, mm_bt(k, q * masks[h]) * scale, -1000000000.0)
                p = jnp.exp(s - lse_ref[i, 2 * pair + h : 2 * pair + h + 1, :])
                gp = mm_bt(v, g * masks[h])
                inner = jnp.sum(p * gp, axis=0, keepdims=True)
                gs = (p * (gp - inner)).astype(BF)
                gv.append(mm(p.astype(BF), g))
                gk.append(mm(gs, q))
                gq.append(mm_at(gs, k))
            grads_ref[rows, at : at + 2 * head] = (jnp.where(low, gq[0], gq[1]) * scale).astype(BF)
            grads_ref[rows, width + at : width + at + 2 * head] = (
                jnp.where(low, gk[0], gk[1]) * scale
            ).astype(BF)
            grads_ref[rows, 2 * width + at : 2 * width + at + 2 * head] = jnp.where(
                low, gv[0], gv[1]
            ).astype(BF)
        return carry

    lax.fori_loop(0, chains, chain, 0)
    xb = x_ref[...].astype(BF)
    for n, name in enumerate(names):
        cols = slice(n * width, (n + 1) * width)
        grad_w[:, cols] = mm_at(xb, grads_ref[:, cols]).astype(BF)
        places = [(b, r, c + n * width) for b, r, c in dims.places[name]]
        start_stores(dims, outs_parts, outs, pos, places, grad_w, sem_out)
    at = 0
    for ref in given_refs:
        sums_ref[at : at + ref.shape[0], :] = ref[...]
        at += ref.shape[0]
    put_rows(sums_ref, 0, col_sum(grads_ref[:, :width]))
    put_rows(sums_ref, 1, col_sum(grads_ref[:, 2 * width :]))
    gx = gz1_ref[...]
    for n in range(3):
        cols = slice(n * width, (n + 1) * width)
        wait_for(w.at[:, cols], sems.at[n])
        gx = gx + mm_bt(grads_ref[:, cols], w[:, cols])
    gx_ref[...] = gx
    wait_for(grad_w, sem_out)


def attention_backward(dims, parts, outs_parts, pos, lengths, gz1, gctx, qkv, lse, x, sums, deps=()):
    parts = needed_parts(dims, parts, ("q", "k", "v"))
    rows, width = dims.rows, dims.model
    grads = grad_shapes(dims, outs_parts)
    out = launch(
        functools.partial(attention_backward_kernel, dims, parts, outs_parts, lengths.shape[0], len(sums)),
        "attention_backward",
        [(pos, SMEM), (lengths, SMEM)] + [(a, VMEM) for a in (gz1, gctx, qkv, lse, x, *sums)] + weight_ins(parts),
        [shape((rows, width), F32), shape((sum(a.shape[0] for a in sums), 128), F32)] + grads,
        [VMEM] * 2 + [ANY] * len(grads),
        deps,
        [
            pltpu.VMEM((width, 3 * width), BF),
            pltpu.VMEM((rows, 3 * width), BF),
            pltpu.VMEM((width, 3 * width), BF),
            pltpu.SemaphoreType.DMA((3,)),
            pltpu.SemaphoreType.DMA,
        ],
        (24 * rows * width * width, 24 << 20, 1 << 20),
        limit=56,
    )
    return out[0], out[1], pair_up(out[2:], outs_parts)


class AnySlice:
    def __init__(self, dims):
        self.dims = dims
        own = range(dims.own)
        self.early = [Part((1, 2, 3), own, "yx")]
        self.late = [Part((0,), own, "yx")]

    def position(self):
        return jnp.zeros((4,), jnp.int32)

    def gather(self, low):
        dims = self.dims
        whole = lax.all_gather(low, "fsdp", axis=1, tiled=True)
        whole = lax.all_gather(whole, "grp", axis=0, tiled=True)
        split = whole.reshape(Z_SLABS, 2, dims.own, 2, 2, dims.piece, dims.block)
        order = split.transpose(4, 3, 1, 0, 2, 5, 6).reshape(4, -1, dims.piece, dims.block)
        return [Part(range(Z_SLABS), range(dims.own), "yx", [order[n] for n in range(4)])]

    def reduce(self, early, late):
        dims = self.dims
        pieces = []
        for part in (late[0], early[0]):
            stacked = jnp.stack(part.arrays)
            split = stacked.reshape(2, 2, 2, len(part.zs), dims.own, dims.piece, dims.block)
            pieces.append(split.transpose(3, 2, 4, 1, 0, 5, 6))
        whole = jnp.concatenate(pieces, axis=0).reshape(dims.blocks, dims.block, dims.block)
        rows = lax.psum_scatter(whole, "fsdp", scatter_dimension=1, tiled=True)
        return lax.psum_scatter(rows, "grp", scatter_dimension=0, tiled=True).astype(F32)

    def small_sum(self, values):
        return lax.psum(values, ("grp", "fsdp"))

    def group(self, owned):
        return lax.all_gather(owned, "fsdp", axis=1, tiled=True)


def swap_of(axis):
    def move(z, x, y, c):
        return (z, x ^ (axis == "x"), y ^ (axis == "y"), c ^ (axis == "c"))

    return move


def join_kernel(ranges, *refs):
    pairs = len(ranges)
    ins, outs, hold, sems = refs[: 2 * pairs], refs[2 * pairs : 3 * pairs + 1], refs[-3], refs[-2:]
    runs, at = [], 0
    for n, (low, count) in enumerate(ranges):
        runs.append(hold.at[pl.ds(at, 2 * count)])
        for half in range(2):
            src = ins[2 * n + half].at[pl.ds(low, count)]
            pltpu.make_async_copy(src, hold.at[pl.ds(at + half * count, count)], sems[0].at[n]).start()
        at += 2 * count
    for n in range(pairs):
        wait_for(runs[n], sems[0].at[n])
        pltpu.make_async_copy(runs[n], outs[n], sems[1].at[n]).start()
    pltpu.make_async_copy(hold, outs[pairs], sems[1].at[pairs]).start()
    for n in range(pairs):
        wait_for(runs[n], sems[1].at[n])
    wait_for(hold, sems[1].at[pairs])


def stack_kernel(*refs):
    *ins, out, sem = refs
    count = ins[0].shape[0]
    for n, ref in enumerate(ins):
        pltpu.make_async_copy(ref, out.at[pl.ds(n * count, count)], sem).start()
    wait_for(out, sem)


def round_kernel(src_ref, dst_ref):
    dst_ref[...] = src_ref[...].astype(BF)


def add_kernel(a_ref, b_ref, first_ref, second_ref):
    half = first_ref.shape[0]

    def piece(i, carry):
        for out, at in ((first_ref, i), (second_ref, i + half)):
            out[i] = (a_ref[at].astype(F32) + b_ref[at].astype(F32)).astype(BF)
        return carry

    lax.fori_loop(0, half, piece, 0)


def collect_kernel(zs, *refs):
    pairs = len(zs)
    ins, out, total, holds, sems = refs[: 2 * pairs], refs[2 * pairs], refs[2 * pairs + 1], refs[2 * pairs + 2 : -1], refs[-1]
    for n in range(2 * pairs):
        pltpu.make_async_copy(ins[n], holds[n], sems.at[n]).start()
    half = holds[0].shape[0] // len(zs[0])
    copies = []
    for n, z_list in enumerate(zs):
        wait_for(holds[2 * n], sems.at[2 * n])
        wait_for(holds[2 * n + 1], sems.at[2 * n + 1])
        for place, want in enumerate(z_list):
            piece, at = pl.ds(place * half, half), pl.ds((2 * want + n % 2) * half, half)
            value = holds[2 * n][piece].astype(F32) + holds[2 * n + 1][piece].astype(F32)
            total[at] = value.astype(BF)
            copies.append(pltpu.make_async_copy(total.at[at], out.at[at], sems.at[2 * pairs]))
            copies[-1].start()
    wait_for(total, sems.at[2 * pairs])


def pick_kernel(places, src_ref, *refs):
    outs, holds, sems = refs[: len(places)], refs[len(places) : -2], refs[-2:]
    for n, runs in enumerate(places):
        at = 0
        for low, count in runs:
            dst = holds[n].at[pl.ds(at, count)]
            pltpu.make_async_copy(src_ref.at[pl.ds(low, count)], dst, sems[0].at[n]).start()
            at += count
    for n in range(len(places)):
        wait_for(holds[n], sems[0].at[n])
        pltpu.make_async_copy(holds[n], outs[n], sems[1].at[n]).start()
    for n in range(len(places)):
        wait_for(holds[n], sems[1].at[n])


def pass_kernel(*refs):
    pass


class SmallSlice:
    def __init__(self, dims):
        self.dims = dims
        a, b = range(dims.own // 2), range(dims.own // 2, dims.own)
        self.early = [Part((1, 2, 3), a, "yx"), Part((1, 2, 3), b, "xy")]
        self.late = [Part((0,), a, "yx"), Part((0,), b, "xy")]
        group, shard = lax.axis_index("grp"), lax.axis_index("fsdp")
        self.z, self.x, self.y, self.c = group // 2, group % 2, shard // 2, shard % 2
        self.pos = jnp.stack([self.z, self.x, self.y, self.c]).astype(jnp.int32)

    def position(self):
        return self.pos

    def pieces(self, count):
        return shape((count, self.dims.piece, self.dims.block), BF)

    def permute(self, array, move):
        pairs = []
        for flat in range(8 * Z_SLABS):
            to = move(flat // 8, flat // 4 % 2, flat // 2 % 2, flat % 2)
            if to is not None:
                pairs.append((flat, ((to[0] * 2 + to[1]) * 2 + to[2]) * 2 + to[3]))
        return lax.ppermute(array, ("grp", "fsdp"), pairs)

    def swap(self, array, axis):
        return self.permute(array, swap_of(axis))

    def rounded(self, wide, deps=()):
        return launch(round_kernel, "rounded", [(wide, VMEM)], shape(wide.shape, BF), VMEM, deps)

    def columns(self):
        return [[2 * z + x for z in range(Z_SLABS)] for x in range(2)]

    def whole_column(self, own):
        return lax.all_gather(own, "grp", axis_index_groups=self.columns(), axis=0, tiled=True)

    def whole_lot(self, whole, zs, js, deps=()):
        half, count = len(js) // 2, len(js)
        places = [[(z * count + low, half) for z in zs] for low in (0, half)]
        sizes = [self.pieces(len(zs) * half)] * 2
        arrays = launch(
            functools.partial(pick_kernel, places),
            "pick",
            [(whole, ANY)],
            sizes,
            [ANY] * 2,
            deps,
            [pltpu.VMEM(s.shape, BF) for s in sizes] + [pltpu.SemaphoreType.DMA((2,))] * 2,
            limit=60,
        )
        halves = ((js[:half], "yx"), (js[half:], "xy"))
        return [(Part(zs, j, order), a) for (j, order), a in zip(halves, arrays)]

    def gate(self, arrays, deps):
        return launch(
            pass_kernel,
            "gate",
            [(a, ANY) for a in arrays],
            [shape(a.shape, a.dtype) for a in arrays],
            [ANY] * len(arrays),
            deps,
            aliases={n: n for n in range(len(arrays))},
            limit=60,
        )

    def hold(self, parts, deps):
        for part, array in zip(parts, self.gate([p.arrays[1] for p in parts], deps)):
            part.arrays[1] = array

    def first_swap(self, lot):
        return [self.swap(a, part.order[1]) for part, a in lot]

    def joined(self, lot, got, zs, deps=()):
        ins, ranges, sizes = [], [], []
        for (part, own), g in zip(lot, got):
            count = own.shape[0] // len(part.zs)
            ranges.append((part.zs.index(zs[0]) * count, len(zs) * count))
            sizes.append(self.pieces(2 * len(zs) * count))
            ins += [own, g]
        return launch(
            functools.partial(join_kernel, ranges),
            "join",
            [(a, ANY) for a in ins],
            sizes + [self.pieces(sum(a.shape[0] for a in sizes))],
            [ANY] * (len(lot) + 1),
            deps,
            [pltpu.VMEM((sum(a.shape[0] for a in sizes),) + sizes[0].shape[1:], BF)]
            + [pltpu.SemaphoreType.DMA((2,)), pltpu.SemaphoreType.DMA((3,))],
            limit=60,
        )

    def second_swap(self, lot, both):
        return [self.swap(b, part.order[0]) for (part, _), b in zip(lot, both)]

    def plane(self, own, js, deps):
        got = [self.swap(own, "x"), self.swap(own, "y")]
        got.append(self.permute(own, lambda z, x, y, c: (z, 1 - x, 1 - y, c)))
        count = own.shape[0]
        whole = launch(
            stack_kernel,
            "stack",
            [(a, ANY) for a in [own, *got]],
            self.pieces(4 * count),
            VMEM,
            deps,
            [pltpu.SemaphoreType.DMA],
        )
        part = Part(range(Z_SLABS), js, "yx", None, (0, 2 * count) * 2, (2 * count, count, 4 * count, 1))
        return part, whole

    def core_swap(self, lot, zs, both, got):
        others = self.swap(both[-1], "c")
        parts, at = [], 0
        for (part, _), b, g in zip(lot, both, got):
            parts.append(Part(zs, part.js, part.order, [b, g, others, self.swap(g, "c")], (0, 0, at, 0)))
            at += b.shape[0]
        return parts

    def add(self, keep, got, deps=(), weight=0):
        sums = []
        for own, other in zip(keep, got):
            out = [self.pieces(own.shape[0] // 2)] * 2
            sums.append(launch(add_kernel, "add", [(own, VMEM), (other, VMEM)], out, [VMEM] * 2, deps, weight=weight))
        return [kept for kept, _ in sums], [sent for _, sent in sums]

    def core_sum(self, parts, deps=(), weight=0):
        got = [self.swap(p.arrays[1], "c") for p in parts]
        return self.add([p.arrays[0] for p in parts], got, deps, weight)

    def swaps(self, sums, axes):
        return [self.swap(a, axis) for a, axis in zip(sums[1], axes)]

    def collect(self, zs, sums, got, deps=(), weight=0):
        ins = []
        for (kept, _), others in zip(sums, got):
            for own, other in zip(kept, others):
                ins += [own, other]
        return launch(
            functools.partial(collect_kernel, [z for z in zs for _ in range(2)]),
            "collect",
            [(a, ANY) for a in ins],
            self.pieces(Z_SLABS * self.dims.own),
            ANY,
            deps,
            [pltpu.VMEM((Z_SLABS * self.dims.own,) + ins[0].shape[1:], BF)]
            + [pltpu.VMEM(a.shape, BF) for a in ins]
            + [pltpu.SemaphoreType.DMA((len(ins) + 1,))],
            weight=weight,
            limit=60,
        )

    def column_sum(self, whole):
        return lax.psum_scatter(
            whole, "grp", axis_index_groups=self.columns(), scatter_dimension=0, tiled=True
        )

    def small_sum(self, values, axes, bits):
        for axis in axes:
            values = values + self.swap(values, axis)
        for bit in bits:
            values = values + self.permute(values, lambda z, x, y, c, bit=bit: (z ^ bit, x, y, c))
        return values

    def group(self, own, deps=()):
        (other,) = self.gate([self.swap(own, "y")], deps)
        return [own, other, self.swap(own, "c"), self.swap(other, "c")]


def update_kernel(layer, first, count_grads, pos_ref, own_ref, *rest):
    stats, grads, rest = rest[:4], rest[4 : 4 + count_grads], rest[4 + count_grads :]
    roots, rest = rest[:4], rest[4:]
    if not first:
        rest = rest[5:]
    outs, rest = rest[:5], rest[5:]
    g_ref, r_ref, turned, own, held, fresh, low_ref, sem_g, sem_r, sem_in, sem_out = rest
    y, c = pos_ref[2], pos_ref[3]
    count, piece, block = own_ref.shape

    def quarter(yq, cq):
        return pl.ds(pl.multiple_of(piece * (2 * yq + cq), 16), piece)

    for n in range(count_grads):
        rows = quarter(y ^ (n % 2), c ^ (n // 2)) if count_grads == 4 else pl.ds(0, block)
        if count_grads == 4:
            pltpu.make_async_copy(grads[n], g_ref.at[:, rows, :], sem_g).start()
    if count_grads == 1:
        for n in range(4):
            mine = grads[0].at[pl.ds(n * count, count)]
            pltpu.make_async_copy(mine, g_ref.at[:, pl.ds(n * piece, piece), :], sem_g).start()
    for n in range(4):
        mine = roots[n].at[pl.ds(layer * count, count)]
        pltpu.make_async_copy(mine, r_ref.at[:, quarter(y ^ (n % 2), c ^ (n // 2)), :], sem_r).start()
    for n in range(4):
        pltpu.make_async_copy(stats[n].at[layer], held.at[n], sem_in.at[n]).start()
    pltpu.make_async_copy(own_ref, own, sem_in.at[4]).start()
    own_rows = quarter(y, c)
    wait_for(g_ref, sem_g)
    def halves(value):
        high = value.astype(BF)
        return [high, (value - high.astype(F32)).astype(BF)]

    for b in range(count):
        g = g_ref[b]
        turned[...] = g.T
        if b == 0:
            wait_for(held.at[0], sem_in.at[0])
        fresh[1, b] = decay_rate * held[0, b] + (1.0 - decay_rate) * mm_bt(g_ref[b, own_rows, :], g)
        if b == 0:
            wait_for(held.at[1], sem_in.at[1])
            wait_for(held.at[2], sem_in.at[2])
        products = mm(jnp.concatenate([turned[own_rows, :], *halves(held[2, b])], axis=0), g)
        fresh[2, b] = decay_rate * held[1, b] + (1.0 - decay_rate) * products[:piece]
        if b == 0:
            wait_for(r_ref, sem_r)
        mixed = products[piece : 2 * piece] + products[2 * piece :]
        products = mm(jnp.concatenate(halves(mixed), axis=0), r_ref[b])
        update = products[:piece] + products[piece:]
        if b == 0:
            wait_for(held.at[3], sem_in.at[3])
            wait_for(own, sem_in.at[4])
        master = held[3, b] - matrix_rate * update
        fresh[3, b] = master
        low_ref[b] = master.astype(BF)
        fresh[0, b] = own[b].astype(F32)
        for n in range(4):
            pltpu.make_async_copy(fresh.at[n, b], outs[n].at[layer, b], sem_out.at[0]).start()
        pltpu.make_async_copy(low_ref.at[b], outs[4].at[layer, b], sem_out.at[1]).start()
    wait_for(fresh, sem_out.at[0])
    wait_for(low_ref, sem_out.at[1])


def update_layer(layer, pos, own, left, right, left_roots, masters, grads, roots, before, deps=()):
    count, piece, block = own.shape
    whole = (LAYERS, count, piece, block)
    ins = [(pos, SMEM), (own, ANY)] + [(a, ANY) for a in (left, right, left_roots, masters)]
    ins += [(a, ANY) for a in grads] + [(a, ANY) for a in roots]
    aliases = {}
    if before is not None:
        aliases = {len(ins) + n: n for n in range(5)}
        ins += [(a, ANY) for a in before]
    return launch(
        functools.partial(update_kernel, layer, before is None, len(grads)),
        "update_layer",
        ins,
        [shape(whole, F32)] * 4 + [shape(whole, BF)],
        [ANY] * 5,
        deps,
        [
            pltpu.VMEM((count, block, block), BF),
            pltpu.VMEM((count, block, block), BF),
            pltpu.VMEM((block, block), BF),
            pltpu.VMEM(own.shape, own.dtype),
            pltpu.VMEM((4,) + own.shape, F32),
            pltpu.VMEM((4,) + own.shape, F32),
            pltpu.VMEM(own.shape, BF),
            pltpu.SemaphoreType.DMA,
            pltpu.SemaphoreType.DMA,
            pltpu.SemaphoreType.DMA((5,)),
            pltpu.SemaphoreType.DMA((2,)),
        ],
        (0, 0, 0),
        aliases,
        limit=56,
    )


def update_plain(net, owned, masters, left_stats, right_stats, left_roots, right_roots):
    own_rows = masters.shape[2]
    first_row = lax.axis_index("fsdp") * own_rows
    highest = lax.Precision.HIGHEST
    grads = jnp.stack(owned)
    whole = jnp.stack([net.group(g.astype(BF)) for g in owned]).astype(F32)
    roots = jnp.stack([net.group(right_roots[n].astype(BF)) for n in range(LAYERS)]).astype(F32)
    columns = lax.dynamic_slice_in_dim(whole, first_row, own_rows, 3)
    new_left = decay_rate * left_stats + (1.0 - decay_rate) * jnp.einsum(
        "lbrk,lbck->lbrc", grads, whole, precision=highest
    )
    new_right = decay_rate * right_stats + (1.0 - decay_rate) * jnp.einsum(
        "lbkr,lbkc->lbrc", columns, whole, precision=highest
    )
    mixed = jnp.einsum("lbrk,lbkc->lbrc", whole, roots, precision=highest)
    update = jnp.einsum("lbrk,lbkc->lbrc", left_roots, mixed, precision=highest)
    new_masters = masters - matrix_rate * update
    return grads, new_left, new_right, new_masters, new_masters.astype(BF)


def update_small_kernel(sums_ref, moments_ref, params_ref, grads_out, moments_out, params_out):
    count = moments_ref.shape[1] // 128
    for layer in range(LAYERS):
        for n in range(count):
            at, cols = layer * count + n, slice(128 * n, 128 * (n + 1))
            grads_out[layer : layer + 1, cols] = sums_ref[at : at + 1, :]
    grads = grads_out[...]
    moments = decay_rate * moments_ref[...] + (1.0 - decay_rate) * grads * grads
    moments_out[...] = moments
    params_out[...] = params_ref[...] - small_rate * grads / (jnp.sqrt(moments) + moment_epsilon)


def update_small(sums, moments, params):
    return launch(
        update_small_kernel,
        "update_small",
        [(a, VMEM) for a in (sums, moments, params)],
        [shape(moments.shape, F32)] * 3,
        [VMEM] * 3,
    )


def run_any(net, dims, small, lengths, x, cot, low):
    pos = net.position()
    weights = [net.gather(low[n]) for n in range(LAYERS)]
    last = LAYERS - 1
    saved = []
    for n in range(LAYERS):
        qkv, lse, ctx, *normed = attention_forward(
            dims, weights[n], pos, lengths, x, small[n], projected=n < last
        )
        saved.append([x, qkv, lse, ctx, *normed])
        if n < last:
            *rest, x = ffn_forward(dims, weights[n], pos, normed[0], small[n])
            saved[n] += rest
    owned = [None] * LAYERS
    for n in reversed(range(LAYERS)):
        x, qkv, lse, ctx, *rest = saved[n]
        if n == last:
            y, gz1, gctx, sums_a, early = ffn_both(
                dims, weights[n], net.early, pos, lengths, cot, small[n], x, ctx
            )
        else:
            unit, inv, act, slope, unit2, inv2 = rest
            gz1, gctx, sums_a, early = ffn_backward(
                dims, weights[n], net.early, pos, gy, small[n], unit, inv, ctx, unit2, inv2, act, slope
            )
        sums = [sums_a] if n == last else [sums_a, sums]
        gy, sums, late = attention_backward(
            dims, weights[n], net.late, pos, lengths, gz1, gctx, qkv, lse, x, sums
        )
        owned[n] = net.reduce(early, late)
    return y, gy, owned, net.small_sum(sums)


def run_small(net, dims, small, lengths, x, cot, left_stats, right_stats, left_roots, right_roots, masters):
    pos = net.position()
    own, every = tuple(range(dims.own)), tuple(range(Z_SLABS))
    third = dims.own // 3

    low_zs, high_zs = every[:1], every[1:]
    third = dims.own // 3
    whole_a = net.whole_column(masters[0, :third].astype(BF))
    whole_b = net.whole_column(masters[0, third:].astype(BF))
    most = 2 * third
    whole1 = net.whole_column(masters[1, :most].astype(BF))
    part1, plane1 = net.plane(masters[1, most:].astype(BF), own[most:], [whole_a])
    lot = net.whole_lot(whole_a, every, own[:third], [plane1])
    plane1 = net.whole_column(plane1)
    both = net.joined(lot, net.first_swap(lot), every)
    got = net.second_swap(lot, both)
    weights0 = net.core_swap(lot, every, both, got)
    lot = net.whole_lot(whole_b, every, own[third:], both)
    both = net.joined(lot, net.first_swap(lot), every, got)
    got = net.second_swap(lot, both)
    lot_b = net.whole_lot(whole1, every, own[:most], both)
    weights0 += net.core_swap(lot, every, both, net.gate(got, [a for _, a in lot_b]))

    lot = lot_b
    got = net.first_swap(lot)
    qkv0, lse0, ctx0, unit0, inv0 = attention_forward(
        dims, weights0, pos, lengths, x, small[0], [a for _, a in lot]
    )
    both = net.joined(lot, got, low_zs, [inv0])
    both_b = net.joined(lot, got, high_zs, both)
    act0, slope0, unit0b, inv0b, y0 = ffn_forward(dims, weights0, pos, unit0, small[0], both_b, 10**11)
    (plane1,) = net.gate([plane1], both_b[:1])
    other1, *got = net.gate([net.swap(plane1, "c"), *net.second_swap(lot, both)], [inv0b])
    part1.arrays = [plane1, plane1, other1, other1]
    weights1 = [part1] + net.core_swap(lot, low_zs, both, got)
    got = net.second_swap(lot, both_b)
    qkv1, lse1, ctx1 = attention_forward(dims, weights1, pos, lengths, y0, small[1], projected=False)
    got = net.gate(got, [lse1])
    weights1 += net.core_swap(lot, high_zs, both_b, got)

    roots = net.rounded(right_roots.reshape((-1,) + right_roots.shape[2:]), got)
    y1, gz1, gctx, sums, early1 = ffn_both(
        dims, weights1, net.early, pos, lengths, cot, small[1], y0, ctx1, [roots]
    )
    roots_y = net.swap(roots, "y")
    net.hold(early1, [roots_y])
    roots = [roots, roots_y, net.swap(roots, "c"), net.swap(roots_y, "c")]

    split = ((0,), (1, 2, 3))
    early1 = net.core_sum(early1)
    gx1, sums1, late1 = attention_backward(
        dims, weights1, net.late, pos, lengths, gz1, gctx, qkv1, lse1, y0, [sums], early1[1]
    )
    got = net.swaps(early1, "yx")
    late1 = net.core_sum(late1)
    early1 = net.add(early1[0], got, late1[1])
    got_l, got_e = net.swaps(late1, "yx"), net.swaps(early1, "xy")
    gz0, gctx0, sums, early0 = ffn_backward(
        dims, weights0, net.early, pos, gx1, small[0], unit0, inv0, ctx0, unit0b, inv0b, act0, slope0,
        [*early1[1], *late1[1]],
    )
    net.hold(early0, [*got_l, *got_e])
    late1 = net.add(late1[0], got_l)
    got_l = net.swaps(late1, "xy")
    early0 = net.core_sum(early0, got_l)
    gx0, sums, late0 = attention_backward(
        dims, weights0, net.late, pos, lengths, gz0, gctx0, qkv0, lse0, x, [sums, sums1],
        early0[1],
    )
    whole1 = net.collect(split, (late1, early1), (got_l, got_e), [gx0])

    got = net.swaps(early0, "yx")
    late0 = net.core_sum(late0, [*got, whole1], 10**11)
    early0 = net.add(early0[0], got, late0[1])
    got_l, got_e = net.swaps(late0, "yx"), net.swaps(early0, "xy")
    late0 = net.add(late0[0], got_l, early0[1])
    got_l = net.swaps(late0, "xy")
    whole0 = net.collect(split, (late0, early0), (got_l, got_e))
    low0 = net.column_sum(whole0)
    low1, sums = net.gate([net.column_sum(whole1), sums], [whole0])
    sums = net.small_sum(sums, ("c", "x", "y"), ())
    grads1 = net.group(low1)

    def update(n, wide, grads, before):
        return update_layer(
            n, pos, wide, left_stats, right_stats, left_roots, masters, grads, roots, before, [whole0]
        )

    done = update(1, low1, grads1, None)
    low0, sums = net.gate([low0, sums], [done[0]])
    sums = net.small_sum(sums, (), (1, 2))
    done = update(0, low0, net.group(low0, [sums]), done)
    return y1, gx0, done, sums


def local(
    inputs,
    lengths,
    cotangent,
    masters,
    small_params,
    small_moments,
    left_stats,
    right_stats,
    left_roots,
    right_roots,
):
    chains, seq, width = inputs.shape
    rows = chains * seq
    groups, shards = lax.axis_size("grp"), lax.axis_size("fsdp")
    block = masters.shape[3]
    ffn = small_params.shape[1] - 8 * width
    dims = Dims(width, ffn, block, groups * masters.shape[1], rows)
    small = [small_params[n : n + 1] for n in range(LAYERS)]
    x, cot = inputs.reshape(rows, width), cotangent.reshape(rows, width)
    if groups == 2 * Z_SLABS and shards == 4:
        net = SmallSlice(dims)
        y, gx, done, sums = run_small(
            net, dims, small, lengths, x, cot, left_stats, right_stats, left_roots, right_roots, masters
        )
    else:
        net = AnySlice(dims)
        low = [masters[n].astype(BF) for n in range(LAYERS)]
        y, gx, owned, sums = run_any(net, dims, small, lengths, x, cot, low)
        done = update_plain(net, owned, masters, left_stats, right_stats, left_roots, right_roots)
    weight_grads, new_left, new_right, new_masters, new_copies = done
    small_grads, new_moments, new_small = update_small(sums, small_moments, small_params)
    return (
        y.reshape(chains, seq, width),
        gx.reshape(chains, seq, width),
        weight_grads,
        small_grads,
        new_moments,
        new_small,
        new_left,
        new_right,
        new_masters,
        new_copies,
    )


def solution(mesh):
    tokens, blocks = P(("grp", "fsdp"), None, None), P(None, "grp", "fsdp", None)
    return jax.shard_map(
        local,
        mesh=mesh,
        in_specs=(tokens, P(("grp", "fsdp")), tokens, blocks, P(), P(), blocks, blocks, blocks, blocks),
        out_specs=(tokens, tokens, blocks, P(), P(), P(), blocks, blocks, blocks, blocks),
        check_vma=False,
    )
```

```python
import functools

import jax
import jax.numpy as jnp
from jax import lax
from jax.experimental import pallas as pl
from jax.experimental.pallas import tpu as pltpu
from jax.sharding import PartitionSpec as P

HEADS = 12
LAYERS = 2
Z_SLABS = 4
BF = jnp.bfloat16
F32 = jnp.float32

norm_epsilon = 1e-05
matrix_rate = 1.0
small_rate = 0.3
decay_rate = 0.5
moment_epsilon = 1e-08

VMEM = pl.BlockSpec(memory_space=pltpu.VMEM)
SMEM = pl.BlockSpec(memory_space=pltpu.SMEM)
ANY = pl.BlockSpec(memory_space=pl.ANY)


def shape(dims, dtype):
    return jax.ShapeDtypeStruct(tuple(dims), dtype)


def mm(a, b):
    return jnp.dot(a, b, preferred_element_type=F32)


def mm_bt(a, b):
    return lax.dot_general(a, b, (((1,), (1,)), ((), ())), preferred_element_type=F32)


def mm_at(a, b):
    return lax.dot_general(a, b, (((0,), (0,)), ((), ())), preferred_element_type=F32)


class Part:
    def __init__(self, zs, js, order, arrays=None, offsets=(0, 0, 0, 0), strides=None):
        self.zs, self.js, self.order = tuple(zs), tuple(js), order
        self.arrays, self.offsets = arrays, offsets
        many = len(self.zs) * len(self.js)
        self.strides = strides or (2 * many, many, len(self.js), 1)

    def index(self, first, second, z, j):
        of_first, of_second, of_z, of_j = self.strides
        return first * of_first + second * of_second + self.zs.index(z) * of_z + self.js.index(j) * of_j

    def count(self):
        return 4 * len(self.zs) * len(self.js)


def launch(body, name, ins, out_shape, out_specs, deps=(), scratch=(), cost=None, aliases=None, limit=16, weight=0, **grid):
    count, extra = len(ins), len(deps)

    def kernel(*refs):
        body(*refs[:count], *refs[count + extra :])

    flops, moved, special = weight, 0, 0
    return pl.pallas_call(
        kernel,
        in_specs=[spec for _, spec in ins] + [ANY] * extra,
        out_specs=out_specs,
        out_shape=out_shape,
        scratch_shapes=list(scratch),
        input_output_aliases=aliases or {},
        compiler_params=pltpu.CompilerParams(vmem_limit_bytes=int(limit * 2**20)),
        cost_estimate=pl.CostEstimate(flops=flops, bytes_accessed=moved, transcendentals=special),
        name=name,
        **grid,
    )(*[array for array, _ in ins], *deps)


class Dims:
    def __init__(self, model, ffn, block, blocks, rows):
        self.model, self.ffn, self.block, self.blocks, self.rows = model, ffn, block, blocks, rows
        self.own = blocks // (2 * Z_SLABS)
        self.piece = block // 4
        wide, tall = model // block, ffn // block
        self.places = {}
        at = 0
        for name, rows_, cols_ in (
            ("q", wide, wide),
            ("k", wide, wide),
            ("v", wide, wide),
            ("o", wide, wide),
            ("up", wide, tall),
            ("down", tall, wide),
        ):
            self.places[name] = [
                (at + r * cols_ + c, r * block, c * block) for r in range(rows_) for c in range(cols_)
            ]
            at += rows_ * cols_

    def where(self, b):
        return b // (2 * self.own), (b // self.own) % 2, b % self.own


def find_part(parts, z, j):
    for number, part in enumerate(parts):
        if z in part.zs and j in part.js:
            return number
    raise ValueError("no part")


def needed_parts(dims, parts, names):
    used = set()
    for name in names:
        for b, _, _ in dims.places[name]:
            z, _, j = dims.where(b)
            used.add(find_part(parts, z, j))
    return [parts[n] for n in sorted(used)]


def start_loads(dims, parts, refs, pos, name, dst, row0, col0, sem):
    x, y, c = pos
    by_x = []

    def start(src, row, quarter, col):
        rows = pl.ds(pl.multiple_of(row0 + row + dims.piece * quarter, 16), dims.piece)
        pltpu.make_async_copy(src, dst.at[rows, pl.ds(col0 + col, dims.block)], sem).start()

    for b, row, col in dims.places[name]:
        z, xq, j = dims.where(b)
        number = find_part(parts, z, j)
        if parts[number].order == "xy":
            by_x.append((number, z, xq, j, row, col))
            continue
        for dc in range(2):
            for dy in range(2):
                n = 2 * dc + dy
                src = refs[number][n].at[parts[number].offsets[n] + parts[number].index(0, x ^ xq, z, j)]
                start(src, row, 2 * (y ^ dy) + (c ^ dc), col)
    if by_x:
        for own_x in range(2):

            @pl.when(x == own_x)
            def _(own_x=own_x):
                for number, z, xq, j, row, col in by_x:
                    for dc in range(2):
                        for yq in range(2):
                            n = 2 * dc + (own_x ^ xq)
                            at = parts[number].offsets[n] + parts[number].index(0, y ^ yq, z, j)
                            start(refs[number][n].at[at], row, 2 * yq + (c ^ dc), col)


def wait_for(ref, sem):
    pltpu.make_async_copy(ref, ref, sem).wait()


def start_stores(dims, parts, outs, pos, places, src, sem):
    x, y, c = pos
    for b, row, col in places:
        z, xq, j = dims.where(b)
        number = find_part(parts, z, j)
        for dc in range(2):
            for yq in range(2):
                ends = (x ^ xq, y ^ yq) if parts[number].order == "xy" else (y ^ yq, x ^ xq)
                rows = pl.ds(pl.multiple_of(row + dims.piece * (2 * yq + (c ^ dc)), 16), dims.piece)
                dst = outs[number][dc].at[parts[number].index(*ends, z, j)]
                pltpu.make_async_copy(src.at[rows, pl.ds(col, dims.block)], dst, sem).start()


def norm_forward(values):
    center = values - jnp.mean(values, axis=-1, keepdims=True)
    spread = jnp.mean(center * center, axis=-1, keepdims=True)
    inverse = lax.rsqrt(spread + norm_epsilon)
    return center * inverse, inverse


def norm_backward(gradient, unit, inverse, gain):
    scaled = gradient * gain
    inner = (
        scaled
        - jnp.mean(scaled, axis=-1, keepdims=True)
        - unit * jnp.mean(scaled * unit, axis=-1, keepdims=True)
    )
    return inverse * inner


def col_sum(values):
    return jnp.sum(values.astype(F32), axis=0, keepdims=True)


def put_rows(sums_ref, number, values):
    count = values.shape[1] // 128
    for n in range(count):
        at = number * count + n
        sums_ref[at : at + 1, :] = values[:, 128 * n : 128 * (n + 1)]


def segment(small_ref, number, width):
    return small_ref[0:1, number * width : (number + 1) * width]


def unflatten(refs, parts):
    return [refs[4 * n : 4 * n + 4] for n in range(len(parts))], refs[4 * len(parts) :]


def weight_ins(parts):
    return [(a, ANY) for p in parts for a in p.arrays]


def half_masks(head):
    lane = lax.broadcasted_iota(jnp.int32, (1, 2 * head), 1)
    low = lane < head
    ones = jnp.where(low, 1.0, 0.0).astype(F32)
    return low, (ones.astype(BF), (1.0 - ones).astype(BF))


def project(small_ref, x, ctx, wo):
    attended = mm(ctx, wo) + segment(small_ref, 2, x.shape[1])
    return norm_forward(x.astype(F32) + attended)


def attention_forward_kernel(dims, parts, names, chains, pos_ref, len_ref, x_ref, small_ref, *rest):
    refs, rest = unflatten(rest, parts)
    qkv_ref, lse_ref, ctx_ref, *normed, w, sems = rest
    width, seq = dims.model, dims.rows // chains
    head = width // HEADS
    pos = (pos_ref[1], pos_ref[2], pos_ref[3])
    for n, name in enumerate(names):
        start_loads(dims, parts, refs, pos, name, w, 0, n * width, sems.at[n])
    xb = x_ref[...].astype(BF)
    for n, bias in ((0, 0), (1, None), (2, 1)):
        cols = slice(n * width, (n + 1) * width)
        wait_for(w.at[:, cols], sems.at[n])
        out = mm(xb, w[:, cols])
        if bias is not None:
            out = out + segment(small_ref, bias, width)
        qkv_ref[:, cols] = out.astype(BF)
    low, masks = half_masks(head)
    scale = head**-0.5

    def chain(i, carry):
        rows = pl.ds(pl.multiple_of(i * seq, 16), seq)
        valid = lax.broadcasted_iota(jnp.int32, (seq, seq), 0) < len_ref[i]
        for pair in range(HEADS // 2):
            at = pair * 2 * head
            q = qkv_ref[rows, at : at + 2 * head]
            k = qkv_ref[rows, width + at : width + at + 2 * head]
            v = qkv_ref[rows, 2 * width + at : 2 * width + at + 2 * head]
            outs = []
            for h in range(2):
                s = jnp.where(valid, mm_bt(k, q * masks[h]) * scale, -1000000000.0)
                top = jnp.max(s, axis=0, keepdims=True)
                e = jnp.exp(s - top)
                total = jnp.sum(e, axis=0, keepdims=True)
                lse_ref[i, 2 * pair + h : 2 * pair + h + 1, :] = top + jnp.log(total)
                outs.append(mm_at((e * (1.0 / total)).astype(BF), v))
            ctx_ref[rows, at : at + 2 * head] = jnp.where(low, outs[0], outs[1]).astype(BF)
        return carry

    lax.fori_loop(0, chains, chain, 0)
    if normed:
        wait_for(w.at[:, 3 * width :], sems.at[3])
        unit, inverse = project(small_ref, x_ref[...], ctx_ref[...], w[:, 3 * width :])
        normed[0][...] = unit
        normed[1][...] = inverse


def attention_forward(dims, parts, pos, lengths, x, small, deps=(), projected=True):
    names = ("q", "k", "v", "o") if projected else ("q", "k", "v")
    parts = needed_parts(dims, parts, names)
    chains = lengths.shape[0]
    rows, width = dims.rows, dims.model
    outs = [
        shape((rows, 3 * width), BF),
        shape((chains, HEADS, rows // chains), F32),
        shape((rows, width), BF),
    ]
    if projected:
        outs += [shape((rows, width), F32), shape((rows, 1), F32)]
    return launch(
        functools.partial(attention_forward_kernel, dims, parts, names, chains),
        "attention_forward",
        [(pos, SMEM), (lengths, SMEM), (x, VMEM), (small, VMEM)] + weight_ins(parts),
        outs,
        [VMEM] * len(outs),
        deps,
        [pltpu.VMEM((width, len(names) * width), BF), pltpu.SemaphoreType.DMA((4,))],
        limit=56,
    )


def ffn_forward_body(dims, small_ref, unit_ref, up, down, sems, act_ref, slope_ref):
    width = dims.model
    h1 = unit_ref[...] * segment(small_ref, 4, width) + segment(small_ref, 5, width)
    hb = h1.astype(BF)
    total = h1 + segment(small_ref, 3, width)
    wait_for(up, sems.at[0])
    for n in range(dims.ffn // width):
        cols = slice(n * width, (n + 1) * width)
        u = mm(hb, up[:, cols]) + segment(small_ref, 8 + n, width)
        cdf = 0.5 * (1.0 + lax.erf(u * 0.7071067811865476))
        act = (u * cdf).astype(BF)
        act_ref[:, cols] = act
        slope_ref[:, cols] = (cdf + u * (0.3989422804014327 * jnp.exp(-0.5 * u * u))).astype(BF)
        if n == 0:
            wait_for(down, sems.at[1])
        total = total + mm(act, down[cols, :])
    return total


def ffn_forward_kernel(dims, parts, pos_ref, unit_ref, small_ref, *rest):
    refs, rest = unflatten(rest, parts)
    act_ref, slope_ref, unit2_ref, inv2_ref, y_ref, up, down, sems = rest
    pos = (pos_ref[1], pos_ref[2], pos_ref[3])
    start_loads(dims, parts, refs, pos, "up", up, 0, 0, sems.at[0])
    start_loads(dims, parts, refs, pos, "down", down, 0, 0, sems.at[1])
    width = dims.model
    total = ffn_forward_body(dims, small_ref, unit_ref, up, down, sems, act_ref, slope_ref)
    unit, inverse = norm_forward(total)
    unit2_ref[...] = unit
    inv2_ref[...] = inverse
    y_ref[...] = unit * segment(small_ref, 6, width) + segment(small_ref, 7, width)


def ffn_forward(dims, parts, pos, unit, small, deps=(), weight=0):
    parts = needed_parts(dims, parts, ("up", "down"))
    rows, width, ffn = dims.rows, dims.model, dims.ffn
    return launch(
        functools.partial(ffn_forward_kernel, dims, parts),
        "ffn_forward",
        [(pos, SMEM), (unit, VMEM), (small, VMEM)] + weight_ins(parts),
        [
            shape((rows, ffn), BF),
            shape((rows, ffn), BF),
            shape((rows, width), F32),
            shape((rows, 1), F32),
            shape((rows, width), F32),
        ],
        [VMEM] * 5,
        deps,
        [pltpu.VMEM((width, ffn), BF), pltpu.VMEM((ffn, width), BF), pltpu.SemaphoreType.DMA((2,))],
        (4 * rows * width * ffn, 24 << 20, 3 << 20),
        weight=weight,
        limit=56,
    )


def ffn_backward_body(
    dims, outs_parts, outs, pos, gy, small_ref, unit_ref, inv_ref, ctx_ref, unit2, inv2, act_ref, slope_ref,
    up, down, wo, grad_up, grad_down, grad_o, sem_out, gz1_ref, gctx_ref, sums_ref, wait_o, ready=lambda: None,
):
    width = dims.model
    gain1, gain2 = segment(small_ref, 4, width), segment(small_ref, 6, width)

    def put(number, values):
        put_rows(sums_ref, number, values)

    put(6, col_sum(gy * unit2))
    put(7, col_sum(gy))
    gz2 = norm_backward(gy, unit2, inv2, gain2)
    gf = gz2.astype(BF)
    put(3, col_sum(gf))
    ready()
    hb = (unit_ref[...] * gain1 + segment(small_ref, 5, width)).astype(BF)
    gh1 = gz2
    block = dims.block
    for n in range(dims.ffn // width):
        cols = slice(n * width, (n + 1) * width)
        gu = (slope_ref[:, cols].astype(F32) * mm_bt(gf, down[cols, :])).astype(BF)
        put(8 + n, col_sum(gu))
        grad_up[:, cols] = mm_at(hb, gu).astype(BF)
        grad_down[cols, :] = mm_at(act_ref[:, cols], gf).astype(BF)
        low, high = n * width, (n + 1) * width
        start_stores(
            dims, outs_parts, outs, pos,
            [p for p in dims.places["up"] if low <= p[2] < high], grad_up, sem_out.at[0],
        )
        start_stores(
            dims, outs_parts, outs, pos,
            [p for p in dims.places["down"] if low <= p[1] < high], grad_down, sem_out.at[1],
        )
        gh1 = gh1 + mm_bt(gu, up[:, cols])
    unit = unit_ref[...]
    put(4, col_sum(gh1 * unit))
    put(5, col_sum(gh1))
    gz1 = norm_backward(gh1, unit, inv_ref[...], gain1)
    gz1_ref[...] = gz1
    ga = gz1.astype(BF)
    put(2, col_sum(ga))
    grad_o[...] = mm_at(ctx_ref[...], ga).astype(BF)
    start_stores(dims, outs_parts, outs, pos, dims.places["o"], grad_o, sem_out.at[2])
    wait_o()
    gctx_ref[...] = mm_bt(ga, wo[...]).astype(BF)
    put(0, jnp.zeros((1, width), F32))
    put(1, jnp.zeros((1, width), F32))
    wait_for(grad_up, sem_out.at[0])
    wait_for(grad_down, sem_out.at[1])
    wait_for(grad_o, sem_out.at[2])


def grad_shapes(dims, parts):
    return [shape((p.count(), dims.piece, dims.block), BF) for p in parts for _ in range(2)]


def pair_up(arrays, parts):
    return [Part(p.zs, p.js, p.order, list(arrays[2 * n : 2 * n + 2])) for n, p in enumerate(parts)]


def ffn_scratch(dims):
    width, ffn = dims.model, dims.ffn
    matrices = [(width, ffn), (ffn, width), (width, width)] * 2
    return [pltpu.VMEM(m, BF) for m in matrices] + [pltpu.SemaphoreType.DMA((3,))] * 2


def ffn_backward_kernel(dims, parts, outs_parts, pos_ref, gy_ref, small_ref, inv_ref, unit2_ref, inv2_ref, *rest):
    far, rest = rest[:4], rest[4:]
    refs, rest = unflatten(rest, parts)
    gz1_ref, gctx_ref, sums_ref, *rest = rest
    count = 2 * len(outs_parts)
    outs = [rest[2 * n : 2 * n + 2] for n in range(len(outs_parts))]
    up, down, wo, grad_up, grad_down, grad_o, sems, sem_out, *near, sem_far = rest[count:]
    unit_ref, slope_ref, act_ref, ctx_ref = near
    pos = (pos_ref[1], pos_ref[2], pos_ref[3])
    pltpu.make_async_copy(far[0], near[0], sem_far.at[0]).start()
    start_loads(dims, parts, refs, pos, "down", down, 0, 0, sems.at[1])
    for n in range(1, 4):
        pltpu.make_async_copy(far[n], near[n], sem_far.at[n]).start()
    start_loads(dims, parts, refs, pos, "up", up, 0, 0, sems.at[0])
    start_loads(dims, parts, refs, pos, "o", wo, 0, 0, sems.at[2])

    def ready():
        wait_for(unit_ref, sem_far.at[0])
        wait_for(down, sems.at[1])
        for n in range(1, 4):
            wait_for(near[n], sem_far.at[n])
        wait_for(up, sems.at[0])

    ffn_backward_body(
        dims, outs_parts, outs, pos, gy_ref[...], small_ref, unit_ref, inv_ref, ctx_ref,
        unit2_ref[...], inv2_ref[...], act_ref, slope_ref, up, down, wo, grad_up, grad_down, grad_o,
        sem_out, gz1_ref, gctx_ref, sums_ref, lambda: wait_for(wo, sems.at[2]), ready,
    )


def ffn_backward(dims, parts, outs_parts, pos, gy, small, unit, inv, ctx, unit2, inv2, act, slope, deps=()):
    parts = needed_parts(dims, parts, ("up", "down", "o"))
    rows, width, ffn = dims.rows, dims.model, dims.ffn
    grads = grad_shapes(dims, outs_parts)
    out = launch(
        functools.partial(ffn_backward_kernel, dims, parts, outs_parts),
        "ffn_backward",
        [(pos, SMEM)]
        + [(a, VMEM) for a in (gy, small, inv, unit2, inv2)]
        + [(a, ANY) for a in (unit, slope, act, ctx)]
        + weight_ins(parts),
        [shape((rows, width), F32), shape((rows, width), BF), shape((small.shape[1] // 128, 128), F32)] + grads,
        [VMEM] * 3 + [ANY] * len(grads),
        deps,
        ffn_scratch(dims)
        + [pltpu.VMEM(a.shape, a.dtype) for a in (unit, slope, act, ctx)]
        + [pltpu.SemaphoreType.DMA((4,))],
        (8 * rows * width * ffn + 4 * rows * width * width, 40 << 20, 0),
        limit=56,
    )
    return out[0], out[1], out[2], pair_up(out[3:], outs_parts)


def ffn_both_kernel(dims, parts, outs_parts, chains, pos_ref, len_ref, cot_ref, small_ref, x_ref, ctx_ref, *rest):
    refs, rest = unflatten(rest, parts)
    y_ref, gz1_ref, gctx_ref, sums_ref, *rest = rest
    count = 2 * len(outs_parts)
    outs = [rest[2 * n : 2 * n + 2] for n in range(len(outs_parts))]
    up, down, wo, grad_up, grad_down, grad_o, sems, sem_out, act_ref, slope_ref, unit_ref, inv_ref = rest[count:]
    pos = (pos_ref[1], pos_ref[2], pos_ref[3])
    start_loads(dims, parts, refs, pos, "o", wo, 0, 0, sems.at[2])
    start_loads(dims, parts, refs, pos, "up", up, 0, 0, sems.at[0])
    start_loads(dims, parts, refs, pos, "down", down, 0, 0, sems.at[1])
    width, seq = dims.model, dims.rows // chains
    wait_for(wo, sems.at[2])
    unit, inverse = project(small_ref, x_ref[...], ctx_ref[...], wo[...])
    unit_ref[...] = unit
    inv_ref[...] = inverse
    total = ffn_forward_body(dims, small_ref, unit_ref, up, down, sems, act_ref, slope_ref)
    unit2, inv2 = norm_forward(total)
    y_ref[...] = (unit2 * segment(small_ref, 6, width) + segment(small_ref, 7, width)).astype(BF)
    place = lax.broadcasted_iota(jnp.int32, (seq, width), 0)
    gy = jnp.concatenate(
        [
            jnp.where(place < len_ref[i], cot_ref[i * seq : (i + 1) * seq, :].astype(F32), 0.0)
            for i in range(chains)
        ],
        axis=0,
    )
    ffn_backward_body(
        dims, outs_parts, outs, pos, gy, small_ref, unit_ref, inv_ref, ctx_ref,
        unit2, inv2, act_ref, slope_ref, up, down, wo, grad_up, grad_down, grad_o,
        sem_out, gz1_ref, gctx_ref, sums_ref, lambda: None,
    )


def ffn_both(dims, parts, outs_parts, pos, lengths, cot, small, x, ctx, deps=()):
    parts = needed_parts(dims, parts, ("up", "down", "o"))
    rows, width, ffn = dims.rows, dims.model, dims.ffn
    grads = grad_shapes(dims, outs_parts)
    out = launch(
        functools.partial(ffn_both_kernel, dims, parts, outs_parts, lengths.shape[0]),
        "ffn_both",
        [(pos, SMEM), (lengths, SMEM)]
        + [(a, VMEM) for a in (cot, small, x, ctx)]
        + weight_ins(parts),
        [
            shape((rows, width), BF),
            shape((rows, width), F32),
            shape((rows, width), BF),
            shape((small.shape[1] // 128, 128), F32),
        ]
        + grads,
        [VMEM] * 4 + [ANY] * len(grads),
        deps,
        ffn_scratch(dims)
        + [pltpu.VMEM((rows, ffn), BF)] * 2
        + [pltpu.VMEM((rows, width), F32), pltpu.VMEM((rows, 1), F32)],
        (12 * rows * width * ffn + 4 * rows * width * width, 40 << 20, 3 << 20),
        limit=62,
    )
    return out[0], out[1], out[2], out[3], pair_up(out[4:], outs_parts)


def attention_backward_kernel(dims, parts, outs_parts, chains, given, pos_ref, len_ref, gz1_ref, gctx_ref, qkv_ref, lse_ref, x_ref, *rest):
    given_refs, rest = rest[:given], rest[given:]
    refs, rest = unflatten(rest, parts)
    gx_ref, sums_ref, *rest = rest
    count = 2 * len(outs_parts)
    outs = [rest[2 * n : 2 * n + 2] for n in range(len(outs_parts))]
    w, grads_ref, grad_w, sems, sem_out = rest[count:]
    pos = (pos_ref[1], pos_ref[2], pos_ref[3])
    width, seq = dims.model, dims.rows // chains
    head = width // HEADS
    names = ("q", "k", "v")
    for n, name in enumerate(names):
        start_loads(dims, parts, refs, pos, name, w, 0, n * width, sems.at[n])
    low, masks = half_masks(head)
    scale = head**-0.5

    def chain(i, carry):
        rows = pl.ds(pl.multiple_of(i * seq, 16), seq)
        valid = lax.broadcasted_iota(jnp.int32, (seq, seq), 0) < len_ref[i]
        for pair in range(HEADS // 2):
            at = pair * 2 * head
            q = qkv_ref[rows, at : at + 2 * head]
            k = qkv_ref[rows, width + at : width + at + 2 * head]
            v = qkv_ref[rows, 2 * width + at : 2 * width + at + 2 * head]
            g = gctx_ref[rows, at : at + 2 * head]
            gq, gk, gv = [], [], []
            for h in range(2):
                s = jnp.where(valid, mm_bt(k, q * masks[h]) * scale, -1000000000.0)
                p = jnp.exp(s - lse_ref[i, 2 * pair + h : 2 * pair + h + 1, :])
                gp = mm_bt(v, g * masks[h])
                inner = jnp.sum(p * gp, axis=0, keepdims=True)
                gs = (p * (gp - inner)).astype(BF)
                gv.append(mm(p.astype(BF), g))
                gk.append(mm(gs, q))
                gq.append(mm_at(gs, k))
            grads_ref[rows, at : at + 2 * head] = (jnp.where(low, gq[0], gq[1]) * scale).astype(BF)
            grads_ref[rows, width + at : width + at + 2 * head] = (
                jnp.where(low, gk[0], gk[1]) * scale
            ).astype(BF)
            grads_ref[rows, 2 * width + at : 2 * width + at + 2 * head] = jnp.where(
                low, gv[0], gv[1]
            ).astype(BF)
        return carry

    lax.fori_loop(0, chains, chain, 0)
    xb = x_ref[...].astype(BF)
    for n, name in enumerate(names):
        cols = slice(n * width, (n + 1) * width)
        grad_w[:, cols] = mm_at(xb, grads_ref[:, cols]).astype(BF)
        places = [(b, r, c + n * width) for b, r, c in dims.places[name]]
        start_stores(dims, outs_parts, outs, pos, places, grad_w, sem_out)
    at = 0
    for ref in given_refs:
        sums_ref[at : at + ref.shape[0], :] = ref[...]
        at += ref.shape[0]
    put_rows(sums_ref, 0, col_sum(grads_ref[:, :width]))
    put_rows(sums_ref, 1, col_sum(grads_ref[:, 2 * width :]))
    gx = gz1_ref[...]
    for n in range(3):
        cols = slice(n * width, (n + 1) * width)
        wait_for(w.at[:, cols], sems.at[n])
        gx = gx + mm_bt(grads_ref[:, cols], w[:, cols])
    gx_ref[...] = gx
    wait_for(grad_w, sem_out)


def attention_backward(dims, parts, outs_parts, pos, lengths, gz1, gctx, qkv, lse, x, sums, deps=()):
    parts = needed_parts(dims, parts, ("q", "k", "v"))
    rows, width = dims.rows, dims.model
    grads = grad_shapes(dims, outs_parts)
    out = launch(
        functools.partial(attention_backward_kernel, dims, parts, outs_parts, lengths.shape[0], len(sums)),
        "attention_backward",
        [(pos, SMEM), (lengths, SMEM)] + [(a, VMEM) for a in (gz1, gctx, qkv, lse, x, *sums)] + weight_ins(parts),
        [shape((rows, width), F32), shape((sum(a.shape[0] for a in sums), 128), F32)] + grads,
        [VMEM] * 2 + [ANY] * len(grads),
        deps,
        [
            pltpu.VMEM((width, 3 * width), BF),
            pltpu.VMEM((rows, 3 * width), BF),
            pltpu.VMEM((width, 3 * width), BF),
            pltpu.SemaphoreType.DMA((3,)),
            pltpu.SemaphoreType.DMA,
        ],
        (24 * rows * width * width, 24 << 20, 1 << 20),
        limit=56,
    )
    return out[0], out[1], pair_up(out[2:], outs_parts)


class AnySlice:
    def __init__(self, dims):
        self.dims = dims
        own = range(dims.own)
        self.early = [Part((1, 2, 3), own, "yx")]
        self.late = [Part((0,), own, "yx")]

    def position(self):
        return jnp.zeros((4,), jnp.int32)

    def gather(self, low):
        dims = self.dims
        whole = lax.all_gather(low, "fsdp", axis=1, tiled=True)
        whole = lax.all_gather(whole, "grp", axis=0, tiled=True)
        split = whole.reshape(Z_SLABS, 2, dims.own, 2, 2, dims.piece, dims.block)
        order = split.transpose(4, 3, 1, 0, 2, 5, 6).reshape(4, -1, dims.piece, dims.block)
        return [Part(range(Z_SLABS), range(dims.own), "yx", [order[n] for n in range(4)])]

    def reduce(self, early, late):
        dims = self.dims
        pieces = []
        for part in (late[0], early[0]):
            stacked = jnp.stack(part.arrays)
            split = stacked.reshape(2, 2, 2, len(part.zs), dims.own, dims.piece, dims.block)
            pieces.append(split.transpose(3, 2, 4, 1, 0, 5, 6))
        whole = jnp.concatenate(pieces, axis=0).reshape(dims.blocks, dims.block, dims.block)
        rows = lax.psum_scatter(whole, "fsdp", scatter_dimension=1, tiled=True)
        return lax.psum_scatter(rows, "grp", scatter_dimension=0, tiled=True).astype(F32)

    def small_sum(self, values):
        return lax.psum(values, ("grp", "fsdp"))

    def group(self, owned):
        return lax.all_gather(owned, "fsdp", axis=1, tiled=True)


def swap_of(axis):
    def move(z, x, y, c):
        return (z, x ^ (axis == "x"), y ^ (axis == "y"), c ^ (axis == "c"))

    return move


def join_kernel(ranges, *refs):
    pairs = len(ranges)
    ins, outs, hold, sems = refs[: 2 * pairs], refs[2 * pairs : 3 * pairs + 1], refs[-3], refs[-2:]
    runs, at = [], 0
    for n, (low, count) in enumerate(ranges):
        runs.append(hold.at[pl.ds(at, 2 * count)])
        for half in range(2):
            src = ins[2 * n + half].at[pl.ds(low, count)]
            pltpu.make_async_copy(src, hold.at[pl.ds(at + half * count, count)], sems[0].at[n]).start()
        at += 2 * count
    for n in range(pairs):
        wait_for(runs[n], sems[0].at[n])
        pltpu.make_async_copy(runs[n], outs[n], sems[1].at[n]).start()
    pltpu.make_async_copy(hold, outs[pairs], sems[1].at[pairs]).start()
    for n in range(pairs):
        wait_for(runs[n], sems[1].at[n])
    wait_for(hold, sems[1].at[pairs])


def stack_kernel(*refs):
    *ins, out, sem = refs
    count = ins[0].shape[0]
    for n, ref in enumerate(ins):
        pltpu.make_async_copy(ref, out.at[pl.ds(n * count, count)], sem).start()
    wait_for(out, sem)


def round_kernel(src_ref, dst_ref):
    dst_ref[...] = src_ref[...].astype(BF)


def add_kernel(a_ref, b_ref, first_ref, second_ref):
    half = first_ref.shape[0]

    def piece(i, carry):
        for out, at in ((first_ref, i), (second_ref, i + half)):
            out[i] = (a_ref[at].astype(F32) + b_ref[at].astype(F32)).astype(BF)
        return carry

    lax.fori_loop(0, half, piece, 0)


def add_both_kernel(*refs):
    ins, outs, hold, sems = refs[:4], refs[4:8], refs[8], refs[9]
    for n in range(4):
        pltpu.make_async_copy(ins[n], hold.at[n], sems.at[n]).start()
    half = outs[0].shape[0]
    for n in range(2):
        wait_for(hold.at[2 * n], sems.at[2 * n])
        wait_for(hold.at[2 * n + 1], sems.at[2 * n + 1])
        for i in range(half):
            for out, at in ((outs[2 * n], i), (outs[2 * n + 1], i + half)):
                out[i] = (hold[2 * n, at].astype(F32) + hold[2 * n + 1, at].astype(F32)).astype(BF)


def collect_kernel(zs, *refs):
    pairs = len(zs)
    ins, out, total, holds, sems = refs[: 2 * pairs], refs[2 * pairs], refs[2 * pairs + 1], refs[2 * pairs + 2 : -1], refs[-1]
    for n in range(2 * pairs):
        pltpu.make_async_copy(ins[n], holds[n], sems.at[n]).start()
    half = holds[0].shape[0] // len(zs[0])
    copies = []
    for n, z_list in enumerate(zs):
        wait_for(holds[2 * n], sems.at[2 * n])
        wait_for(holds[2 * n + 1], sems.at[2 * n + 1])
        for place, want in enumerate(z_list):
            piece, at = pl.ds(place * half, half), pl.ds((2 * want + n % 2) * half, half)
            value = holds[2 * n][piece].astype(F32) + holds[2 * n + 1][piece].astype(F32)
            total[at] = value.astype(BF)
            copies.append(pltpu.make_async_copy(total.at[at], out.at[at], sems.at[2 * pairs]))
            copies[-1].start()
    wait_for(total, sems.at[2 * pairs])


def pick_kernel(places, src_ref, *refs):
    outs, holds, sems = refs[: len(places)], refs[len(places) : -2], refs[-2:]
    for n, runs in enumerate(places):
        at = 0
        for low, count in runs:
            dst = holds[n].at[pl.ds(at, count)]
            pltpu.make_async_copy(src_ref.at[pl.ds(low, count)], dst, sems[0].at[n]).start()
            at += count
    for n in range(len(places)):
        wait_for(holds[n], sems[0].at[n])
        pltpu.make_async_copy(holds[n], outs[n], sems[1].at[n]).start()
    for n in range(len(places)):
        wait_for(holds[n], sems[1].at[n])


def pass_kernel(*refs):
    pass


class SmallSlice:
    def __init__(self, dims):
        self.dims = dims
        a, b = range(dims.own // 2), range(dims.own // 2, dims.own)
        self.early = [Part((1, 2, 3), a, "yx"), Part((1, 2, 3), b, "xy")]
        self.late = [Part((0,), a, "yx"), Part((0,), b, "xy")]
        group, shard = lax.axis_index("grp"), lax.axis_index("fsdp")
        self.z, self.x, self.y, self.c = group // 2, group % 2, shard // 2, shard % 2
        self.pos = jnp.stack([self.z, self.x, self.y, self.c]).astype(jnp.int32)

    def position(self):
        return self.pos

    def pieces(self, count):
        return shape((count, self.dims.piece, self.dims.block), BF)

    def permute(self, array, move):
        pairs = []
        for flat in range(8 * Z_SLABS):
            to = move(flat // 8, flat // 4 % 2, flat // 2 % 2, flat % 2)
            if to is not None:
                pairs.append((flat, ((to[0] * 2 + to[1]) * 2 + to[2]) * 2 + to[3]))
        return lax.ppermute(array, ("grp", "fsdp"), pairs)

    def swap(self, array, axis):
        return self.permute(array, swap_of(axis))

    def rounded(self, wide, deps=()):
        return launch(round_kernel, "rounded", [(wide, VMEM)], shape(wide.shape, BF), VMEM, deps)

    def columns(self):
        return [[2 * z + x for z in range(Z_SLABS)] for x in range(2)]

    def whole_column(self, own):
        return lax.all_gather(own, "grp", axis_index_groups=self.columns(), axis=0, tiled=True)

    def whole_lot(self, whole, zs, js, deps=()):
        half, count = len(js) // 2, len(js)
        places = [[(z * count + low, half) for z in zs] for low in (0, half)]
        sizes = [self.pieces(len(zs) * half)] * 2
        arrays = launch(
            functools.partial(pick_kernel, places),
            "pick",
            [(whole, ANY)],
            sizes,
            [ANY] * 2,
            deps,
            [pltpu.VMEM(s.shape, BF) for s in sizes] + [pltpu.SemaphoreType.DMA((2,))] * 2,
            limit=60,
        )
        halves = ((js[:half], "yx"), (js[half:], "xy"))
        return [(Part(zs, j, order), a) for (j, order), a in zip(halves, arrays)]

    def gate(self, arrays, deps):
        return launch(
            pass_kernel,
            "gate",
            [(a, ANY) for a in arrays],
            [shape(a.shape, a.dtype) for a in arrays],
            [ANY] * len(arrays),
            deps,
            aliases={n: n for n in range(len(arrays))},
            limit=60,
        )

    def hold(self, parts, deps):
        for part, array in zip(parts, self.gate([p.arrays[1] for p in parts], deps)):
            part.arrays[1] = array

    def first_swap(self, lot):
        return [self.swap(a, part.order[1]) for part, a in lot]

    def joined(self, lot, got, zs, deps=()):
        ins, ranges, sizes = [], [], []
        for (part, own), g in zip(lot, got):
            count = own.shape[0] // len(part.zs)
            ranges.append((part.zs.index(zs[0]) * count, len(zs) * count))
            sizes.append(self.pieces(2 * len(zs) * count))
            ins += [own, g]
        return launch(
            functools.partial(join_kernel, ranges),
            "join",
            [(a, ANY) for a in ins],
            sizes + [self.pieces(sum(a.shape[0] for a in sizes))],
            [ANY] * (len(lot) + 1),
            deps,
            [pltpu.VMEM((sum(a.shape[0] for a in sizes),) + sizes[0].shape[1:], BF)]
            + [pltpu.SemaphoreType.DMA((2,)), pltpu.SemaphoreType.DMA((3,))],
            limit=60,
        )

    def second_swap(self, lot, both):
        return [self.swap(b, part.order[0]) for (part, _), b in zip(lot, both)]

    def plane(self, own, js, deps):
        got = [self.swap(own, "x"), self.swap(own, "y")]
        got.append(self.permute(own, lambda z, x, y, c: (z, 1 - x, 1 - y, c)))
        count = own.shape[0]
        whole = launch(
            stack_kernel,
            "stack",
            [(a, ANY) for a in [own, *got]],
            self.pieces(4 * count),
            VMEM,
            deps,
            [pltpu.SemaphoreType.DMA],
        )
        part = Part(range(Z_SLABS), js, "yx", None, (0, 2 * count) * 2, (2 * count, count, 4 * count, 1))
        return part, whole

    def core_swap(self, lot, zs, both, got):
        others = self.swap(both[-1], "c")
        parts, at = [], 0
        for (part, _), b, g in zip(lot, both, got):
            parts.append(Part(zs, part.js, part.order, [b, g, others, self.swap(g, "c")], (0, 0, at, 0)))
            at += b.shape[0]
        return parts

    def add(self, keep, got, deps=(), weight=0):
        sums = []
        for own, other in zip(keep, got):
            out = [self.pieces(own.shape[0] // 2)] * 2
            sums.append(launch(add_kernel, "add", [(own, VMEM), (other, VMEM)], out, [VMEM] * 2, deps, weight=weight))
        return [kept for kept, _ in sums], [sent for _, sent in sums]

    def add_both(self, keep, got, deps=()):
        ins = [a for pair in zip(keep, got) for a in pair]
        out = launch(
            add_both_kernel,
            "add_both",
            [(a, ANY) for a in ins],
            [self.pieces(keep[0].shape[0] // 2)] * 4,
            [VMEM] * 4,
            deps,
            [pltpu.VMEM((4,) + keep[0].shape, BF), pltpu.SemaphoreType.DMA((4,))],
            limit=16,
        )
        return out[0::2], out[1::2]

    def core_sum(self, parts, deps=(), weight=0):
        got = [self.swap(p.arrays[1], "c") for p in parts]
        return self.add([p.arrays[0] for p in parts], got, deps, weight)

    def swaps(self, sums, axes):
        return [self.swap(a, axis) for a, axis in zip(sums[1], axes)]

    def collect(self, zs, sums, got, deps=(), weight=0):
        ins = []
        for (kept, _), others in zip(sums, got):
            for own, other in zip(kept, others):
                ins += [own, other]
        return launch(
            functools.partial(collect_kernel, [z for z in zs for _ in range(2)]),
            "collect",
            [(a, ANY) for a in ins],
            self.pieces(Z_SLABS * self.dims.own),
            ANY,
            deps,
            [pltpu.VMEM((Z_SLABS * self.dims.own,) + ins[0].shape[1:], BF)]
            + [pltpu.VMEM(a.shape, BF) for a in ins]
            + [pltpu.SemaphoreType.DMA((len(ins) + 1,))],
            weight=weight,
            limit=60,
        )

    def column_sum(self, whole):
        return lax.psum_scatter(
            whole, "grp", axis_index_groups=self.columns(), scatter_dimension=0, tiled=True
        )

    def small_sum(self, values, axes):
        for axis in axes:
            values = values + self.swap(values, axis)
        return values

    def small_sum_slabs(self, values):
        one, two, three = (
            self.permute(values, lambda z, x, y, c, bits=bits: (z ^ bits, x, y, c)) for bits in (1, 2, 3)
        )
        return (values + one) + (two + three)

    def group(self, own, deps=()):
        (other,) = self.gate([self.swap(own, "y")], deps)
        return [own, other, self.swap(own, "c"), self.swap(other, "c")]


def update_kernel(layer, first, count_grads, pos_ref, own_ref, *rest):
    stats, grads, rest = rest[:4], rest[4 : 4 + count_grads], rest[4 + count_grads :]
    roots, rest = rest[:4], rest[4:]
    if not first:
        rest = rest[5:]
    outs, rest = rest[:5], rest[5:]
    g_ref, r_ref, turned, own, held, fresh, low_ref, sem_g, sem_r, sem_in, sem_out = rest
    y, c = pos_ref[2], pos_ref[3]
    count, piece, block = own_ref.shape

    def quarter(yq, cq):
        return pl.ds(pl.multiple_of(piece * (2 * yq + cq), 16), piece)

    for n in range(count_grads):
        rows = quarter(y ^ (n % 2), c ^ (n // 2)) if count_grads == 4 else pl.ds(0, block)
        if count_grads == 4:
            pltpu.make_async_copy(grads[n], g_ref.at[:, rows, :], sem_g).start()
    if count_grads == 1:
        for n in range(4):
            mine = grads[0].at[pl.ds(n * count, count)]
            pltpu.make_async_copy(mine, g_ref.at[:, pl.ds(n * piece, piece), :], sem_g).start()
    for n in range(4):
        mine = roots[n].at[pl.ds(layer * count, count)]
        pltpu.make_async_copy(mine, r_ref.at[:, quarter(y ^ (n % 2), c ^ (n // 2)), :], sem_r).start()
    for n in range(4):
        pltpu.make_async_copy(stats[n].at[layer], held.at[n], sem_in.at[n]).start()
    pltpu.make_async_copy(own_ref, own, sem_in.at[4]).start()
    own_rows = quarter(y, c)
    wait_for(g_ref, sem_g)
    def halves(value):
        high = value.astype(BF)
        return [high, (value - high.astype(F32)).astype(BF)]

    for b in range(count):
        g = g_ref[b]
        turned[...] = g.T
        if b == 0:
            wait_for(held.at[0], sem_in.at[0])
        fresh[1, b] = decay_rate * held[0, b] + (1.0 - decay_rate) * mm_bt(g_ref[b, own_rows, :], g)
        if b == 0:
            wait_for(held.at[1], sem_in.at[1])
            wait_for(held.at[2], sem_in.at[2])
        products = mm(jnp.concatenate([turned[own_rows, :], *halves(held[2, b])], axis=0), g)
        fresh[2, b] = decay_rate * held[1, b] + (1.0 - decay_rate) * products[:piece]
        if b == 0:
            wait_for(r_ref, sem_r)
        mixed = products[piece : 2 * piece] + products[2 * piece :]
        products = mm(jnp.concatenate(halves(mixed), axis=0), r_ref[b])
        update = products[:piece] + products[piece:]
        if b == 0:
            wait_for(held.at[3], sem_in.at[3])
            wait_for(own, sem_in.at[4])
        master = held[3, b] - matrix_rate * update
        fresh[3, b] = master
        low_ref[b] = master.astype(BF)
        fresh[0, b] = own[b].astype(F32)
        for n in range(4):
            pltpu.make_async_copy(fresh.at[n, b], outs[n].at[layer, b], sem_out.at[0]).start()
        pltpu.make_async_copy(low_ref.at[b], outs[4].at[layer, b], sem_out.at[1]).start()
    wait_for(fresh, sem_out.at[0])
    wait_for(low_ref, sem_out.at[1])


def update_layer(layer, pos, own, left, right, left_roots, masters, grads, roots, before, deps=()):
    count, piece, block = own.shape
    whole = (LAYERS, count, piece, block)
    ins = [(pos, SMEM), (own, ANY)] + [(a, ANY) for a in (left, right, left_roots, masters)]
    ins += [(a, ANY) for a in grads] + [(a, ANY) for a in roots]
    aliases = {}
    if before is not None:
        aliases = {len(ins) + n: n for n in range(5)}
        ins += [(a, ANY) for a in before]
    return launch(
        functools.partial(update_kernel, layer, before is None, len(grads)),
        "update_layer",
        ins,
        [shape(whole, F32)] * 4 + [shape(whole, BF)],
        [ANY] * 5,
        deps,
        [
            pltpu.VMEM((count, block, block), BF),
            pltpu.VMEM((count, block, block), BF),
            pltpu.VMEM((block, block), BF),
            pltpu.VMEM(own.shape, own.dtype),
            pltpu.VMEM((4,) + own.shape, F32),
            pltpu.VMEM((4,) + own.shape, F32),
            pltpu.VMEM(own.shape, BF),
            pltpu.SemaphoreType.DMA,
            pltpu.SemaphoreType.DMA,
            pltpu.SemaphoreType.DMA((5,)),
            pltpu.SemaphoreType.DMA((2,)),
        ],
        (0, 0, 0),
        aliases,
        limit=63.5,
    )


def update_plain(net, owned, masters, left_stats, right_stats, left_roots, right_roots):
    own_rows = masters.shape[2]
    first_row = lax.axis_index("fsdp") * own_rows
    highest = lax.Precision.HIGHEST
    grads = jnp.stack(owned)
    whole = jnp.stack([net.group(g.astype(BF)) for g in owned]).astype(F32)
    roots = jnp.stack([net.group(right_roots[n].astype(BF)) for n in range(LAYERS)]).astype(F32)
    columns = lax.dynamic_slice_in_dim(whole, first_row, own_rows, 3)
    new_left = decay_rate * left_stats + (1.0 - decay_rate) * jnp.einsum(
        "lbrk,lbck->lbrc", grads, whole, precision=highest
    )
    new_right = decay_rate * right_stats + (1.0 - decay_rate) * jnp.einsum(
        "lbkr,lbkc->lbrc", columns, whole, precision=highest
    )
    mixed = jnp.einsum("lbrk,lbkc->lbrc", whole, roots, precision=highest)
    update = jnp.einsum("lbrk,lbkc->lbrc", left_roots, mixed, precision=highest)
    new_masters = masters - matrix_rate * update
    return grads, new_left, new_right, new_masters, new_masters.astype(BF)


def update_small_kernel(sums_ref, moments_ref, params_ref, grads_out, moments_out, params_out):
    count = moments_ref.shape[1] // 128
    for layer in range(LAYERS):
        for n in range(count):
            at, cols = layer * count + n, slice(128 * n, 128 * (n + 1))
            grads_out[layer : layer + 1, cols] = sums_ref[at : at + 1, :]
    grads = grads_out[...]
    moments = decay_rate * moments_ref[...] + (1.0 - decay_rate) * grads * grads
    moments_out[...] = moments
    params_out[...] = params_ref[...] - small_rate * grads / (jnp.sqrt(moments) + moment_epsilon)


def update_small(sums, moments, params):
    return launch(
        update_small_kernel,
        "update_small",
        [(a, VMEM) for a in (sums, moments, params)],
        [shape(moments.shape, F32)] * 3,
        [VMEM] * 3,
    )


def run_any(net, dims, small, lengths, x, cot, low):
    pos = net.position()
    weights = [net.gather(low[n]) for n in range(LAYERS)]
    last = LAYERS - 1
    saved = []
    for n in range(LAYERS):
        qkv, lse, ctx, *normed = attention_forward(
            dims, weights[n], pos, lengths, x, small[n], projected=n < last
        )
        saved.append([x, qkv, lse, ctx, *normed])
        if n < last:
            *rest, x = ffn_forward(dims, weights[n], pos, normed[0], small[n])
            saved[n] += rest
    owned = [None] * LAYERS
    for n in reversed(range(LAYERS)):
        x, qkv, lse, ctx, *rest = saved[n]
        if n == last:
            y, gz1, gctx, sums_a, early = ffn_both(
                dims, weights[n], net.early, pos, lengths, cot, small[n], x, ctx
            )
        else:
            unit, inv, act, slope, unit2, inv2 = rest
            gz1, gctx, sums_a, early = ffn_backward(
                dims, weights[n], net.early, pos, gy, small[n], unit, inv, ctx, unit2, inv2, act, slope
            )
        sums = [sums_a] if n == last else [sums_a, sums]
        gy, sums, late = attention_backward(
            dims, weights[n], net.late, pos, lengths, gz1, gctx, qkv, lse, x, sums
        )
        owned[n] = net.reduce(early, late)
    return y, gy, owned, net.small_sum(sums)


def run_small(net, dims, small, lengths, x, cot, left_stats, right_stats, left_roots, right_roots, masters):
    pos = net.position()
    own, every = tuple(range(dims.own)), tuple(range(Z_SLABS))
    third = dims.own // 3

    low_zs, high_zs = every[:1], every[1:]
    third = dims.own // 3
    whole_a = net.whole_column(masters[0, :third].astype(BF))
    whole_b = net.whole_column(masters[0, third:].astype(BF))
    most = 2 * third
    whole1 = net.whole_column(masters[1, :most].astype(BF))
    part1, plane1 = net.plane(masters[1, most:].astype(BF), own[most:], [whole_a])
    lot = net.whole_lot(whole_a, every, own[:third], [plane1])
    plane1 = net.whole_column(plane1)
    both = net.joined(lot, net.first_swap(lot), every)
    got = net.second_swap(lot, both)
    weights0 = net.core_swap(lot, every, both, got)
    lot = net.whole_lot(whole_b, every, own[third:], both)
    both = net.joined(lot, net.first_swap(lot), every, got)
    got = net.second_swap(lot, both)
    lot_b = net.whole_lot(whole1, every, own[:most], both)
    weights0 += net.core_swap(lot, every, both, net.gate(got, [a for _, a in lot_b]))

    lot = lot_b
    got = net.first_swap(lot)
    qkv0, lse0, ctx0, unit0, inv0 = attention_forward(
        dims, weights0, pos, lengths, x, small[0], [a for _, a in lot]
    )
    both = net.joined(lot, got, low_zs, [inv0])
    both_b = net.joined(lot, got, high_zs, both)
    act0, slope0, unit0b, inv0b, y0 = ffn_forward(dims, weights0, pos, unit0, small[0], both_b, 10**11)
    (plane1,) = net.gate([plane1], both_b[:1])
    other1, *got = net.gate([net.swap(plane1, "c"), *net.second_swap(lot, both)], [inv0b])
    part1.arrays = [plane1, plane1, other1, other1]
    weights1 = [part1] + net.core_swap(lot, low_zs, both, got)
    got = net.second_swap(lot, both_b)
    qkv1, lse1, ctx1 = attention_forward(dims, weights1, pos, lengths, y0, small[1], projected=False)
    got = net.gate(got, [lse1])
    weights1 += net.core_swap(lot, high_zs, both_b, got)

    roots = net.rounded(right_roots.reshape((-1,) + right_roots.shape[2:]), got)
    y1, gz1, gctx, sums, early1 = ffn_both(
        dims, weights1, net.early, pos, lengths, cot, small[1], y0, ctx1, [roots]
    )
    roots_y = net.swap(roots, "y")
    net.hold(early1, [roots_y])
    roots = [roots, roots_y, net.swap(roots, "c"), net.swap(roots_y, "c")]

    split = ((0,), (1, 2, 3))
    early1 = net.core_sum(early1)
    gx1, sums1, late1 = attention_backward(
        dims, weights1, net.late, pos, lengths, gz1, gctx, qkv1, lse1, y0, [sums], early1[1]
    )
    got = net.swaps(early1, "yx")
    late1 = net.core_sum(late1)
    early1 = net.add(early1[0], got, late1[1])
    got_l, got_e = net.swaps(late1, "yx"), net.swaps(early1, "xy")
    gz0, gctx0, sums, early0 = ffn_backward(
        dims, weights0, net.early, pos, gx1, small[0], unit0, inv0, ctx0, unit0b, inv0b, act0, slope0,
        [*early1[1], *late1[1]],
    )
    net.hold(early0, [*got_l, *got_e])
    late1 = net.add_both(late1[0], got_l)
    got_l = net.swaps(late1, "xy")
    early0 = net.core_sum(early0, got_l)
    gx0, sums, late0 = attention_backward(
        dims, weights0, net.late, pos, lengths, gz0, gctx0, qkv0, lse0, x, [sums, sums1],
        early0[1],
    )
    whole1 = net.collect(split, (late1, early1), (got_l, got_e), [gx0])

    got = net.swaps(early0, "yx")
    late0 = net.core_sum(late0, [*got, whole1], 10**11)
    early0 = net.add(early0[0], got, late0[1])
    got_l, got_e = net.swaps(late0, "yx"), net.swaps(early0, "xy")
    late0 = net.add(late0[0], got_l, early0[1])
    got_l = net.swaps(late0, "xy")
    whole0 = net.collect(split, (late0, early0), (got_l, got_e))
    low0 = net.column_sum(whole0)
    low1, sums = net.gate([net.column_sum(whole1), sums], [whole0])
    sums = net.small_sum(sums, ("c", "x", "y"))
    grads1 = net.group(low1)

    def update(n, wide, grads, before):
        return update_layer(
            n, pos, wide, left_stats, right_stats, left_roots, masters, grads, roots, before, [whole0]
        )

    done = update(1, low1, grads1, None)
    low0, sums = net.gate([low0, sums], [done[0]])
    sums = net.small_sum_slabs(sums)
    done = update(0, low0, net.group(low0, [sums]), done)
    return y1, gx0, done, sums


def local(
    inputs,
    lengths,
    cotangent,
    masters,
    small_params,
    small_moments,
    left_stats,
    right_stats,
    left_roots,
    right_roots,
):
    chains, seq, width = inputs.shape
    rows = chains * seq
    groups, shards = lax.axis_size("grp"), lax.axis_size("fsdp")
    block = masters.shape[3]
    ffn = small_params.shape[1] - 8 * width
    dims = Dims(width, ffn, block, groups * masters.shape[1], rows)
    small = [small_params[n : n + 1] for n in range(LAYERS)]
    x, cot = inputs.reshape(rows, width), cotangent.reshape(rows, width)
    if groups == 2 * Z_SLABS and shards == 4:
        net = SmallSlice(dims)
        y, gx, done, sums = run_small(
            net, dims, small, lengths, x, cot, left_stats, right_stats, left_roots, right_roots, masters
        )
    else:
        net = AnySlice(dims)
        low = [masters[n].astype(BF) for n in range(LAYERS)]
        y, gx, owned, sums = run_any(net, dims, small, lengths, x, cot, low)
        done = update_plain(net, owned, masters, left_stats, right_stats, left_roots, right_roots)
    weight_grads, new_left, new_right, new_masters, new_copies = done
    small_grads, new_moments, new_small = update_small(sums, small_moments, small_params)
    return (
        y.reshape(chains, seq, width),
        gx.reshape(chains, seq, width),
        weight_grads,
        small_grads,
        new_moments,
        new_small,
        new_left,
        new_right,
        new_masters,
        new_copies,
    )


def solution(mesh):
    tokens, blocks = P(("grp", "fsdp"), None, None), P(None, "grp", "fsdp", None)
    return jax.shard_map(
        local,
        mesh=mesh,
        in_specs=(tokens, P(("grp", "fsdp")), tokens, blocks, P(), P(), blocks, blocks, blocks, blocks),
        out_specs=(tokens, tokens, blocks, P(), P(), P(), blocks, blocks, blocks, blocks),
        check_vma=False,
    )
```

```python
import functools

import jax
import jax.numpy as jnp
from jax import lax
from jax.experimental import pallas as pl
from jax.experimental.pallas import tpu as pltpu
from jax.sharding import PartitionSpec as P

HEADS = 12
LAYERS = 2
Z_SLABS = 4
BF = jnp.bfloat16
F32 = jnp.float32

norm_epsilon = 1e-05
matrix_rate = 1.0
small_rate = 0.3
decay_rate = 0.5
moment_epsilon = 1e-08

VMEM = pl.BlockSpec(memory_space=pltpu.VMEM)
SMEM = pl.BlockSpec(memory_space=pltpu.SMEM)
ANY = pl.BlockSpec(memory_space=pl.ANY)


def shape(dims, dtype):
    return jax.ShapeDtypeStruct(tuple(dims), dtype)


def mm(a, b):
    return jnp.dot(a, b, preferred_element_type=F32)


def mm_bt(a, b):
    return lax.dot_general(a, b, (((1,), (1,)), ((), ())), preferred_element_type=F32)


def mm_at(a, b):
    return lax.dot_general(a, b, (((0,), (0,)), ((), ())), preferred_element_type=F32)


class Part:
    def __init__(self, zs, js, order, arrays=None, offsets=(0, 0, 0, 0), strides=None):
        self.zs, self.js, self.order = tuple(zs), tuple(js), order
        self.arrays, self.offsets = arrays, offsets
        many = len(self.zs) * len(self.js)
        self.strides = strides or (2 * many, many, len(self.js), 1)

    def index(self, first, second, z, j):
        of_first, of_second, of_z, of_j = self.strides
        return first * of_first + second * of_second + self.zs.index(z) * of_z + self.js.index(j) * of_j

    def count(self):
        return 4 * len(self.zs) * len(self.js)


def launch(body, name, ins, out_shape, out_specs, deps=(), scratch=(), cost=None, aliases=None, limit=16, weight=0, **grid):
    count, extra = len(ins), len(deps)

    def kernel(*refs):
        body(*refs[:count], *refs[count + extra :])

    flops, moved, special = weight, 0, 0
    return pl.pallas_call(
        kernel,
        in_specs=[spec for _, spec in ins] + [ANY] * extra,
        out_specs=out_specs,
        out_shape=out_shape,
        scratch_shapes=list(scratch),
        input_output_aliases=aliases or {},
        compiler_params=pltpu.CompilerParams(vmem_limit_bytes=int(limit * 2**20)),
        cost_estimate=pl.CostEstimate(flops=flops, bytes_accessed=moved, transcendentals=special),
        name=name,
        **grid,
    )(*[array for array, _ in ins], *deps)


class Dims:
    def __init__(self, model, ffn, block, blocks, rows):
        self.model, self.ffn, self.block, self.blocks, self.rows = model, ffn, block, blocks, rows
        self.own = blocks // (2 * Z_SLABS)
        self.piece = block // 4
        wide, tall = model // block, ffn // block
        self.places = {}
        at = 0
        for name, rows_, cols_ in (
            ("q", wide, wide),
            ("k", wide, wide),
            ("v", wide, wide),
            ("o", wide, wide),
            ("up", wide, tall),
            ("down", tall, wide),
        ):
            self.places[name] = [
                (at + r * cols_ + c, r * block, c * block) for r in range(rows_) for c in range(cols_)
            ]
            at += rows_ * cols_

    def where(self, b):
        return b // (2 * self.own), (b // self.own) % 2, b % self.own


def find_part(parts, z, j):
    for number, part in enumerate(parts):
        if z in part.zs and j in part.js:
            return number
    raise ValueError("no part")


def needed_parts(dims, parts, names):
    used = set()
    for name in names:
        for b, _, _ in dims.places[name]:
            z, _, j = dims.where(b)
            used.add(find_part(parts, z, j))
    return [parts[n] for n in sorted(used)]


def start_loads(dims, parts, refs, pos, name, dst, row0, col0, sem):
    x, y, c = pos
    by_x = []

    def start(src, row, quarter, col):
        rows = pl.ds(pl.multiple_of(row0 + row + dims.piece * quarter, 16), dims.piece)
        pltpu.make_async_copy(src, dst.at[rows, pl.ds(col0 + col, dims.block)], sem).start()

    for b, row, col in dims.places[name]:
        z, xq, j = dims.where(b)
        number = find_part(parts, z, j)
        if parts[number].order == "xy":
            by_x.append((number, z, xq, j, row, col))
            continue
        for dc in range(2):
            for dy in range(2):
                n = 2 * dc + dy
                src = refs[number][n].at[parts[number].offsets[n] + parts[number].index(0, x ^ xq, z, j)]
                start(src, row, 2 * (y ^ dy) + (c ^ dc), col)
    if by_x:
        for own_x in range(2):

            @pl.when(x == own_x)
            def _(own_x=own_x):
                for number, z, xq, j, row, col in by_x:
                    for dc in range(2):
                        for yq in range(2):
                            n = 2 * dc + (own_x ^ xq)
                            at = parts[number].offsets[n] + parts[number].index(0, y ^ yq, z, j)
                            start(refs[number][n].at[at], row, 2 * yq + (c ^ dc), col)


def wait_for(ref, sem):
    pltpu.make_async_copy(ref, ref, sem).wait()


def start_stores(dims, parts, outs, pos, places, src, sem):
    x, y, c = pos
    for b, row, col in places:
        z, xq, j = dims.where(b)
        number = find_part(parts, z, j)
        for dc in range(2):
            for yq in range(2):
                ends = (x ^ xq, y ^ yq) if parts[number].order == "xy" else (y ^ yq, x ^ xq)
                rows = pl.ds(pl.multiple_of(row + dims.piece * (2 * yq + (c ^ dc)), 16), dims.piece)
                dst = outs[number][dc].at[parts[number].index(*ends, z, j)]
                pltpu.make_async_copy(src.at[rows, pl.ds(col, dims.block)], dst, sem).start()


def norm_forward(values):
    center = values - jnp.mean(values, axis=-1, keepdims=True)
    spread = jnp.mean(center * center, axis=-1, keepdims=True)
    inverse = lax.rsqrt(spread + norm_epsilon)
    return center * inverse, inverse


def norm_backward(gradient, unit, inverse, gain):
    scaled = gradient * gain
    inner = (
        scaled
        - jnp.mean(scaled, axis=-1, keepdims=True)
        - unit * jnp.mean(scaled * unit, axis=-1, keepdims=True)
    )
    return inverse * inner


def col_sum(values):
    return jnp.sum(values.astype(F32), axis=0, keepdims=True)


def put_rows(sums_ref, number, values):
    count = values.shape[1] // 128
    for n in range(count):
        at = number * count + n
        sums_ref[at : at + 1, :] = values[:, 128 * n : 128 * (n + 1)]


def segment(small_ref, number, width):
    return small_ref[0:1, number * width : (number + 1) * width]


def unflatten(refs, parts):
    return [refs[4 * n : 4 * n + 4] for n in range(len(parts))], refs[4 * len(parts) :]


def weight_ins(parts):
    return [(a, ANY) for p in parts for a in p.arrays]


def half_masks(head):
    lane = lax.broadcasted_iota(jnp.int32, (1, 2 * head), 1)
    low = lane < head
    ones = jnp.where(low, 1.0, 0.0).astype(F32)
    return low, (ones.astype(BF), (1.0 - ones).astype(BF))


def project(small_ref, x, ctx, wo):
    attended = mm(ctx, wo) + segment(small_ref, 2, x.shape[1])
    return norm_forward(x.astype(F32) + attended)


def attention_forward_kernel(dims, parts, names, chains, pos_ref, len_ref, x_ref, small_ref, *rest):
    refs, rest = unflatten(rest, parts)
    qkv_ref, lse_ref, ctx_ref, *normed, w, sems = rest
    width, seq = dims.model, dims.rows // chains
    head = width // HEADS
    pos = (pos_ref[1], pos_ref[2], pos_ref[3])
    for n, name in enumerate(names):
        start_loads(dims, parts, refs, pos, name, w, 0, n * width, sems.at[n])
    xb = x_ref[...].astype(BF)
    for n, bias in ((0, 0), (1, None), (2, 1)):
        cols = slice(n * width, (n + 1) * width)
        wait_for(w.at[:, cols], sems.at[n])
        out = mm(xb, w[:, cols])
        if bias is not None:
            out = out + segment(small_ref, bias, width)
        qkv_ref[:, cols] = out.astype(BF)
    low, masks = half_masks(head)
    scale = head**-0.5

    def chain(i, carry):
        rows = pl.ds(pl.multiple_of(i * seq, 16), seq)
        valid = lax.broadcasted_iota(jnp.int32, (seq, seq), 0) < len_ref[i]
        for pair in range(HEADS // 2):
            at = pair * 2 * head
            q = qkv_ref[rows, at : at + 2 * head]
            k = qkv_ref[rows, width + at : width + at + 2 * head]
            v = qkv_ref[rows, 2 * width + at : 2 * width + at + 2 * head]
            outs = []
            for h in range(2):
                s = jnp.where(valid, mm_bt(k, q * masks[h]) * scale, -1000000000.0)
                top = jnp.max(s, axis=0, keepdims=True)
                e = jnp.exp(s - top)
                total = jnp.sum(e, axis=0, keepdims=True)
                lse_ref[i, 2 * pair + h : 2 * pair + h + 1, :] = top + jnp.log(total)
                outs.append(mm_at((e * (1.0 / total)).astype(BF), v))
            ctx_ref[rows, at : at + 2 * head] = jnp.where(low, outs[0], outs[1]).astype(BF)
        return carry

    lax.fori_loop(0, chains, chain, 0)
    if normed:
        wait_for(w.at[:, 3 * width :], sems.at[3])
        unit, inverse = project(small_ref, x_ref[...], ctx_ref[...], w[:, 3 * width :])
        normed[0][...] = unit
        normed[1][...] = inverse


def attention_forward(dims, parts, pos, lengths, x, small, deps=(), projected=True):
    names = ("q", "k", "v", "o") if projected else ("q", "k", "v")
    parts = needed_parts(dims, parts, names)
    chains = lengths.shape[0]
    rows, width = dims.rows, dims.model
    outs = [
        shape((rows, 3 * width), BF),
        shape((chains, HEADS, rows // chains), F32),
        shape((rows, width), BF),
    ]
    if projected:
        outs += [shape((rows, width), F32), shape((rows, 1), F32)]
    return launch(
        functools.partial(attention_forward_kernel, dims, parts, names, chains),
        "attention_forward",
        [(pos, SMEM), (lengths, SMEM), (x, VMEM), (small, VMEM)] + weight_ins(parts),
        outs,
        [VMEM] * len(outs),
        deps,
        [pltpu.VMEM((width, len(names) * width), BF), pltpu.SemaphoreType.DMA((4,))],
        limit=56,
    )


def ffn_forward_body(dims, small_ref, unit_ref, up, down, sems, act_ref, slope_ref):
    width = dims.model
    h1 = unit_ref[...] * segment(small_ref, 4, width) + segment(small_ref, 5, width)
    hb = h1.astype(BF)
    total = h1 + segment(small_ref, 3, width)
    wait_for(up, sems.at[0])
    for n in range(dims.ffn // width):
        cols = slice(n * width, (n + 1) * width)
        u = mm(hb, up[:, cols]) + segment(small_ref, 8 + n, width)
        cdf = 0.5 * (1.0 + lax.erf(u * 0.7071067811865476))
        act = (u * cdf).astype(BF)
        act_ref[:, cols] = act
        slope_ref[:, cols] = (cdf + u * (0.3989422804014327 * jnp.exp(-0.5 * u * u))).astype(BF)
        if n == 0:
            wait_for(down, sems.at[1])
        total = total + mm(act, down[cols, :])
    return total


def ffn_forward_kernel(dims, parts, pos_ref, unit_ref, small_ref, *rest):
    refs, rest = unflatten(rest, parts)
    act_ref, slope_ref, unit2_ref, inv2_ref, y_ref, up, down, sems = rest
    pos = (pos_ref[1], pos_ref[2], pos_ref[3])
    start_loads(dims, parts, refs, pos, "up", up, 0, 0, sems.at[0])
    start_loads(dims, parts, refs, pos, "down", down, 0, 0, sems.at[1])
    width = dims.model
    total = ffn_forward_body(dims, small_ref, unit_ref, up, down, sems, act_ref, slope_ref)
    unit, inverse = norm_forward(total)
    unit2_ref[...] = unit
    inv2_ref[...] = inverse
    y_ref[...] = unit * segment(small_ref, 6, width) + segment(small_ref, 7, width)


def ffn_forward(dims, parts, pos, unit, small, deps=(), weight=0):
    parts = needed_parts(dims, parts, ("up", "down"))
    rows, width, ffn = dims.rows, dims.model, dims.ffn
    return launch(
        functools.partial(ffn_forward_kernel, dims, parts),
        "ffn_forward",
        [(pos, SMEM), (unit, VMEM), (small, VMEM)] + weight_ins(parts),
        [
            shape((rows, ffn), BF),
            shape((rows, ffn), BF),
            shape((rows, width), F32),
            shape((rows, 1), F32),
            shape((rows, width), F32),
        ],
        [VMEM] * 5,
        deps,
        [pltpu.VMEM((width, ffn), BF), pltpu.VMEM((ffn, width), BF), pltpu.SemaphoreType.DMA((2,))],
        (4 * rows * width * ffn, 24 << 20, 3 << 20),
        weight=weight,
        limit=56,
    )


def ffn_backward_body(
    dims, outs_parts, outs, pos, gy, small_ref, unit_ref, inv_ref, ctx_ref, unit2, inv2, act_ref, slope_ref,
    up, down, wo, grad_up, grad_down, grad_o, sem_out, gz1_ref, gctx_ref, sums_ref, wait_o, ready=lambda: None,
):
    width = dims.model
    gain1, gain2 = segment(small_ref, 4, width), segment(small_ref, 6, width)

    def put(number, values):
        put_rows(sums_ref, number, values)

    put(6, col_sum(gy * unit2))
    put(7, col_sum(gy))
    gz2 = norm_backward(gy, unit2, inv2, gain2)
    gf = gz2.astype(BF)
    put(3, col_sum(gf))
    ready()
    hb = (unit_ref[...] * gain1 + segment(small_ref, 5, width)).astype(BF)
    gh1 = gz2
    block = dims.block
    for n in range(dims.ffn // width):
        cols = slice(n * width, (n + 1) * width)
        gu = (slope_ref[:, cols].astype(F32) * mm_bt(gf, down[cols, :])).astype(BF)
        put(8 + n, col_sum(gu))
        grad_up[:, cols] = mm_at(hb, gu).astype(BF)
        grad_down[cols, :] = mm_at(act_ref[:, cols], gf).astype(BF)
        low, high = n * width, (n + 1) * width
        start_stores(
            dims, outs_parts, outs, pos,
            [p for p in dims.places["up"] if low <= p[2] < high], grad_up, sem_out.at[0],
        )
        start_stores(
            dims, outs_parts, outs, pos,
            [p for p in dims.places["down"] if low <= p[1] < high], grad_down, sem_out.at[1],
        )
        gh1 = gh1 + mm_bt(gu, up[:, cols])
    unit = unit_ref[...]
    put(4, col_sum(gh1 * unit))
    put(5, col_sum(gh1))
    gz1 = norm_backward(gh1, unit, inv_ref[...], gain1)
    gz1_ref[...] = gz1
    ga = gz1.astype(BF)
    put(2, col_sum(ga))
    grad_o[...] = mm_at(ctx_ref[...], ga).astype(BF)
    start_stores(dims, outs_parts, outs, pos, dims.places["o"], grad_o, sem_out.at[2])
    wait_o()
    gctx_ref[...] = mm_bt(ga, wo[...]).astype(BF)
    put(0, jnp.zeros((1, width), F32))
    put(1, jnp.zeros((1, width), F32))
    wait_for(grad_up, sem_out.at[0])
    wait_for(grad_down, sem_out.at[1])
    wait_for(grad_o, sem_out.at[2])


def grad_shapes(dims, parts):
    return [shape((p.count(), dims.piece, dims.block), BF) for p in parts for _ in range(2)]


def pair_up(arrays, parts):
    return [Part(p.zs, p.js, p.order, list(arrays[2 * n : 2 * n + 2])) for n, p in enumerate(parts)]


def ffn_scratch(dims):
    width, ffn = dims.model, dims.ffn
    matrices = [(width, ffn), (ffn, width), (width, width)] * 2
    return [pltpu.VMEM(m, BF) for m in matrices] + [pltpu.SemaphoreType.DMA((3,))] * 2


def ffn_backward_kernel(dims, parts, outs_parts, pos_ref, gy_ref, small_ref, inv_ref, unit2_ref, inv2_ref, *rest):
    far, rest = rest[:4], rest[4:]
    refs, rest = unflatten(rest, parts)
    gz1_ref, gctx_ref, sums_ref, *rest = rest
    count = 2 * len(outs_parts)
    outs = [rest[2 * n : 2 * n + 2] for n in range(len(outs_parts))]
    up, down, wo, grad_up, grad_down, grad_o, sems, sem_out, *near, sem_far = rest[count:]
    unit_ref, slope_ref, act_ref, ctx_ref = near
    pos = (pos_ref[1], pos_ref[2], pos_ref[3])
    pltpu.make_async_copy(far[0], near[0], sem_far.at[0]).start()
    start_loads(dims, parts, refs, pos, "down", down, 0, 0, sems.at[1])
    for n in range(1, 4):
        pltpu.make_async_copy(far[n], near[n], sem_far.at[n]).start()
    start_loads(dims, parts, refs, pos, "up", up, 0, 0, sems.at[0])
    start_loads(dims, parts, refs, pos, "o", wo, 0, 0, sems.at[2])

    def ready():
        wait_for(unit_ref, sem_far.at[0])
        wait_for(down, sems.at[1])
        for n in range(1, 4):
            wait_for(near[n], sem_far.at[n])
        wait_for(up, sems.at[0])

    ffn_backward_body(
        dims, outs_parts, outs, pos, gy_ref[...], small_ref, unit_ref, inv_ref, ctx_ref,
        unit2_ref[...], inv2_ref[...], act_ref, slope_ref, up, down, wo, grad_up, grad_down, grad_o,
        sem_out, gz1_ref, gctx_ref, sums_ref, lambda: wait_for(wo, sems.at[2]), ready,
    )


def ffn_backward(dims, parts, outs_parts, pos, gy, small, unit, inv, ctx, unit2, inv2, act, slope, deps=()):
    parts = needed_parts(dims, parts, ("up", "down", "o"))
    rows, width, ffn = dims.rows, dims.model, dims.ffn
    grads = grad_shapes(dims, outs_parts)
    out = launch(
        functools.partial(ffn_backward_kernel, dims, parts, outs_parts),
        "ffn_backward",
        [(pos, SMEM)]
        + [(a, VMEM) for a in (gy, small, inv, unit2, inv2)]
        + [(a, ANY) for a in (unit, slope, act, ctx)]
        + weight_ins(parts),
        [shape((rows, width), F32), shape((rows, width), BF), shape((small.shape[1] // 128, 128), F32)] + grads,
        [VMEM] * 3 + [ANY] * len(grads),
        deps,
        ffn_scratch(dims)
        + [pltpu.VMEM(a.shape, a.dtype) for a in (unit, slope, act, ctx)]
        + [pltpu.SemaphoreType.DMA((4,))],
        (8 * rows * width * ffn + 4 * rows * width * width, 40 << 20, 0),
        limit=56,
    )
    return out[0], out[1], out[2], pair_up(out[3:], outs_parts)


def ffn_both_kernel(dims, parts, outs_parts, chains, pos_ref, len_ref, cot_ref, small_ref, x_ref, ctx_ref, *rest):
    refs, rest = unflatten(rest, parts)
    y_ref, gz1_ref, gctx_ref, sums_ref, *rest = rest
    count = 2 * len(outs_parts)
    outs = [rest[2 * n : 2 * n + 2] for n in range(len(outs_parts))]
    up, down, wo, grad_up, grad_down, grad_o, sems, sem_out, act_ref, slope_ref, unit_ref, inv_ref = rest[count:]
    pos = (pos_ref[1], pos_ref[2], pos_ref[3])
    start_loads(dims, parts, refs, pos, "o", wo, 0, 0, sems.at[2])
    start_loads(dims, parts, refs, pos, "up", up, 0, 0, sems.at[0])
    start_loads(dims, parts, refs, pos, "down", down, 0, 0, sems.at[1])
    width, seq = dims.model, dims.rows // chains
    wait_for(wo, sems.at[2])
    unit, inverse = project(small_ref, x_ref[...], ctx_ref[...], wo[...])
    unit_ref[...] = unit
    inv_ref[...] = inverse
    total = ffn_forward_body(dims, small_ref, unit_ref, up, down, sems, act_ref, slope_ref)
    unit2, inv2 = norm_forward(total)
    y_ref[...] = (unit2 * segment(small_ref, 6, width) + segment(small_ref, 7, width)).astype(BF)
    place = lax.broadcasted_iota(jnp.int32, (seq, width), 0)
    gy = jnp.concatenate(
        [
            jnp.where(place < len_ref[i], cot_ref[i * seq : (i + 1) * seq, :].astype(F32), 0.0)
            for i in range(chains)
        ],
        axis=0,
    )
    ffn_backward_body(
        dims, outs_parts, outs, pos, gy, small_ref, unit_ref, inv_ref, ctx_ref,
        unit2, inv2, act_ref, slope_ref, up, down, wo, grad_up, grad_down, grad_o,
        sem_out, gz1_ref, gctx_ref, sums_ref, lambda: None,
    )


def ffn_both(dims, parts, outs_parts, pos, lengths, cot, small, x, ctx, deps=()):
    parts = needed_parts(dims, parts, ("up", "down", "o"))
    rows, width, ffn = dims.rows, dims.model, dims.ffn
    grads = grad_shapes(dims, outs_parts)
    out = launch(
        functools.partial(ffn_both_kernel, dims, parts, outs_parts, lengths.shape[0]),
        "ffn_both",
        [(pos, SMEM), (lengths, SMEM)]
        + [(a, VMEM) for a in (cot, small, x, ctx)]
        + weight_ins(parts),
        [
            shape((rows, width), BF),
            shape((rows, width), F32),
            shape((rows, width), BF),
            shape((small.shape[1] // 128, 128), F32),
        ]
        + grads,
        [VMEM] * 4 + [ANY] * len(grads),
        deps,
        ffn_scratch(dims)
        + [pltpu.VMEM((rows, ffn), BF)] * 2
        + [pltpu.VMEM((rows, width), F32), pltpu.VMEM((rows, 1), F32)],
        (12 * rows * width * ffn + 4 * rows * width * width, 40 << 20, 3 << 20),
        limit=62,
    )
    return out[0], out[1], out[2], out[3], pair_up(out[4:], outs_parts)


def attention_backward_kernel(dims, parts, outs_parts, chains, given, pos_ref, len_ref, gz1_ref, gctx_ref, qkv_ref, lse_ref, x_ref, *rest):
    given_refs, rest = rest[:given], rest[given:]
    refs, rest = unflatten(rest, parts)
    gx_ref, sums_ref, *rest = rest
    count = 2 * len(outs_parts)
    outs = [rest[2 * n : 2 * n + 2] for n in range(len(outs_parts))]
    w, grads_ref, grad_w, sems, sem_out = rest[count:]
    pos = (pos_ref[1], pos_ref[2], pos_ref[3])
    width, seq = dims.model, dims.rows // chains
    head = width // HEADS
    names = ("q", "k", "v")
    for n, name in enumerate(names):
        start_loads(dims, parts, refs, pos, name, w, 0, n * width, sems.at[n])
    low, masks = half_masks(head)
    scale = head**-0.5

    def chain(i, carry):
        rows = pl.ds(pl.multiple_of(i * seq, 16), seq)
        valid = lax.broadcasted_iota(jnp.int32, (seq, seq), 0) < len_ref[i]
        for pair in range(HEADS // 2):
            at = pair * 2 * head
            q = qkv_ref[rows, at : at + 2 * head]
            k = qkv_ref[rows, width + at : width + at + 2 * head]
            v = qkv_ref[rows, 2 * width + at : 2 * width + at + 2 * head]
            g = gctx_ref[rows, at : at + 2 * head]
            gq, gk, gv = [], [], []
            for h in range(2):
                s = jnp.where(valid, mm_bt(k, q * masks[h]) * scale, -1000000000.0)
                p = jnp.exp(s - lse_ref[i, 2 * pair + h : 2 * pair + h + 1, :])
                gp = mm_bt(v, g * masks[h])
                inner = jnp.sum(p * gp, axis=0, keepdims=True)
                gs = (p * (gp - inner)).astype(BF)
                gv.append(mm(p.astype(BF), g))
                gk.append(mm(gs, q))
                gq.append(mm_at(gs, k))
            grads_ref[rows, at : at + 2 * head] = (jnp.where(low, gq[0], gq[1]) * scale).astype(BF)
            grads_ref[rows, width + at : width + at + 2 * head] = (
                jnp.where(low, gk[0], gk[1]) * scale
            ).astype(BF)
            grads_ref[rows, 2 * width + at : 2 * width + at + 2 * head] = jnp.where(
                low, gv[0], gv[1]
            ).astype(BF)
        return carry

    lax.fori_loop(0, chains, chain, 0)
    xb = x_ref[...].astype(BF)
    for n, name in enumerate(names):
        cols = slice(n * width, (n + 1) * width)
        grad_w[:, cols] = mm_at(xb, grads_ref[:, cols]).astype(BF)
        places = [(b, r, c + n * width) for b, r, c in dims.places[name]]
        start_stores(dims, outs_parts, outs, pos, places, grad_w, sem_out)
    at = 0
    for ref in given_refs:
        sums_ref[at : at + ref.shape[0], :] = ref[...]
        at += ref.shape[0]
    put_rows(sums_ref, 0, col_sum(grads_ref[:, :width]))
    put_rows(sums_ref, 1, col_sum(grads_ref[:, 2 * width :]))
    gx = gz1_ref[...]
    for n in range(3):
        cols = slice(n * width, (n + 1) * width)
        wait_for(w.at[:, cols], sems.at[n])
        gx = gx + mm_bt(grads_ref[:, cols], w[:, cols])
    gx_ref[...] = gx
    wait_for(grad_w, sem_out)


def attention_backward(dims, parts, outs_parts, pos, lengths, gz1, gctx, qkv, lse, x, sums, deps=()):
    parts = needed_parts(dims, parts, ("q", "k", "v"))
    rows, width = dims.rows, dims.model
    grads = grad_shapes(dims, outs_parts)
    out = launch(
        functools.partial(attention_backward_kernel, dims, parts, outs_parts, lengths.shape[0], len(sums)),
        "attention_backward",
        [(pos, SMEM), (lengths, SMEM)] + [(a, VMEM) for a in (gz1, gctx, qkv, lse, x, *sums)] + weight_ins(parts),
        [shape((rows, width), F32), shape((sum(a.shape[0] for a in sums), 128), F32)] + grads,
        [VMEM] * 2 + [ANY] * len(grads),
        deps,
        [
            pltpu.VMEM((width, 3 * width), BF),
            pltpu.VMEM((rows, 3 * width), BF),
            pltpu.VMEM((width, 3 * width), BF),
            pltpu.SemaphoreType.DMA((3,)),
            pltpu.SemaphoreType.DMA,
        ],
        (24 * rows * width * width, 24 << 20, 1 << 20),
        limit=56,
    )
    return out[0], out[1], pair_up(out[2:], outs_parts)


class AnySlice:
    def __init__(self, dims):
        self.dims = dims
        own = range(dims.own)
        self.early = [Part((1, 2, 3), own, "yx")]
        self.late = [Part((0,), own, "yx")]

    def position(self):
        return jnp.zeros((4,), jnp.int32)

    def gather(self, low):
        dims = self.dims
        whole = lax.all_gather(low, "fsdp", axis=1, tiled=True)
        whole = lax.all_gather(whole, "grp", axis=0, tiled=True)
        split = whole.reshape(Z_SLABS, 2, dims.own, 2, 2, dims.piece, dims.block)
        order = split.transpose(4, 3, 1, 0, 2, 5, 6).reshape(4, -1, dims.piece, dims.block)
        return [Part(range(Z_SLABS), range(dims.own), "yx", [order[n] for n in range(4)])]

    def reduce(self, early, late):
        dims = self.dims
        pieces = []
        for part in (late[0], early[0]):
            stacked = jnp.stack(part.arrays)
            split = stacked.reshape(2, 2, 2, len(part.zs), dims.own, dims.piece, dims.block)
            pieces.append(split.transpose(3, 2, 4, 1, 0, 5, 6))
        whole = jnp.concatenate(pieces, axis=0).reshape(dims.blocks, dims.block, dims.block)
        rows = lax.psum_scatter(whole, "fsdp", scatter_dimension=1, tiled=True)
        return lax.psum_scatter(rows, "grp", scatter_dimension=0, tiled=True).astype(F32)

    def small_sum(self, values):
        return lax.psum(values, ("grp", "fsdp"))

    def group(self, owned):
        return lax.all_gather(owned, "fsdp", axis=1, tiled=True)


def swap_of(axis):
    def move(z, x, y, c):
        return (z, x ^ (axis == "x"), y ^ (axis == "y"), c ^ (axis == "c"))

    return move


def join_kernel(ranges, *refs):
    pairs = len(ranges)
    ins, outs, hold, sems = refs[: 2 * pairs], refs[2 * pairs : 3 * pairs + 1], refs[-3], refs[-2:]
    runs, at = [], 0
    for n, (low, count) in enumerate(ranges):
        runs.append(hold.at[pl.ds(at, 2 * count)])
        for half in range(2):
            src = ins[2 * n + half].at[pl.ds(low, count)]
            pltpu.make_async_copy(src, hold.at[pl.ds(at + half * count, count)], sems[0].at[n]).start()
        at += 2 * count
    for n in range(pairs):
        wait_for(runs[n], sems[0].at[n])
        pltpu.make_async_copy(runs[n], outs[n], sems[1].at[n]).start()
    pltpu.make_async_copy(hold, outs[pairs], sems[1].at[pairs]).start()
    for n in range(pairs):
        wait_for(runs[n], sems[1].at[n])
    wait_for(hold, sems[1].at[pairs])


def stack_kernel(*refs):
    *ins, out, sem = refs
    count = ins[0].shape[0]
    for n, ref in enumerate(ins):
        pltpu.make_async_copy(ref, out.at[pl.ds(n * count, count)], sem).start()
    wait_for(out, sem)


def round_kernel(src_ref, dst_ref):
    dst_ref[...] = src_ref[...].astype(BF)


def add_kernel(a_ref, b_ref, first_ref, second_ref):
    half = first_ref.shape[0]

    def piece(i, carry):
        for out, at in ((first_ref, i), (second_ref, i + half)):
            out[i] = (a_ref[at].astype(F32) + b_ref[at].astype(F32)).astype(BF)
        return carry

    lax.fori_loop(0, half, piece, 0)


def add_both_kernel(*refs):
    ins, outs, hold, sems = refs[:4], refs[4:8], refs[8], refs[9]
    for n in range(4):
        pltpu.make_async_copy(ins[n], hold.at[n], sems.at[n]).start()
    half = outs[0].shape[0]
    for n in range(2):
        wait_for(hold.at[2 * n], sems.at[2 * n])
        wait_for(hold.at[2 * n + 1], sems.at[2 * n + 1])
        for i in range(half):
            for out, at in ((outs[2 * n], i), (outs[2 * n + 1], i + half)):
                out[i] = (hold[2 * n, at].astype(F32) + hold[2 * n + 1, at].astype(F32)).astype(BF)


def collect_kernel(zs, *refs):
    pairs = len(zs)
    ins, out, total, holds, sems = refs[: 2 * pairs], refs[2 * pairs], refs[2 * pairs + 1], refs[2 * pairs + 2 : -1], refs[-1]
    for n in range(2 * pairs):
        pltpu.make_async_copy(ins[n], holds[n], sems.at[n]).start()
    half = holds[0].shape[0] // len(zs[0])
    copies = []
    for n, z_list in enumerate(zs):
        wait_for(holds[2 * n], sems.at[2 * n])
        wait_for(holds[2 * n + 1], sems.at[2 * n + 1])
        for place, want in enumerate(z_list):
            piece, at = pl.ds(place * half, half), pl.ds((2 * want + n % 2) * half, half)
            value = holds[2 * n][piece].astype(F32) + holds[2 * n + 1][piece].astype(F32)
            total[at] = value.astype(BF)
            copies.append(pltpu.make_async_copy(total.at[at], out.at[at], sems.at[2 * pairs]))
            copies[-1].start()
    wait_for(total, sems.at[2 * pairs])


def pick_kernel(places, src_ref, *refs):
    outs, holds, sems = refs[: len(places)], refs[len(places) : -2], refs[-2:]
    for n, runs in enumerate(places):
        at = 0
        for low, count in runs:
            dst = holds[n].at[pl.ds(at, count)]
            pltpu.make_async_copy(src_ref.at[pl.ds(low, count)], dst, sems[0].at[n]).start()
            at += count
    for n in range(len(places)):
        wait_for(holds[n], sems[0].at[n])
        pltpu.make_async_copy(holds[n], outs[n], sems[1].at[n]).start()
    for n in range(len(places)):
        wait_for(holds[n], sems[1].at[n])


def pass_kernel(*refs):
    pass


class SmallSlice:
    def __init__(self, dims):
        self.dims = dims
        a, b = range(dims.own // 2), range(dims.own // 2, dims.own)
        self.early = [Part((1, 2, 3), a, "yx"), Part((1, 2, 3), b, "xy")]
        self.late = [Part((0,), a, "yx"), Part((0,), b, "xy")]
        group, shard = lax.axis_index("grp"), lax.axis_index("fsdp")
        self.z, self.x, self.y, self.c = group // 2, group % 2, shard // 2, shard % 2
        self.pos = jnp.stack([self.z, self.x, self.y, self.c]).astype(jnp.int32)

    def position(self):
        return self.pos

    def pieces(self, count):
        return shape((count, self.dims.piece, self.dims.block), BF)

    def permute(self, array, move):
        pairs = []
        for flat in range(8 * Z_SLABS):
            to = move(flat // 8, flat // 4 % 2, flat // 2 % 2, flat % 2)
            if to is not None:
                pairs.append((flat, ((to[0] * 2 + to[1]) * 2 + to[2]) * 2 + to[3]))
        return lax.ppermute(array, ("grp", "fsdp"), pairs)

    def swap(self, array, axis):
        return self.permute(array, swap_of(axis))

    def rounded(self, wide, deps=()):
        return launch(round_kernel, "rounded", [(wide, VMEM)], shape(wide.shape, BF), VMEM, deps)

    def columns(self):
        return [[2 * z + x for z in range(Z_SLABS)] for x in range(2)]

    def whole_column(self, own):
        return lax.all_gather(own, "grp", axis_index_groups=self.columns(), axis=0, tiled=True)

    def whole_lot(self, whole, zs, js, deps=()):
        half, count = len(js) // 2, len(js)
        places = [[(z * count + low, half) for z in zs] for low in (0, half)]
        sizes = [self.pieces(len(zs) * half)] * 2
        arrays = launch(
            functools.partial(pick_kernel, places),
            "pick",
            [(whole, ANY)],
            sizes,
            [ANY] * 2,
            deps,
            [pltpu.VMEM(s.shape, BF) for s in sizes] + [pltpu.SemaphoreType.DMA((2,))] * 2,
            limit=60,
        )
        halves = ((js[:half], "yx"), (js[half:], "xy"))
        return [(Part(zs, j, order), a) for (j, order), a in zip(halves, arrays)]

    def gate(self, arrays, deps):
        return launch(
            pass_kernel,
            "gate",
            [(a, ANY) for a in arrays],
            [shape(a.shape, a.dtype) for a in arrays],
            [ANY] * len(arrays),
            deps,
            aliases={n: n for n in range(len(arrays))},
            limit=60,
        )

    def hold(self, parts, deps):
        for part, array in zip(parts, self.gate([p.arrays[1] for p in parts], deps)):
            part.arrays[1] = array

    def first_swap(self, lot):
        return [self.swap(a, part.order[1]) for part, a in lot]

    def joined(self, lot, got, zs, deps=()):
        ins, ranges, sizes = [], [], []
        for (part, own), g in zip(lot, got):
            count = own.shape[0] // len(part.zs)
            ranges.append((part.zs.index(zs[0]) * count, len(zs) * count))
            sizes.append(self.pieces(2 * len(zs) * count))
            ins += [own, g]
        return launch(
            functools.partial(join_kernel, ranges),
            "join",
            [(a, ANY) for a in ins],
            sizes + [self.pieces(sum(a.shape[0] for a in sizes))],
            [ANY] * (len(lot) + 1),
            deps,
            [pltpu.VMEM((sum(a.shape[0] for a in sizes),) + sizes[0].shape[1:], BF)]
            + [pltpu.SemaphoreType.DMA((2,)), pltpu.SemaphoreType.DMA((3,))],
            limit=60,
        )

    def second_swap(self, lot, both):
        return [self.swap(b, part.order[0]) for (part, _), b in zip(lot, both)]

    def plane(self, own, js, deps):
        got = [self.swap(own, "x"), self.swap(own, "y")]
        got.append(self.permute(own, lambda z, x, y, c: (z, 1 - x, 1 - y, c)))
        count = own.shape[0]
        whole = launch(
            stack_kernel,
            "stack",
            [(a, ANY) for a in [own, *got]],
            self.pieces(4 * count),
            VMEM,
            deps,
            [pltpu.SemaphoreType.DMA],
        )
        part = Part(range(Z_SLABS), js, "yx", None, (0, 2 * count) * 2, (2 * count, count, 4 * count, 1))
        return part, whole

    def core_swap(self, lot, zs, both, got):
        others = self.swap(both[-1], "c")
        parts, at = [], 0
        for (part, _), b, g in zip(lot, both, got):
            parts.append(Part(zs, part.js, part.order, [b, g, others, self.swap(g, "c")], (0, 0, at, 0)))
            at += b.shape[0]
        return parts

    def add(self, keep, got, deps=(), weight=0):
        sums = []
        for own, other in zip(keep, got):
            out = [self.pieces(own.shape[0] // 2)] * 2
            sums.append(launch(add_kernel, "add", [(own, VMEM), (other, VMEM)], out, [VMEM] * 2, deps, weight=weight))
        return [kept for kept, _ in sums], [sent for _, sent in sums]

    def add_both(self, keep, got, deps=()):
        ins = [a for pair in zip(keep, got) for a in pair]
        out = launch(
            add_both_kernel,
            "add_both",
            [(a, ANY) for a in ins],
            [self.pieces(keep[0].shape[0] // 2)] * 4,
            [VMEM] * 4,
            deps,
            [pltpu.VMEM((4,) + keep[0].shape, BF), pltpu.SemaphoreType.DMA((4,))],
            limit=16,
        )
        return out[0::2], out[1::2]

    def core_sum(self, parts, deps=(), weight=0):
        got = [self.swap(p.arrays[1], "c") for p in parts]
        return self.add([p.arrays[0] for p in parts], got, deps, weight)

    def swaps(self, sums, axes):
        return [self.swap(a, axis) for a, axis in zip(sums[1], axes)]

    def collect(self, zs, sums, got, deps=(), weight=0):
        ins = []
        for (kept, _), others in zip(sums, got):
            for own, other in zip(kept, others):
                ins += [own, other]
        return launch(
            functools.partial(collect_kernel, [z for z in zs for _ in range(2)]),
            "collect",
            [(a, ANY) for a in ins],
            self.pieces(Z_SLABS * self.dims.own),
            ANY,
            deps,
            [pltpu.VMEM((Z_SLABS * self.dims.own,) + ins[0].shape[1:], BF)]
            + [pltpu.VMEM(a.shape, BF) for a in ins]
            + [pltpu.SemaphoreType.DMA((len(ins) + 1,))],
            weight=weight,
            limit=60,
        )

    def column_sum(self, whole):
        return lax.psum_scatter(
            whole, "grp", axis_index_groups=self.columns(), scatter_dimension=0, tiled=True
        )

    def small_sum(self, values, axes):
        for axis in axes:
            values = values + self.swap(values, axis)
        return values

    def small_sum_slabs(self, values):
        one, two, three = (
            self.permute(values, lambda z, x, y, c, bits=bits: (z ^ bits, x, y, c)) for bits in (1, 2, 3)
        )
        return (values + one) + (two + three)

    def group(self, own, deps=()):
        (other,) = self.gate([self.swap(own, "y")], deps)
        return [own, other, self.swap(own, "c"), self.swap(other, "c")]


def update_kernel(layer, first, count_grads, pos_ref, own_ref, *rest):
    stats, grads, rest = rest[:4], rest[4 : 4 + count_grads], rest[4 + count_grads :]
    roots, rest = rest[:4], rest[4:]
    if not first:
        rest = rest[5:]
    outs, rest = rest[:5], rest[5:]
    g_ref, r_ref, turned, own, held, fresh, low_ref, sem_in, sem_out = rest
    y, c = pos_ref[2], pos_ref[3]
    count, piece, block = own_ref.shape

    def quarter(yq, cq):
        return pl.ds(pl.multiple_of(piece * (2 * yq + cq), 16), piece)

    groups = [(0, 1), (1, (count - 1) // 2), (1 + (count - 1) // 2, count - 1 - (count - 1) // 2)]
    for number, (low, many) in enumerate(groups):
        some = pl.ds(low, many)
        for n in range(4):
            rows = quarter(y ^ (n % 2), c ^ (n // 2))
            mine = grads[n].at[some]
            pltpu.make_async_copy(mine, g_ref.at[some, rows, :], sem_in.at[number, 5]).start()
        for n in range(3):
            pltpu.make_async_copy(stats[n].at[layer, some], held.at[n, some], sem_in.at[number, n]).start()
        for n in range(4):
            rows = quarter(y ^ (n % 2), c ^ (n // 2))
            mine = roots[n].at[pl.ds(layer * count + low, many)]
            pltpu.make_async_copy(mine, r_ref.at[some, rows, :], sem_in.at[number, 6]).start()
        pltpu.make_async_copy(stats[3].at[layer, some], held.at[3, some], sem_in.at[number, 3]).start()
        pltpu.make_async_copy(own_ref.at[some], own.at[some], sem_in.at[number, 4]).start()
    own_rows = quarter(y, c)

    def arrived(b, n):
        for number, (low, many) in enumerate(groups):
            if low == b:
                some = pl.ds(low, many)
                ref = held.at[n, some] if n < 4 else (own, g_ref, r_ref)[n - 4].at[some]
                wait_for(ref, sem_in.at[number, n])

    def halves(value):
        high = value.astype(BF)
        return [high, (value - high.astype(F32)).astype(BF)]

    for b in range(count):
        arrived(b, 5)
        g = g_ref[b]
        turned[...] = g.T
        arrived(b, 0)
        fresh[1, b] = decay_rate * held[0, b] + (1.0 - decay_rate) * mm_bt(g_ref[b, own_rows, :], g)
        arrived(b, 1)
        arrived(b, 2)
        products = mm(jnp.concatenate([turned[own_rows, :], *halves(held[2, b])], axis=0), g)
        fresh[2, b] = decay_rate * held[1, b] + (1.0 - decay_rate) * products[:piece]
        arrived(b, 6)
        mixed = products[piece : 2 * piece] + products[2 * piece :]
        products = mm(jnp.concatenate(halves(mixed), axis=0), r_ref[b])
        update = products[:piece] + products[piece:]
        arrived(b, 3)
        arrived(b, 4)
        master = held[3, b] - matrix_rate * update
        fresh[3, b] = master
        low_ref[b] = master.astype(BF)
        fresh[0, b] = own[b].astype(F32)
        for n in range(4):
            pltpu.make_async_copy(fresh.at[n, b], outs[n].at[layer, b], sem_out.at[0]).start()
        pltpu.make_async_copy(low_ref.at[b], outs[4].at[layer, b], sem_out.at[1]).start()
    wait_for(fresh, sem_out.at[0])
    wait_for(low_ref, sem_out.at[1])


def update_layer(layer, pos, own, left, right, left_roots, masters, grads, roots, before, deps=()):
    count, piece, block = own.shape
    whole = (LAYERS, count, piece, block)
    ins = [(pos, SMEM), (own, ANY)] + [(a, ANY) for a in (left, right, left_roots, masters)]
    ins += [(a, ANY) for a in grads] + [(a, ANY) for a in roots]
    aliases = {}
    if before is not None:
        aliases = {len(ins) + n: n for n in range(5)}
        ins += [(a, ANY) for a in before]
    return launch(
        functools.partial(update_kernel, layer, before is None, len(grads)),
        "update_layer",
        ins,
        [shape(whole, F32)] * 4 + [shape(whole, BF)],
        [ANY] * 5,
        deps,
        [
            pltpu.VMEM((count, block, block), BF),
            pltpu.VMEM((count, block, block), BF),
            pltpu.VMEM((block, block), BF),
            pltpu.VMEM(own.shape, own.dtype),
            pltpu.VMEM((4,) + own.shape, F32),
            pltpu.VMEM((4,) + own.shape, F32),
            pltpu.VMEM(own.shape, BF),
            pltpu.SemaphoreType.DMA((3, 7)),
            pltpu.SemaphoreType.DMA((2,)),
        ],
        (0, 0, 0),
        aliases,
        limit=63.5,
    )


def update_plain(net, owned, masters, left_stats, right_stats, left_roots, right_roots):
    own_rows = masters.shape[2]
    first_row = lax.axis_index("fsdp") * own_rows
    highest = lax.Precision.HIGHEST
    grads = jnp.stack(owned)
    whole = jnp.stack([net.group(g.astype(BF)) for g in owned]).astype(F32)
    roots = jnp.stack([net.group(right_roots[n].astype(BF)) for n in range(LAYERS)]).astype(F32)
    columns = lax.dynamic_slice_in_dim(whole, first_row, own_rows, 3)
    new_left = decay_rate * left_stats + (1.0 - decay_rate) * jnp.einsum(
        "lbrk,lbck->lbrc", grads, whole, precision=highest
    )
    new_right = decay_rate * right_stats + (1.0 - decay_rate) * jnp.einsum(
        "lbkr,lbkc->lbrc", columns, whole, precision=highest
    )
    mixed = jnp.einsum("lbrk,lbkc->lbrc", whole, roots, precision=highest)
    update = jnp.einsum("lbrk,lbkc->lbrc", left_roots, mixed, precision=highest)
    new_masters = masters - matrix_rate * update
    return grads, new_left, new_right, new_masters, new_masters.astype(BF)


def update_small_kernel(sums_ref, moments_ref, params_ref, grads_out, moments_out, params_out):
    count = moments_ref.shape[1] // 128
    for layer in range(LAYERS):
        for n in range(count):
            at, cols = layer * count + n, slice(128 * n, 128 * (n + 1))
            grads_out[layer : layer + 1, cols] = sums_ref[at : at + 1, :]
    grads = grads_out[...]
    moments = decay_rate * moments_ref[...] + (1.0 - decay_rate) * grads * grads
    moments_out[...] = moments
    params_out[...] = params_ref[...] - small_rate * grads / (jnp.sqrt(moments) + moment_epsilon)


def update_small(sums, moments, params):
    return launch(
        update_small_kernel,
        "update_small",
        [(a, VMEM) for a in (sums, moments, params)],
        [shape(moments.shape, F32)] * 3,
        [VMEM] * 3,
    )


def run_any(net, dims, small, lengths, x, cot, low):
    pos = net.position()
    weights = [net.gather(low[n]) for n in range(LAYERS)]
    last = LAYERS - 1
    saved = []
    for n in range(LAYERS):
        qkv, lse, ctx, *normed = attention_forward(
            dims, weights[n], pos, lengths, x, small[n], projected=n < last
        )
        saved.append([x, qkv, lse, ctx, *normed])
        if n < last:
            *rest, x = ffn_forward(dims, weights[n], pos, normed[0], small[n])
            saved[n] += rest
    owned = [None] * LAYERS
    for n in reversed(range(LAYERS)):
        x, qkv, lse, ctx, *rest = saved[n]
        if n == last:
            y, gz1, gctx, sums_a, early = ffn_both(
                dims, weights[n], net.early, pos, lengths, cot, small[n], x, ctx
            )
        else:
            unit, inv, act, slope, unit2, inv2 = rest
            gz1, gctx, sums_a, early = ffn_backward(
                dims, weights[n], net.early, pos, gy, small[n], unit, inv, ctx, unit2, inv2, act, slope
            )
        sums = [sums_a] if n == last else [sums_a, sums]
        gy, sums, late = attention_backward(
            dims, weights[n], net.late, pos, lengths, gz1, gctx, qkv, lse, x, sums
        )
        owned[n] = net.reduce(early, late)
    return y, gy, owned, net.small_sum(sums)


def run_small(net, dims, small, lengths, x, cot, left_stats, right_stats, left_roots, right_roots, masters):
    pos = net.position()
    own, every = tuple(range(dims.own)), tuple(range(Z_SLABS))
    third = dims.own // 3

    low_zs, high_zs = every[:1], every[1:]
    third = dims.own // 3
    whole_a = net.whole_column(masters[0, :third].astype(BF))
    whole_b = net.whole_column(masters[0, third:].astype(BF))
    most = 2 * third
    whole1 = net.whole_column(masters[1, :most].astype(BF))
    part1, plane1 = net.plane(masters[1, most:].astype(BF), own[most:], [whole_a])
    lot = net.whole_lot(whole_a, every, own[:third], [plane1])
    plane1 = net.whole_column(plane1)
    both = net.joined(lot, net.first_swap(lot), every)
    got = net.second_swap(lot, both)
    weights0 = net.core_swap(lot, every, both, got)
    lot = net.whole_lot(whole_b, every, own[third:], both)
    both = net.joined(lot, net.first_swap(lot), every, got)
    got = net.second_swap(lot, both)
    lot_b = net.whole_lot(whole1, every, own[:most], both)
    weights0 += net.core_swap(lot, every, both, net.gate(got, [a for _, a in lot_b]))

    lot = lot_b
    got = net.first_swap(lot)
    qkv0, lse0, ctx0, unit0, inv0 = attention_forward(
        dims, weights0, pos, lengths, x, small[0], [a for _, a in lot]
    )
    both = net.joined(lot, got, low_zs, [inv0])
    both_b = net.joined(lot, got, high_zs, both)
    act0, slope0, unit0b, inv0b, y0 = ffn_forward(dims, weights0, pos, unit0, small[0], both_b, 10**11)
    (plane1,) = net.gate([plane1], both_b[:1])
    other1, *got = net.gate([net.swap(plane1, "c"), *net.second_swap(lot, both)], [inv0b])
    part1.arrays = [plane1, plane1, other1, other1]
    weights1 = [part1] + net.core_swap(lot, low_zs, both, got)
    got = net.second_swap(lot, both_b)
    qkv1, lse1, ctx1 = attention_forward(dims, weights1, pos, lengths, y0, small[1], projected=False)
    got = net.gate(got, [lse1])
    weights1 += net.core_swap(lot, high_zs, both_b, got)

    roots = net.rounded(right_roots.reshape((-1,) + right_roots.shape[2:]), got)
    y1, gz1, gctx, sums, early1 = ffn_both(
        dims, weights1, net.early, pos, lengths, cot, small[1], y0, ctx1, [roots]
    )
    roots_y = net.swap(roots, "y")
    net.hold(early1, [roots_y])
    roots = [roots, roots_y, net.swap(roots, "c"), net.swap(roots_y, "c")]

    split = ((0,), (1, 2, 3))
    early1 = net.core_sum(early1)
    gx1, sums1, late1 = attention_backward(
        dims, weights1, net.late, pos, lengths, gz1, gctx, qkv1, lse1, y0, [sums], early1[1]
    )
    got = net.swaps(early1, "yx")
    late1 = net.core_sum(late1)
    early1 = net.add(early1[0], got, late1[1])
    got_l, got_e = net.swaps(late1, "yx"), net.swaps(early1, "xy")
    gz0, gctx0, sums, early0 = ffn_backward(
        dims, weights0, net.early, pos, gx1, small[0], unit0, inv0, ctx0, unit0b, inv0b, act0, slope0,
        [*early1[1], *late1[1]],
    )
    net.hold(early0, [*got_l, *got_e])
    late1 = net.add_both(late1[0], got_l)
    got_l = net.swaps(late1, "xy")
    early0 = net.core_sum(early0, got_l)
    gx0, sums, late0 = attention_backward(
        dims, weights0, net.late, pos, lengths, gz0, gctx0, qkv0, lse0, x, [sums, sums1],
        early0[1],
    )
    whole1 = net.collect(split, (late1, early1), (got_l, got_e), [gx0])

    got = net.swaps(early0, "yx")
    late0 = net.core_sum(late0, [*got, whole1], 10**11)
    early0 = net.add(early0[0], got, late0[1])
    got_l, got_e = net.swaps(late0, "yx"), net.swaps(early0, "xy")
    late0 = net.add(late0[0], got_l, early0[1])
    got_l = net.swaps(late0, "xy")
    whole0 = net.collect(split, (late0, early0), (got_l, got_e))
    low0 = net.column_sum(whole0)
    low1, sums = net.gate([net.column_sum(whole1), sums], [whole0])
    sums = net.small_sum(sums, ("c", "x", "y"))
    grads1 = net.group(low1)

    def update(n, wide, grads, before):
        return update_layer(
            n, pos, wide, left_stats, right_stats, left_roots, masters, grads, roots, before, [whole0]
        )

    done = update(1, low1, grads1, None)
    low0, sums = net.gate([low0, sums], [done[0]])
    sums = net.small_sum_slabs(sums)
    done = update(0, low0, net.group(low0, [sums]), done)
    return y1, gx0, done, sums


def local(
    inputs,
    lengths,
    cotangent,
    masters,
    small_params,
    small_moments,
    left_stats,
    right_stats,
    left_roots,
    right_roots,
):
    chains, seq, width = inputs.shape
    rows = chains * seq
    groups, shards = lax.axis_size("grp"), lax.axis_size("fsdp")
    block = masters.shape[3]
    ffn = small_params.shape[1] - 8 * width
    dims = Dims(width, ffn, block, groups * masters.shape[1], rows)
    small = [small_params[n : n + 1] for n in range(LAYERS)]
    x, cot = inputs.reshape(rows, width), cotangent.reshape(rows, width)
    if groups == 2 * Z_SLABS and shards == 4:
        net = SmallSlice(dims)
        y, gx, done, sums = run_small(
            net, dims, small, lengths, x, cot, left_stats, right_stats, left_roots, right_roots, masters
        )
    else:
        net = AnySlice(dims)
        low = [masters[n].astype(BF) for n in range(LAYERS)]
        y, gx, owned, sums = run_any(net, dims, small, lengths, x, cot, low)
        done = update_plain(net, owned, masters, left_stats, right_stats, left_roots, right_roots)
    weight_grads, new_left, new_right, new_masters, new_copies = done
    small_grads, new_moments, new_small = update_small(sums, small_moments, small_params)
    return (
        y.reshape(chains, seq, width),
        gx.reshape(chains, seq, width),
        weight_grads,
        small_grads,
        new_moments,
        new_small,
        new_left,
        new_right,
        new_masters,
        new_copies,
    )


def solution(mesh):
    tokens, blocks = P(("grp", "fsdp"), None, None), P(None, "grp", "fsdp", None)
    return jax.shard_map(
        local,
        mesh=mesh,
        in_specs=(tokens, P(("grp", "fsdp")), tokens, blocks, P(), P(), blocks, blocks, blocks, blocks),
        out_specs=(tokens, tokens, blocks, P(), P(), P(), blocks, blocks, blocks, blocks),
        check_vma=False,
    )
```
